32 devices in a mesh: head: 8 (over y, x, core), seq: 4 (over z).
Axes of the slice: x: 2, y: 2, z: 4, core: 2. Of those that a mesh axis runs over, the one named last changes fastest.
Arguments:
- inputs: bfloat16 [4, 4, 1024, 1024], P(None, 'seq', 'head'), may hold values from -6 to 6
- skips: bfloat16 [4, 4, 1024, 1024], P(None, 'seq', 'head'), may hold values from -6 to 6
- flow_time: float32 [4, 4, 1024], P(None, 'seq', 'head'), may hold values from 0 to 1, as said below
- segment_ids: int32 [4, 4, 1024], P(None, 'seq', 'head'), may hold values from 0 to 7, as said below
- frame_mask: int32 [4, 4, 1024], P(None, 'seq', 'head'), may hold values from 0 to 1, as said below
- cotangent: bfloat16 [4, 4, 1024, 1024], P(None, 'seq', 'head'), may hold values from -6 to 6
- w_skip: bfloat16 [2048, 1024], replicated, may hold values from -0.125 to 0.125
- w_time: bfloat16 [256, 4096], replicated, may hold values from -0.375 to 0.375
- w_qkv: bfloat16 [1024, 3072], replicated, may hold values from -0.1875 to 0.1875
- w_out: bfloat16 [1024, 1024], replicated, may hold values from -0.375 to 0.375
- w_up: bfloat16 [1024, 4096], replicated, may hold values from -0.1875 to 0.1875
- w_down: bfloat16 [4096, 1024], replicated, may hold values from -0.09375 to 0.09375
Outputs:
- output: bfloat16 [4, 4, 1024, 1024], P(None, 'seq', 'head')
- input_grad: float32 [4, 4, 1024, 1024], P(None, 'seq', 'head')
- skip_grad: float32 [4, 4, 1024, 1024], P(None, 'seq', 'head')
- grad_skip: float32 [2048, 1024], P(('head', 'seq'))
- grad_time: float32 [256, 4096], P(('head', 'seq'))
- grad_qkv: float32 [1024, 3072], P(('head', 'seq'))
- grad_out: float32 [1024, 1024], P(('head', 'seq'))
- grad_up: float32 [1024, 4096], P(('head', 'seq'))
- grad_down: float32 [4096, 1024], P(('head', 'seq'))
The draws below stay inside these ranges and needn't reach their ends.
Inputs may be any that keep to these rules, and one draw needn't show every extreme that they name: segment_ids never fall along a bucket, start at 0 and rise by 0 or 1 from frame to frame. frame_mask is 1 on a leading run of each bucket and 0 after it, with at most 64 zeros in a bucket. flow_time is equal on all frames of one segment.
All inputs are finite; a program needn't handle non-finite values.
Results may differ from the reference program's by a relative error of at most 0.015.
Values may be sent and summed in bfloat16 or wider, within the bound.
No kernel may reach another device: no remote copies, remote signals or barrier semaphores. Data moves between devices by JAX's collectives and lax.ppermute only.
A program may use at most 320 MiB of HBM per device.

```python
import math
from functools import partial
import jax
import jax.numpy as jnp
from jax import lax

D = 1024
H = 16
HD = 64
FF = 4096
FREQ = 256
TM = 128
MB = 4
BUCKETS = 4
BLEN = 1024


def segment_layout(key):
    full_shape = (MB, BUCKETS, BLEN)
    boundary_flags = jax.random.randint(jax.random.fold_in(key, 11), full_shape, 0, max(BLEN // 4, 2)) == 0
    chosen = jax.random.randint(jax.random.fold_in(key, 12), (1, BUCKETS, 1), 0, MB)
    frame_place = lax.broadcasted_iota(jnp.int32, full_shape, 2)
    micro_place = lax.broadcasted_iota(jnp.int32, full_shape, 0)
    spanning = (micro_place == chosen) & (frame_place >= TM) & (frame_place <= BLEN - TM)
    forced = (micro_place == (chosen + 1) % MB) & (frame_place % (BLEN // 8) == 0)
    boundary_flags = (boundary_flags | forced) & jnp.logical_not(spanning) & (frame_place > 0)
    return jnp.minimum(jnp.cumsum(boundary_flags.astype(jnp.int32), axis=2), 7)


def draw_segment_ids(key, part):
    layout = segment_layout(key)
    return layout


def draw_flow_time(key, part):
    layout = segment_layout(key)
    key = jax.random.fold_in(key, 2)
    time_table = jax.random.uniform(key, (MB, BUCKETS, BLEN), jnp.float32, 0.0, 1.0)
    return jnp.take_along_axis(time_table, layout, axis=2)


def draw_frame_mask(key, part):
    key = jax.random.fold_in(key, 3)
    pad_count = jax.random.randint(key, (MB, BUCKETS, 1), 0, TM // 2 + 1)
    frame_place = lax.broadcasted_iota(jnp.int32, (MB, BUCKETS, BLEN), 2)
    return (frame_place < BLEN - pad_count).astype(jnp.int32)


def steps_of(own_key, dims, cuts, low, largest):
    def one(position, blocks):
        draws = jax.random.uniform(jax.random.fold_in(jax.random.fold_in(own_key, 6), position), (blocks,), jnp.float32, low / len(cuts), largest / len(cuts))
        return jnp.repeat(jnp.exp(draws), dims[position] // blocks).reshape((-1,) + (1,) * (len(dims) - position - 1))

    gain = one(*cuts[0])
    for cut in cuts[1:]:
        gain = gain * one(*cut)
    return gain


def normal_values(own_key, shape, deviation, most, cuts=(), kind=jnp.bfloat16):
    values = jax.random.normal(own_key, shape, jnp.float32) * deviation
    if len(cuts) > 0:
        values = steps_of(own_key, shape, cuts, -0.22, 0.18) * values
    return jnp.clip(values, min=-most, max=most).astype(kind)


def setup_inputs(seed: int = 0) -> dict:
    arg_keys = jax.random.split(jax.random.key(seed), 13)
    return {
        "inputs": normal_values(arg_keys[0], (MB, BUCKETS, BLEN, D), 1.0, 6.0, ((1, 4), (2, 8))),
        "skips": normal_values(arg_keys[1], (MB, BUCKETS, BLEN, D), 1.0, 6.0, ((1, 4), (2, 8))),
        "flow_time": draw_flow_time(jax.random.fold_in(arg_keys[12], 71), 0),
        "segment_ids": draw_segment_ids(jax.random.fold_in(arg_keys[12], 71), 0),
        "frame_mask": draw_frame_mask(jax.random.fold_in(arg_keys[12], 71), 0),
        "cotangent": normal_values(arg_keys[5], (MB, BUCKETS, BLEN, D), 1.0, 6.0, ((1, 4), (2, 8))),
        "w_skip": normal_values(arg_keys[6], (2 * D, D), (2 * D) ** -0.5, 0.125),
        "w_time": normal_values(arg_keys[7], (FREQ, 4 * D), FREQ ** -0.5, 0.375),
        "w_qkv": normal_values(arg_keys[8], (D, 3 * D), D ** -0.5, 0.1875),
        "w_out": normal_values(arg_keys[9], (D, D), (D // 4) ** -0.5, 0.375),
        "w_up": normal_values(arg_keys[10], (D, FF), D ** -0.5, 0.1875),
        "w_down": normal_values(arg_keys[11], (FF, D), FF ** -0.5, 0.09375),
    }


@jax.custom_vjp
def low(v):
    return lax.optimization_barrier(v.astype(jnp.bfloat16)).astype(jnp.float32)

@jax.custom_vjp
def low_back(v):
    return v

def low_keep(v):
    return (low(v), None)

def low_pass(kept, grad):
    return (grad,)

def back_keep(v):
    return (v, None)

def back_low(kept, grad):
    return (low(grad),)
low.defvjp(low_keep, low_pass)
low_back.defvjp(back_keep, back_low)
eps_norm = 1e-06
neg_fill = -1e+30

def both_ways(values):
    return low_back(low(values))

def matmul_rows(left, right):
    return jnp.einsum('bld,de->ble', left, right, precision=lax.Precision.HIGHEST)

def modulated_norm(hidden, shift_term, scale_term):
    centre = lax.optimization_barrier(jnp.mean(hidden, axis=-1, keepdims=True))
    centered = hidden - centre
    spread = lax.optimization_barrier(jnp.mean(centered * centered, axis=-1, keepdims=True))
    return centered * lax.rsqrt(spread + eps_norm) * (1.0 + scale_term) + shift_term

def gelu_tanh(values):
    return jax.nn.gelu(values, approximate=True)

def time_features(times, feature_count):
    half_size = feature_count // 2
    freq_steps = jnp.exp(jnp.arange(half_size, dtype=jnp.float32) * (-math.log(10000.0) / (half_size - 1)))
    angles = 1000.0 * times[..., None] * freq_steps
    return jnp.concatenate([jnp.sin(angles), jnp.cos(angles)], axis=-1)

def rotate_last(values, cos_table, sin_table):
    half_size = values.shape[-1] // 2
    turned = jnp.concatenate([-values[..., half_size:], values[..., :half_size]], axis=-1)
    return values * cos_table + turned * sin_table

def bucket_attention(items):
    queries, key_rows, values, seg_row, mask_row = items
    bucket_len = queries.shape[0]
    raw_scores = jnp.einsum('ihd,jhd->hij', queries, key_rows, precision=lax.Precision.HIGHEST) * HD ** (-0.5)
    frame_place = jnp.arange(bucket_len, dtype=jnp.int32)
    allowed = (seg_row[:, None] == seg_row[None, :]) & ((mask_row[None, :] == 1) | (frame_place[:, None] == frame_place[None, :]))
    scores = low_back(jnp.where(allowed[None], raw_scores, neg_fill))
    row_max = lax.optimization_barrier(jnp.max(scores, axis=-1, keepdims=True))
    powered = jnp.exp(scores - row_max)
    attn_probs = low(powered / lax.optimization_barrier(jnp.sum(powered, axis=-1, keepdims=True)))
    return jnp.einsum('hij,jhd->ihd', attn_probs, values, precision=lax.Precision.HIGHEST)

def layer_forward(inputs, skips, w_skip, w_time, w_qkv, w_out, w_up, w_down, features, cos_table, sin_table, seg_rows, mask_rows):
    bucket_count, bucket_len, model_width = inputs.shape
    joined = jnp.concatenate([inputs, skips], axis=-1)
    resid_in = low_back(matmul_rows(joined, w_skip))
    modulation = low_back(matmul_rows(features, w_time))
    shift_first, scale_first, shift_second, scale_second = jnp.split(modulation, 4, axis=-1)
    normed_attn = low(modulated_norm(resid_in, shift_first, scale_first))
    projected = low_back(matmul_rows(normed_attn, w_qkv)).reshape(bucket_count, bucket_len, 3, H, HD)
    queries = both_ways(rotate_last(projected[:, :, 0], cos_table, sin_table))
    key_rows = both_ways(rotate_last(projected[:, :, 1], cos_table, sin_table))
    values = both_ways(projected[:, :, 2])
    attended = lax.map(jax.checkpoint(bucket_attention), (queries, key_rows, values, seg_rows, mask_rows))
    attended = both_ways(attended).reshape(bucket_count, bucket_len, model_width)
    resid_mid = resid_in + low_back(matmul_rows(attended, w_out))
    normed_ffn = low(modulated_norm(resid_mid, shift_second, scale_second))
    up_proj = low_back(matmul_rows(normed_ffn, w_up))
    hidden = low(gelu_tanh(up_proj))
    return resid_mid + matmul_rows(hidden, w_down)

def reference(inputs, skips, flow_time, segment_ids, frame_mask, cotangent, w_skip, w_time, w_qkv, w_out, w_up, w_down):
    bucket_count = MB * BUCKETS
    seg_rows = segment_ids.reshape(bucket_count, BLEN).astype(jnp.int32)
    mask_rows = frame_mask.reshape(bucket_count, BLEN).astype(jnp.int32)
    frame_place = lax.broadcasted_iota(jnp.int32, (bucket_count, BLEN), 1)
    boundary = jnp.concatenate([jnp.ones((bucket_count, 1), jnp.bool_), seg_rows[:, 1:] != seg_rows[:, :-1]], axis=1)
    starts = lax.cummax(jnp.where(boundary, frame_place, 0), axis=1)
    inv_freq = jnp.exp(jnp.arange(HD // 2, dtype=jnp.float32) * (-2.0 * math.log(10000.0) / HD))
    angles = (frame_place - starts).astype(jnp.float32)[..., None] * inv_freq
    cos_table = jnp.concatenate([jnp.cos(angles), jnp.cos(angles)], axis=-1)[:, :, None, :]
    sin_table = jnp.concatenate([jnp.sin(angles), jnp.sin(angles)], axis=-1)[:, :, None, :]
    features = low(time_features(flow_time.reshape(bucket_count, BLEN).astype(jnp.float32), FREQ))
    forward = partial(layer_forward, features=features, cos_table=cos_table, sin_table=sin_table, seg_rows=seg_rows, mask_rows=mask_rows)
    frames_in = inputs.reshape(bucket_count, BLEN, D).astype(jnp.float32)
    skips_in = skips.reshape(bucket_count, BLEN, D).astype(jnp.float32)
    result, pull_back = jax.vjp(forward, frames_in, skips_in, w_skip.astype(jnp.float32), w_time.astype(jnp.float32), w_qkv.astype(jnp.float32), w_out.astype(jnp.float32), w_up.astype(jnp.float32), w_down.astype(jnp.float32))
    grads = pull_back(cotangent.reshape(bucket_count, BLEN, D).astype(jnp.float32))
    full_shape = (MB, BUCKETS, BLEN, D)
    return (result.astype(jnp.bfloat16).reshape(full_shape), grads[0].reshape(full_shape), grads[1].reshape(full_shape), grads[2], grads[3], grads[4], grads[5], grads[6], grads[7])
```

```python
import math

import jax
import jax.numpy as jnp
from jax import lax
from jax.experimental import pallas as pl
from jax.experimental.pallas import tpu as pltpu
from jax.sharding import PartitionSpec as P

HD = 64
PAIR = 2 * HD
eps_norm = 1e-06
neg_fill = -1e30
BF = jnp.bfloat16
F32 = jnp.float32
DIMS_FIRST = (((0,), (0,)), ((), ()))
DIMS_LAST = (((1,), (1,)), ((), ()))
VMEM_BYTES = 56 * 1024 * 1024


def dot(left, right, dims=(((1,), (0,)), ((), ()))):
    return lax.dot_general(left, right, dims, preferred_element_type=F32)


def swap(values, axis_name, bits):
    size = lax.axis_size(axis_name)
    return lax.ppermute(values, axis_name, [(i, i ^ bits) for i in range(size)])


def pick(values, index, axis):
    return lax.dynamic_index_in_dim(values, index, axis, keepdims=False)


def to_buckets(parts, span, mine):
    count = parts.shape[0]
    got = [pick(parts, mine, 0)]
    for step in range(1, count):
        got.append(swap(pick(parts, mine ^ step, 0), "head", step * span))
    return jnp.stack(got)


def from_buckets(parts, span, mine):
    count = parts.shape[0]
    got = [parts[0]]
    for step in range(1, count):
        got.append(swap(parts[step], "head", step * span))
    got = jnp.stack(got)
    return jnp.stack([pick(got, mine ^ micro, 0) for micro in range(count)])


def weight_grad(left, right, descending):
    groups = lax.axis_size("head")
    place = lax.axis_index("head")
    frames, rows = left.shape
    width = right.shape[1]
    chunk = rows // groups
    bits = groups.bit_length() - 1
    split = left.reshape(frames, groups // 2, 2, chunk)
    low_bit = place % 2
    away = pick(split, 1 - low_bit, 2).reshape(frames, rows // 2)
    keep = pick(split, low_bit, 2).reshape(frames, rows // 2)
    came = swap(dot(away, right, DIMS_FIRST).astype(BF), "head", 1)
    total = (dot(keep, right, DIMS_FIRST) + came.astype(F32)).astype(BF)
    left_bits = list(range(1, bits))
    if descending:
        left_bits = left_bits[::-1]
    remaining = list(range(1, bits))
    for bit in left_bits:
        after = 2 ** len([b for b in remaining if b < bit]) * chunk
        view = total.reshape(-1, 2, after, width)
        here = (place >> bit) % 2
        came = swap(pick(view, 1 - here, 1), "head", 2**bit)
        total = (pick(view, here, 1).astype(F32) + came.astype(F32)).astype(BF)
        remaining.remove(bit)
    total = total.reshape(chunk, width)
    return lax.psum_scatter(total, "seq", scatter_dimension=0, tiled=True).astype(F32)


def norm_stats(hidden):
    centred = hidden - jnp.mean(hidden, axis=-1, keepdims=True)
    rate = lax.rsqrt(jnp.mean(centred * centred, axis=-1, keepdims=True) + eps_norm)
    return centred * rate, rate


def norm_back(grad, normal, rate, scale_term):
    inner = grad * (1.0 + scale_term)
    return rate * (
        inner
        - jnp.mean(inner, axis=-1, keepdims=True)
        - normal * jnp.mean(inner * normal, axis=-1, keepdims=True)
    )


def turn(values):
    lanes = lax.broadcasted_iota(jnp.int32, values.shape, 1)
    low = lax.rem(lanes, HD) < HD // 2
    return jnp.where(low, pltpu.roll(values, PAIR - HD // 2, 1), pltpu.roll(values, HD // 2, 1))


def project_kernel(rotated_tiles, x_ref, w_ref, cos_ref, sin_ref, o_ref):
    raw = dot(x_ref[...], w_ref[...])

    @pl.when(pl.program_id(0) < rotated_tiles)
    def _():
        for first in range(0, raw.shape[1], PAIR):
            part = raw[:, first : first + PAIR]
            turned = part * cos_ref[...] + turn(part) * sin_ref[...]
            o_ref[:, first : first + PAIR] = turned.astype(BF)

    @pl.when(pl.program_id(0) >= rotated_tiles)
    def _():
        o_ref[...] = raw.astype(BF)


def project(normed, w_qkv, cos_table, sin_table):
    frames, width = normed.shape
    tile = 512
    return pl.pallas_call(
        lambda *refs: project_kernel(2 * width // tile, *refs),
        grid=(3 * width // tile,),
        in_specs=[
            pl.BlockSpec((frames, width), lambda i: (0, 0)),
            pl.BlockSpec((width, tile), lambda i: (0, i)),
            pl.BlockSpec((frames, PAIR), lambda i: (0, 0)),
            pl.BlockSpec((frames, PAIR), lambda i: (0, 0)),
        ],
        out_specs=pl.BlockSpec((frames, tile), lambda i: (0, i)),
        out_shape=jax.ShapeDtypeStruct((frames, 3 * width), BF),
        compiler_params=pltpu.CompilerParams(vmem_limit_bytes=VMEM_BYTES),
        cost_estimate=pl.CostEstimate(
            flops=6 * frames * width * width,
            bytes_accessed=6 * width * width + 8 * frames * width,
            transcendentals=0,
        ),
    )(normed, w_qkv, cos_table, sin_table)


def head_lanes(shape, which):
    lanes = lax.broadcasted_iota(jnp.int32, shape, 1)
    return (lanes >= which * HD) & (lanes < (which + 1) * HD)


def attend_kernel(span, block, q_ref, *refs):
    k_refs, v_refs = refs[:span], refs[span : 2 * span]
    sq_ref, sk_ref, o_ref, p_ref, bias_ref = refs[2 * span :]
    frames = q_ref.shape[0]

    @pl.when(pl.program_id(0) == 0)
    def _():
        seg_q, place_q = sq_ref[:, 0:1], sq_ref[:, 1:2]
        for first in range(0, bias_ref.shape[1], frames):
            here = slice(first, first + frames)
            seg_k, place_k, live_k = sk_ref[0:1, here], sk_ref[1:2, here], sk_ref[2:3, here]
            allowed = (seg_q == seg_k) & ((live_k == 1) | (place_q == place_k))
            bias_ref[:, here] = jnp.where(allowed, 0.0, neg_fill)

    for first in range(0, frames, block):
        rows = slice(first, first + block)
        queries = q_ref[rows, :] * jnp.asarray(HD ** (-0.5), BF)
        kept = None
        for which in range(2):
            mine = head_lanes(queries.shape, which)
            one = jnp.where(mine, queries, jnp.zeros_like(queries))
            scores = jnp.concatenate([dot(one, k[...], DIMS_LAST) for k in k_refs], axis=1)
            scores = scores + bias_ref[rows, :]
            powered = jnp.exp(scores - jnp.max(scores, axis=1, keepdims=True))
            probs = (powered * (1.0 / jnp.sum(powered, axis=1, keepdims=True))).astype(BF)
            p_ref[which, rows, :] = probs
            result = None
            for index, v in enumerate(v_refs):
                part = dot(probs[:, index * frames : (index + 1) * frames], v[...])
                result = part if result is None else result + part
            kept = result if kept is None else jnp.where(mine, result, kept)
        o_ref[rows, :] = kept.astype(BF)


def attend(packed, others, meta_q, meta_k):
    span = len(others) + 1
    frames, width = packed.shape[0], packed.shape[1] // 3
    pairs = width // PAIR
    keys = span * frames

    def column(start):
        return pl.BlockSpec((frames, PAIR), lambda i, start=start: (0, start + i))

    return pl.pallas_call(
        lambda *refs: attend_kernel(span, 128, *refs),
        grid=(pairs,),
        in_specs=[column(0), column(pairs)]
        + [column(0)] * (span - 1)
        + [column(2 * pairs)]
        + [column(pairs)] * (span - 1)
        + [
            pl.BlockSpec((frames, PAIR), lambda i: (0, 0)),
            pl.BlockSpec((8, keys), lambda i: (0, 0)),
        ],
        out_specs=[
            column(0),
            pl.BlockSpec((2, frames, keys), lambda i: (i, 0, 0)),
        ],
        out_shape=[
            jax.ShapeDtypeStruct((frames, width), BF),
            jax.ShapeDtypeStruct((2 * pairs, frames, keys), BF),
        ],
        scratch_shapes=[pltpu.VMEM((frames, keys), F32)],
        compiler_params=pltpu.CompilerParams(vmem_limit_bytes=VMEM_BYTES),
        cost_estimate=pl.CostEstimate(
            flops=16 * pairs * frames * keys * PAIR,
            bytes_accessed=4 * pairs * frames * keys,
            transcendentals=2 * pairs * frames * keys,
        ),
    )(packed, packed, *others, packed, *others, meta_q, meta_k)


def attend_back_kernel(span, block, q_ref, *refs):
    k_refs, v_refs = refs[:span], refs[span : 2 * span]
    p_ref, o_ref, g_ref, cos_ref, sin_ref = refs[2 * span : 2 * span + 5]
    dq_ref = refs[2 * span + 5]
    dk_refs = refs[2 * span + 6 : 3 * span + 6]
    dv_refs = refs[3 * span + 6 : 4 * span + 6]
    ds_ref = refs[4 * span + 6]
    frames = q_ref.shape[0]
    factor = jnp.asarray(HD ** (-0.5), BF)

    def unturn(grad, index):
        rows = slice(index * frames, (index + 1) * frames)
        return grad * cos_ref[rows, :] - turn(grad) * sin_ref[rows, :]

    dk, dv, dq = [None] * span, [None] * span, None
    for which in range(2):
        mine = head_lanes(g_ref.shape, which)
        grads = jnp.where(mine, g_ref[...], jnp.zeros(g_ref.shape, BF))
        queries = jnp.where(mine, q_ref[...] * factor, jnp.zeros(g_ref.shape, BF))
        centre = jnp.sum(grads.astype(F32) * o_ref[...].astype(F32), axis=1, keepdims=True)
        for first in range(0, frames, block):
            rows = slice(first, first + block)
            for index in range(span):
                columns = slice(index * frames, (index + 1) * frames)
                grad_probs = dot(grads[rows, :], v_refs[index][...], DIMS_LAST)
                soft = p_ref[which, rows, columns].astype(F32)
                ds_ref[rows, columns] = (soft * (grad_probs - centre[rows, :])).astype(BF)
        result = None
        for index in range(span):
            columns = slice(index * frames, (index + 1) * frames)
            grad_scores = ds_ref[:, columns]
            part = dot(grad_scores, k_refs[index][...])
            result = part if result is None else result + part
            part = dot(grad_scores, queries, DIMS_FIRST)
            dk[index] = part if dk[index] is None else dk[index] + part
            part = dot(p_ref[which, :, columns], grads, DIMS_FIRST)
            dv[index] = part if dv[index] is None else dv[index] + part
        dq = result if dq is None else jnp.where(mine, result, dq)
    dq_ref[...] = unturn(dq * HD ** (-0.5), 0).astype(BF)
    for index in range(span):
        dk_refs[index][...] = unturn(dk[index], index).astype(BF)
        dv_refs[index][...] = dv[index].astype(BF)


def attend_back(packed, others, probs, attended, grads, cos_keys, sin_keys):
    span = len(others) + 1
    frames, width = packed.shape[0], packed.shape[1] // 3
    pairs = width // PAIR
    keys = span * frames

    def column(start):
        return pl.BlockSpec((frames, PAIR), lambda i, start=start: (0, start + i))

    out = jax.ShapeDtypeStruct((frames, width), BF)
    results = pl.pallas_call(
        lambda *refs: attend_back_kernel(span, 128, *refs),
        grid=(pairs,),
        in_specs=[column(0), column(pairs)]
        + [column(0)] * (span - 1)
        + [column(2 * pairs)]
        + [column(pairs)] * (span - 1)
        + [
            pl.BlockSpec((2, frames, keys), lambda i: (i, 0, 0)),
            column(0),
            column(0),
            pl.BlockSpec((keys, PAIR), lambda i: (0, 0)),
            pl.BlockSpec((keys, PAIR), lambda i: (0, 0)),
        ],
        out_specs=[column(0)] * (2 * span + 1),
        out_shape=[out] * (2 * span + 1),
        scratch_shapes=[pltpu.VMEM((frames, keys), BF)],
        compiler_params=pltpu.CompilerParams(vmem_limit_bytes=VMEM_BYTES),
        cost_estimate=pl.CostEstimate(
            flops=32 * pairs * frames * keys * PAIR,
            bytes_accessed=4 * pairs * frames * keys,
            transcendentals=0,
        ),
    )(packed, packed, *others, packed, *others, probs, attended, grads, cos_keys, sin_keys)
    return results[0], results[1 : span + 1], results[span + 1 :]


def per_device(
    inputs,
    skips,
    flow_time,
    segment_ids,
    frame_mask,
    cotangent,
    w_skip,
    w_time,
    w_qkv,
    w_out,
    w_up,
    w_down,
):
    groups = lax.axis_size("head")
    micro_count, _, rows, width = inputs.shape
    span = groups // micro_count
    place = lax.axis_index("head")
    mine = place // span
    frames = micro_count * rows

    joined = jnp.concatenate([inputs[:, 0], skips[:, 0]], axis=2)
    resid_local = dot(joined.reshape(frames, 2 * width), w_skip).astype(BF)
    resid_in = to_buckets(resid_local.reshape(micro_count, rows, width), span, mine)
    resid_in = resid_in.reshape(frames, width).astype(F32)
    later = jnp.concatenate([cotangent[:, 0], joined], axis=2)
    later = to_buckets(later, span, mine).reshape(frames, 3 * width)
    cot_rows, joined = later[:, :width], later[:, width:]

    meta = jnp.stack(
        [segment_ids[:, 0].astype(F32), frame_mask[:, 0].astype(F32), flow_time[:, 0]]
    )
    meta = lax.all_gather(meta, "head", axis=0)
    meta = pick(meta, mine, 2)
    order = jnp.stack(
        [place ^ other ^ (step * span) for other in range(span) for step in range(micro_count)]
    )
    seg_bucket = meta[:, 0].reshape(-1)
    meta = jnp.take(meta, order, axis=0)
    seg_keys = meta[:, 0].reshape(-1)
    live_keys = meta[:, 1].reshape(-1)
    place_keys = (order[:, None] * rows + jnp.arange(rows)[None, :]).reshape(-1).astype(F32)
    starts = jnp.sum((seg_bucket[None, :] < seg_keys[:, None]).astype(F32), axis=1)
    positions = place_keys - starts
    times = meta[:micro_count, 2].reshape(-1)

    feature_count = w_time.shape[0]
    half = feature_count // 2
    steps = jnp.exp(jnp.arange(half, dtype=F32) * (-math.log(10000.0) / (half - 1)))
    angles = 1000.0 * times[:, None] * steps
    features = jnp.concatenate([jnp.sin(angles), jnp.cos(angles)], axis=-1).astype(BF)
    modulation = dot(features, w_time)
    shift_first, scale_first, shift_second, scale_second = jnp.split(modulation, 4, axis=1)

    inv_freq = jnp.exp(jnp.arange(HD // 2, dtype=F32) * (-2.0 * math.log(10000.0) / HD))
    turns = positions[:, None] * inv_freq
    cos_half, sin_half = jnp.cos(turns), jnp.sin(turns)
    cos_keys = jnp.concatenate([cos_half] * 4, axis=1)
    sin_keys = jnp.concatenate([-sin_half, sin_half] * 2, axis=1)

    normal_first, rate_first = norm_stats(resid_in)
    normed_attn = (normal_first * (1.0 + scale_first) + shift_first).astype(BF)
    packed = project(normed_attn, w_qkv, cos_keys[:frames], sin_keys[:frames])
    others = [swap(packed[:, width:], "head", other) for other in range(1, span)]
    meta_q = jnp.concatenate(
        [seg_keys[:frames, None], place_keys[:frames, None], jnp.zeros((frames, PAIR - 2), F32)],
        axis=1,
    )
    meta_k = jnp.stack([seg_keys, place_keys, live_keys] + [jnp.zeros_like(seg_keys)] * 5)
    attended, probs = attend(packed, others, meta_q, meta_k)
    resid_mid = resid_in + dot(attended, w_out)

    normal_second, rate_second = norm_stats(resid_mid)
    normed_ffn = (normal_second * (1.0 + scale_second) + shift_second).astype(BF)
    up_proj = dot(normed_ffn, w_up)
    activated, pull_gelu = jax.vjp(lambda v: jax.nn.gelu(v, approximate=True), up_proj)
    hidden = activated.astype(BF)
    output = (resid_mid + dot(hidden, w_down)).astype(BF)
    output = from_buckets(output.reshape(micro_count, rows, width), span, mine)

    total_down = weight_grad(hidden, cot_rows, False)
    grad_up_proj = pull_gelu(dot(cot_rows, w_down, DIMS_LAST))[0].astype(BF)
    total_up = weight_grad(normed_ffn, grad_up_proj, True)
    grad_normed_ffn = dot(grad_up_proj, w_up, DIMS_LAST)
    grad_mid = cot_rows.astype(F32) + norm_back(
        grad_normed_ffn, normal_second, rate_second, scale_second
    )
    grad_mid_low = grad_mid.astype(BF)
    total_out = weight_grad(attended, grad_mid_low, False)
    grad_attended = dot(grad_mid_low, w_out, DIMS_LAST).astype(BF)
    dq, dk, dv = attend_back(packed, others, probs, attended, grad_attended, cos_keys, sin_keys)
    key_sum, value_sum = dk[0].astype(F32), dv[0].astype(F32)
    for other in range(1, span):
        both = swap(jnp.concatenate([dk[other], dv[other]], axis=1), "head", other).astype(F32)
        key_sum, value_sum = key_sum + both[:, :width], value_sum + both[:, width:]
    grad_proj = jnp.concatenate([dq, key_sum.astype(BF), value_sum.astype(BF)], axis=1)
    total_qkv = weight_grad(normed_attn, grad_proj, True)
    grad_normed_attn = dot(grad_proj, w_qkv, DIMS_LAST)
    grad_in_low = (
        grad_mid + norm_back(grad_normed_attn, normal_first, rate_first, scale_first)
    ).astype(BF)
    total_skip = weight_grad(joined, grad_in_low, False)
    grad_modulation = jnp.concatenate(
        [
            grad_normed_attn,
            grad_normed_attn * normal_first,
            grad_normed_ffn,
            grad_normed_ffn * normal_second,
        ],
        axis=1,
    ).astype(BF)
    total_time = weight_grad(features, grad_modulation, False)
    grad_local = from_buckets(grad_in_low.reshape(micro_count, rows, width), span, mine)
    grad_local = grad_local.reshape(frames, width)
    shape = (micro_count, 1, rows, width)
    input_grad = dot(grad_local, w_skip[:width], DIMS_LAST).reshape(shape)
    skip_grad = dot(grad_local, w_skip[width:], DIMS_LAST).reshape(shape)
    return (
        output[:, None],
        input_grad,
        skip_grad,
        total_skip,
        total_time,
        total_qkv,
        total_out,
        total_up,
        total_down,
    )


def solution(mesh):
    frames_spec = P(None, "seq", "head", None)
    line_spec = P(None, "seq", "head")
    shard_spec = P(("head", "seq"), None)
    return jax.shard_map(
        per_device,
        mesh=mesh,
        in_specs=(frames_spec, frames_spec, line_spec, line_spec, line_spec, frames_spec)
        + (P(),) * 6,
        out_specs=(frames_spec,) * 3 + (shard_spec,) * 6,
        check_vma=False,
    )
```

```python
import functools
import math

import jax
import jax.numpy as jnp
from jax import lax
from jax.experimental import pallas as pl
from jax.experimental.pallas import tpu as pltpu
from jax.sharding import PartitionSpec as P

HD = 64
PAIR = 2 * HD
eps_norm = 1e-06
neg_fill = -1e30
BF = jnp.bfloat16
F32 = jnp.float32
DIMS_FIRST = (((0,), (0,)), ((), ()))
DIMS_LAST = (((1,), (1,)), ((), ()))
LOG2E = 1.4426950408889634
VMEM_BYTES = 56 * 1024 * 1024


def dot(left, right, dims=(((1,), (0,)), ((), ()))):
    return lax.dot_general(left, right, dims, preferred_element_type=F32)


def swap(values, axis_name, bits):
    size = lax.axis_size(axis_name)
    return lax.ppermute(values, axis_name, [(i, i ^ bits) for i in range(size)])


def pick(values, index, axis):
    return lax.dynamic_index_in_dim(values, index, axis, keepdims=False)


def after(value, *others):
    return lax.optimization_barrier((value, *others))[0]


def to_buckets(parts, span, mine):
    got = [pick(parts, mine, 0)]
    for step in range(1, parts.shape[0]):
        got.append(swap(pick(parts, mine ^ step, 0), "head", step * span))
    return got


def from_buckets(parts, span, mine):
    count = parts.shape[0]
    got = [parts[0]]
    for step in range(1, count):
        got.append(swap(parts[step], "head", step * span))
    got = jnp.stack(got)
    return jnp.stack([pick(got, mine ^ micro, 0) for micro in range(count)])


def core_sum(away, keep):
    return (keep.astype(F32) + swap(away, "head", 1).astype(F32)).astype(BF)


def scatter(total, descending):
    groups = lax.axis_size("head")
    place = lax.axis_index("head")
    width = total.shape[1]
    chunk = total.shape[0] // (groups // 2)
    remaining = list(range(1, groups.bit_length() - 1))
    for bit in remaining[::-1] if descending else list(remaining):
        tail = 2 ** len([b for b in remaining if b < bit]) * chunk
        view = total.reshape(-1, 2, tail, width)
        here = (place >> bit) % 2
        came = swap(pick(view, 1 - here, 1), "head", 2**bit)
        total = (pick(view, here, 1).astype(F32) + came.astype(F32)).astype(BF)
        remaining.remove(bit)
    total = total.reshape(chunk, width)
    return lax.psum_scatter(total, "seq", scatter_dimension=0, tiled=True).astype(F32)


def norm_stats(hidden):
    centred = hidden - jnp.mean(hidden, axis=-1, keepdims=True)
    rate = lax.rsqrt(jnp.mean(centred * centred, axis=-1, keepdims=True) + eps_norm)
    return centred * rate, rate


def norm_back(grad, normal, rate, scale_term):
    inner = grad * (1.0 + scale_term)
    return rate * (
        inner
        - jnp.mean(inner, axis=-1, keepdims=True)
        - normal * jnp.mean(inner * normal, axis=-1, keepdims=True)
    )


def time_features(times, feature_count):
    half = feature_count // 2
    steps = jnp.exp(jnp.arange(half, dtype=F32) * (-math.log(10000.0) / (half - 1)))
    angles = 1000.0 * times[:, None] * steps
    return jnp.concatenate([jnp.sin(angles), jnp.cos(angles)], axis=-1).astype(BF)


def params():
    return pltpu.CompilerParams(vmem_limit_bytes=VMEM_BYTES)


def cost(flops, moved, hard=0):
    return pl.CostEstimate(flops=int(flops), bytes_accessed=int(moved), transcendentals=int(hard))


def turn(values):
    lanes = lax.broadcasted_iota(jnp.int32, values.shape, 1)
    low = lax.rem(lanes, HD) < HD // 2
    return jnp.where(low, pltpu.roll(values, PAIR - HD // 2, 1), pltpu.roll(values, HD // 2, 1))


def project_kernel(tiles, x_ref, w_ref, cos_ref, sin_ref, o_ref):
    raw = dot(x_ref[...], w_ref[...])

    @pl.when(pl.program_id(0) < 2 * tiles)
    def _():
        factor = jnp.where(pl.program_id(0) < tiles, HD ** (-0.5) * LOG2E, 1.0)
        for first in range(0, raw.shape[1], PAIR):
            part = raw[:, first : first + PAIR]
            turned = part * cos_ref[...] + turn(part) * sin_ref[...]
            o_ref[:, first : first + PAIR] = (turned * factor).astype(BF)

    @pl.when(pl.program_id(0) >= 2 * tiles)
    def _():
        o_ref[...] = raw.astype(BF)


def project(normed, w_qkv, cos_table, sin_table):
    frames, width = normed.shape
    tile = 512
    return pl.pallas_call(
        functools.partial(project_kernel, width // tile),
        grid=(3 * width // tile,),
        in_specs=[
            pl.BlockSpec((frames, width), lambda i: (0, 0)),
            pl.BlockSpec((width, tile), lambda i: (0, i)),
            pl.BlockSpec((frames, PAIR), lambda i: (0, 0)),
            pl.BlockSpec((frames, PAIR), lambda i: (0, 0)),
        ],
        out_specs=pl.BlockSpec((frames, tile), lambda i: (0, i)),
        out_shape=jax.ShapeDtypeStruct((frames, 3 * width), BF),
        compiler_params=params(),
        cost_estimate=cost(6 * frames * width * width, 6 * width * width + 8 * frames * width),
    )(normed, w_qkv, cos_table, sin_table)


def only_head(values, which):
    lanes = lax.broadcasted_iota(jnp.int32, values.shape, 1)
    mine = (lanes >= which * HD) & (lanes < (which + 1) * HD)
    return jnp.where(mine, values, jnp.zeros_like(values))


def attend_kernel(span, q_ref, *refs):
    k_refs, v_refs = refs[:span], refs[span : 2 * span]
    mk_ref, mq_ref, o_ref, p_ref, l_ref, bias_ref = refs[2 * span :]
    frames = q_ref.shape[0]

    @pl.when(pl.program_id(0) == 0)
    def _():
        seg_q, place_q = mq_ref[0:1, :], mq_ref[1:2, :]
        for index in range(span):
            rows = slice(index * frames, (index + 1) * frames)
            seg_k, place_k, live_k = mk_ref[rows, 0:1], mk_ref[rows, 1:2], mk_ref[rows, 2:3]
            allowed = (seg_q == seg_k) & ((live_k == 1) | (place_q == place_k))
            bias_ref[rows, :] = jnp.where(allowed, 0.0, neg_fill)

    values_t = [v[...].T for v in v_refs]
    ones = jnp.ones((16, frames), BF)
    results, inverses = [], []
    for which in range(2):
        queries = only_head(q_ref[...], which)
        scores = [
            dot(k[...], queries, DIMS_LAST) + bias_ref[i * frames : (i + 1) * frames, :]
            for i, k in enumerate(k_refs)
        ]
        top = functools.reduce(jnp.maximum, [jnp.max(s, axis=0, keepdims=True) for s in scores])
        result = None
        for index, part in enumerate(scores):
            powered = jnp.exp2(part - top).astype(BF)
            p_ref[which, index * frames : (index + 1) * frames, :] = powered
            lanes = values_t[index][which * HD : (which + 1) * HD]
            part = dot(jnp.concatenate([lanes, ones], axis=0), powered)
            result = part if result is None else result + part
        inverse = 1.0 / result[HD : HD + 1]
        results.append(result[:HD] * inverse)
        inverses.append(inverse)
    o_ref[...] = jnp.concatenate(results, axis=0).T.astype(BF)
    l_ref[0] = jnp.concatenate(inverses + [jnp.zeros((6, frames), F32)], axis=0)


def columns(frames, start=0):
    return pl.BlockSpec((frames, PAIR), lambda i: (0, start + i))


def attend(packed, others, meta_k, meta_q):
    span = len(others) + 1
    frames, width = packed.shape[0], packed.shape[1] // 3
    pairs = width // PAIR
    keys = span * frames
    return pl.pallas_call(
        functools.partial(attend_kernel, span),
        grid=(pairs,),
        in_specs=[columns(frames), columns(frames, pairs)]
        + [columns(frames)] * (span - 1)
        + [columns(frames, 2 * pairs)]
        + [columns(frames, pairs)] * (span - 1)
        + [
            pl.BlockSpec((keys, PAIR), lambda i: (0, 0)),
            pl.BlockSpec((8, frames), lambda i: (0, 0)),
        ],
        out_specs=[
            columns(frames),
            pl.BlockSpec((2, keys, frames), lambda i: (i, 0, 0)),
            pl.BlockSpec((1, 8, frames), lambda i: (i, 0, 0)),
        ],
        out_shape=[
            jax.ShapeDtypeStruct((frames, width), BF),
            jax.ShapeDtypeStruct((2 * pairs, keys, frames), BF),
            jax.ShapeDtypeStruct((pairs, 8, frames), F32),
        ],
        scratch_shapes=[pltpu.VMEM((keys, frames), F32)],
        compiler_params=params(),
        cost_estimate=cost(
            16 * pairs * frames * keys * PAIR,
            4 * pairs * frames * keys,
            2 * pairs * frames * keys,
        ),
    )(packed, packed, *others, packed, *others, meta_k, meta_q)


def grad_heads_kernel(g_ref, w_ref, a_ref, l_ref, o_ref, c_ref):
    grads = dot(g_ref[...], w_ref[...], DIMS_LAST)
    for pair in range(l_ref.shape[0]):
        lanes = slice(pair * PAIR, (pair + 1) * PAIR)
        own = lax.broadcasted_iota(jnp.int32, (8, PAIR), 1) // HD
        own = (own == lax.broadcasted_iota(jnp.int32, (8, PAIR), 0)).astype(F32)
        spread = lax.dot_general(
            l_ref[pair], own, DIMS_FIRST, precision=lax.Precision.HIGHEST, preferred_element_type=F32
        )
        scaled = grads[:, lanes] * spread
        o_ref[:, lanes] = scaled.astype(BF)
        c_ref[pair] = lax.dot_general(
            own,
            scaled * a_ref[:, lanes].astype(F32),
            DIMS_LAST,
            precision=lax.Precision.HIGHEST,
            preferred_element_type=F32,
        )


def grad_heads(grad_low, w_out, attended, inverses):
    frames, width = grad_low.shape
    pairs = width // PAIR
    tile = 2
    return pl.pallas_call(
        grad_heads_kernel,
        grid=(pairs // tile,),
        in_specs=[
            pl.BlockSpec((frames, width), lambda i: (0, 0)),
            pl.BlockSpec((tile * PAIR, width), lambda i: (i, 0)),
            pl.BlockSpec((frames, tile * PAIR), lambda i: (0, i)),
            pl.BlockSpec((tile, 8, frames), lambda i: (i, 0, 0)),
        ],
        out_specs=[
            pl.BlockSpec((frames, tile * PAIR), lambda i: (0, i)),
            pl.BlockSpec((tile, 8, frames), lambda i: (i, 0, 0)),
        ],
        out_shape=[
            jax.ShapeDtypeStruct((frames, width), BF),
            jax.ShapeDtypeStruct((pairs, 8, frames), F32),
        ],
        compiler_params=params(),
        cost_estimate=cost(2 * frames * width * width, 2 * width * width + 6 * frames * width),
    )(grad_low, w_out, attended, inverses)


def attend_back_kernel(span, q_ref, *refs):
    k_refs, v_refs = refs[:span], refs[span : 2 * span]
    p_ref, c_ref, g_ref, cos_ref, sin_ref = refs[2 * span : 2 * span + 5]
    dq_ref = refs[2 * span + 5]
    dk_refs = refs[2 * span + 6 : 3 * span + 6]
    dv_refs = refs[3 * span + 6 : 4 * span + 6]
    ds_ref = refs[4 * span + 6]
    frames = q_ref.shape[0]

    def unturn(grad, index):
        rows = slice(index * frames, (index + 1) * frames)
        return grad * cos_ref[rows, :] - turn(grad) * sin_ref[rows, :]

    keys_t = [k[...].T for k in k_refs]
    dk, dv, dq = [None] * span, [None] * span, []
    for which in range(2):
        centre = c_ref[0, which : which + 1, :]
        grads = only_head(g_ref[...], which)
        queries = only_head(q_ref[...], which)
        result = None
        for index in range(span):
            rows = slice(index * frames, (index + 1) * frames)
            grad_probs = dot(v_refs[index][...], grads, DIMS_LAST)
            soft = p_ref[which, rows, :]
            ds_ref[rows, :] = (soft.astype(F32) * (grad_probs - centre)).astype(BF)
            part = dot(soft, grads)
            dv[index] = part if dv[index] is None else dv[index] + part
            part = dot(ds_ref[rows, :], queries)
            dk[index] = part if dk[index] is None else dk[index] + part
            part = dot(keys_t[index][which * HD : (which + 1) * HD], ds_ref[rows, :])
            result = part if result is None else result + part
        dq.append(result)
    dq = jnp.concatenate(dq, axis=0).T
    dq_ref[...] = unturn(dq * HD ** (-0.5), 0).astype(BF)
    for index in range(span):
        dk_refs[index][...] = unturn(dk[index] * (1.0 / LOG2E), index).astype(BF)
        dv_refs[index][...] = dv[index].astype(BF)


def attend_back(packed, others, probs, centres, grads, cos_keys, sin_keys):
    span = len(others) + 1
    frames, width = packed.shape[0], packed.shape[1] // 3
    pairs = width // PAIR
    keys = span * frames
    out = jax.ShapeDtypeStruct((frames, width), BF)
    results = pl.pallas_call(
        functools.partial(attend_back_kernel, span),
        grid=(pairs,),
        in_specs=[columns(frames), columns(frames, pairs)]
        + [columns(frames)] * (span - 1)
        + [columns(frames, 2 * pairs)]
        + [columns(frames, pairs)] * (span - 1)
        + [
            pl.BlockSpec((2, keys, frames), lambda i: (i, 0, 0)),
            pl.BlockSpec((1, 8, frames), lambda i: (i, 0, 0)),
            columns(frames),
            pl.BlockSpec((keys, PAIR), lambda i: (0, 0)),
            pl.BlockSpec((keys, PAIR), lambda i: (0, 0)),
        ],
        out_specs=[columns(frames)] * (2 * span + 1),
        out_shape=[out] * (2 * span + 1),
        scratch_shapes=[pltpu.VMEM((keys, frames), BF)],
        compiler_params=params(),
        cost_estimate=cost(32 * pairs * frames * keys * PAIR, 4 * pairs * frames * keys),
    )(packed, packed, *others, packed, *others, probs, centres, grads, cos_keys, sin_keys)
    return results[0], results[1 : span + 1], results[span + 1 :]


def split_rows(source, target, groups, low_bit):
    chunk = source.shape[0] // groups
    half = source.shape[0] // 2
    for index in range(groups // 2):
        for part, bit in ((0, 1 - low_bit), (1, low_bit)):
            first = pl.multiple_of((2 * index + bit) * chunk, chunk)
            start = part * half + index * chunk
            target[start : start + chunk, :] = source[pl.ds(first, chunk), :]


def feed_kernel(groups, x_ref, g_ref, up_ref, down_ref, *refs):
    acc_ref, gx_ref, da_ref, dk_ref, ua_ref, uk_ref, t_ref, xt_ref = refs
    step = pl.program_id(0)
    low_bit = lax.axis_index("head") % 2

    @pl.when(step == 0)
    def _():
        t_ref[...] = x_ref[...].T
        split_rows(t_ref, xt_ref, groups, low_bit)
        acc_ref[...] = jnp.zeros_like(acc_ref)
        gx_ref[...] = jnp.zeros_like(gx_ref)

    up = dot(x_ref[...], up_ref[...])
    grad_hidden = dot(g_ref[...], down_ref[...], DIMS_LAST)
    root = math.sqrt(2.0 / math.pi)
    square = up * up
    bent = jnp.tanh(root * up * (1.0 + 0.044715 * square))
    half = 0.5 + 0.5 * bent
    slope = half + 0.5 * up * (1.0 - bent * bent) * (root * (1.0 + 3 * 0.044715 * square))
    hidden = (up * half).astype(BF)
    grad_up = (grad_hidden * slope).astype(BF)
    acc_ref[...] += dot(hidden, down_ref[...])
    gx_ref[...] += dot(grad_up, up_ref[...], DIMS_LAST)
    rows = dot(hidden, g_ref[...], DIMS_FIRST).astype(BF)

    @pl.when(step % 2 == low_bit)
    def _():
        dk_ref[...] = rows

    @pl.when(step % 2 != low_bit)
    def _():
        da_ref[...] = rows

    depth = x_ref.shape[1] // 2
    ua_ref[...] = dot(xt_ref[:depth, :], grad_up).astype(BF)
    uk_ref[...] = dot(xt_ref[depth:, :], grad_up).astype(BF)


def feed(normed, grads, w_up, w_down):
    groups = lax.axis_size("head")
    frames, width = normed.shape
    inner = w_up.shape[1]
    tile = inner // groups
    whole = pl.BlockSpec((frames, width), lambda i: (0, 0))
    rows = pl.BlockSpec((tile, width), lambda i: (i // 2, 0))
    cols = pl.BlockSpec((width // 2, tile), lambda i: (0, i))
    total = jax.ShapeDtypeStruct((frames, width), F32)
    down = jax.ShapeDtypeStruct((inner // 2, width), BF)
    up = jax.ShapeDtypeStruct((width // 2, inner), BF)
    return pl.pallas_call(
        functools.partial(feed_kernel, groups),
        grid=(groups,),
        in_specs=[
            whole,
            whole,
            pl.BlockSpec((width, tile), lambda i: (0, i)),
            pl.BlockSpec((tile, width), lambda i: (i, 0)),
        ],
        out_specs=[whole, whole, rows, rows, cols, cols],
        out_shape=[total, total, down, down, up, up],
        scratch_shapes=[pltpu.VMEM((width, frames), BF), pltpu.VMEM((width, frames), BF)],
        compiler_params=params(),
        cost_estimate=cost(12 * frames * width * inner, 8 * width * inner, frames * inner),
    )(normed, grads, w_up, w_down)


def weight_kernel(groups, x_ref, g_ref, away_ref, keep_ref, t_ref, xt_ref):
    @pl.when(pl.program_id(0) == 0)
    def _():
        t_ref[...] = x_ref[...].T
        split_rows(t_ref, xt_ref, groups, lax.axis_index("head") % 2)

    half = x_ref.shape[1] // 2
    away_ref[...] = dot(xt_ref[:half, :], g_ref[...]).astype(BF)
    keep_ref[...] = dot(xt_ref[half:, :], g_ref[...]).astype(BF)


def weight_grad(left, right):
    groups = lax.axis_size("head")
    frames, rows = left.shape
    width = right.shape[1]
    tile = 512
    spec = pl.BlockSpec((rows // 2, tile), lambda i: (0, i))
    out = jax.ShapeDtypeStruct((rows // 2, width), BF)
    return pl.pallas_call(
        functools.partial(weight_kernel, groups),
        grid=(width // tile,),
        in_specs=[
            pl.BlockSpec((frames, rows), lambda i: (0, 0)),
            pl.BlockSpec((frames, tile), lambda i: (0, i)),
        ],
        out_specs=[spec, spec],
        out_shape=[out, out],
        scratch_shapes=[pltpu.VMEM((rows, frames), BF), pltpu.VMEM((rows, frames), BF)],
        compiler_params=params(),
        cost_estimate=cost(
            2 * frames * rows * width, 2 * rows * width + 2 * frames * (rows + width)
        ),
    )(left, right)


def per_device(
    inputs,
    skips,
    flow_time,
    segment_ids,
    frame_mask,
    cotangent,
    w_skip,
    w_time,
    w_qkv,
    w_out,
    w_up,
    w_down,
):
    groups = lax.axis_size("head")
    micro_count, _, rows, width = inputs.shape
    span = groups // micro_count
    place = lax.axis_index("head")
    mine = place // span
    frames = micro_count * rows
    feature_count = w_time.shape[0]
    inputs, skips, cotangent = inputs[:, 0], skips[:, 0], cotangent[:, 0]

    resid_own = dot(inputs.reshape(frames, width), w_skip[:width]) + dot(
        skips.reshape(frames, width), w_skip[width:]
    )
    own_mod = dot(time_features(flow_time.reshape(-1), feature_count), w_time[:, : 2 * width])
    normed_own = norm_stats(resid_own)[0] * (1.0 + own_mod[:, width:]) + own_mod[:, :width]
    normed_own = normed_own.astype(BF).reshape(micro_count, rows, width)

    meta = jnp.stack(
        [segment_ids[:, 0].astype(F32), frame_mask[:, 0].astype(F32), flow_time[:, 0]], axis=1
    )
    meta = [meta] + [swap(meta, "head", other) for other in range(1, span)]
    meta = jnp.stack(to_buckets(jnp.stack(meta, axis=1), span, mine))
    seg_keys, live_keys, times = [meta[:, :, i].swapaxes(0, 1).reshape(-1) for i in range(3)]
    order = jnp.stack(
        [place ^ other ^ (step * span) for other in range(span) for step in range(micro_count)]
    )
    place_keys = (order[:, None] * rows + jnp.arange(rows)[None, :]).reshape(-1).astype(F32)
    starts = jnp.sum((seg_keys[None, :] < seg_keys[:, None]).astype(F32), axis=1)
    positions = place_keys - starts
    inv_freq = jnp.exp(jnp.arange(HD // 2, dtype=F32) * (-2.0 * math.log(10000.0) / HD))
    turns = positions[:, None] * inv_freq
    cos_half, sin_half = jnp.cos(turns), jnp.sin(turns)
    cos_keys = jnp.concatenate([cos_half] * 4, axis=1)
    sin_keys = jnp.concatenate([-sin_half, sin_half] * 2, axis=1)
    meta_q = jnp.stack(
        [seg_keys[:frames], place_keys[:frames]] + [jnp.zeros((frames,), F32)] * 6
    )
    meta_k = jnp.stack([seg_keys, place_keys, live_keys], axis=1)
    meta_k = jnp.pad(meta_k, ((0, 0), (0, PAIR - 3)))
    features = time_features(times[:frames], feature_count)
    modulation = dot(features, w_time)
    scale_first = modulation[:, width : 2 * width]
    shift_second = modulation[:, 2 * width : 3 * width]
    scale_second = modulation[:, 3 * width :]

    normed_attn = jnp.concatenate(to_buckets(normed_own, span, mine))
    second = jnp.stack(
        [cotangent, resid_own.astype(BF).reshape(micro_count, rows, width)], axis=1
    )
    second = to_buckets(after(second, normed_attn), span, mine)
    cot_rows = jnp.concatenate([part[0] for part in second])
    resid_in = jnp.concatenate([part[1] for part in second])

    packed = project(normed_attn, w_qkv, cos_keys[:frames], sin_keys[:frames])
    others = [swap(packed[:, width:], "head", other) for other in range(1, span)]
    attended, probs, inverses = attend(packed, others, meta_k, meta_q)
    resid_in, cot_rows, attended = lax.optimization_barrier((resid_in, cot_rows, attended))
    joined = to_buckets(after(jnp.concatenate([inputs, skips], axis=2), resid_in), span, mine)
    joined = jnp.concatenate(joined)
    resid_in = resid_in.astype(F32)
    resid_mid = resid_in + dot(attended, w_out)
    normal_second, rate_second = norm_stats(resid_mid)
    normed_ffn = (normal_second * (1.0 + scale_second) + shift_second).astype(BF)
    fed, grad_normed_ffn, down_away, down_keep, up_away, up_keep = feed(
        normed_ffn, cot_rows, w_up, w_down
    )
    down_sum, up_sum = core_sum(down_away, down_keep), core_sum(up_away, up_keep)
    total_down, total_up = scatter(down_sum, False), scatter(up_sum, True)
    output = (resid_mid + fed).astype(BF)
    output = from_buckets(output.reshape(micro_count, rows, width), span, mine)

    grad_mid = cot_rows.astype(F32) + norm_back(
        grad_normed_ffn, normal_second, rate_second, scale_second
    )
    grad_mid_low = grad_mid.astype(BF)
    grads, centres = grad_heads(grad_mid_low, w_out, attended, inverses)
    out_away, out_keep = weight_grad(attended, grad_mid_low)
    grads, down_sum, up_sum, out_away = lax.optimization_barrier((grads, down_sum, up_sum, out_away))
    total_out = scatter(core_sum(out_away, out_keep), False)
    dq, dk, dv = attend_back(packed, others, probs, centres, grads, cos_keys, sin_keys)
    key_sum, value_sum = dk[0].astype(F32), dv[0].astype(F32)
    for other in range(1, span):
        both = swap(jnp.stack([dk[other], dv[other]]), "head", other).astype(F32)
        key_sum, value_sum = key_sum + both[0], value_sum + both[1]
    grad_proj = jnp.concatenate([dq, key_sum.astype(BF), value_sum.astype(BF)], axis=1)
    total_qkv = scatter(core_sum(*weight_grad(normed_attn, grad_proj)), True)
    grad_normed_attn = dot(grad_proj, w_qkv, DIMS_LAST)
    normal_first, rate_first = norm_stats(resid_in)
    grad_in_low = (
        grad_mid + norm_back(grad_normed_attn, normal_first, rate_first, scale_first)
    ).astype(BF)
    total_skip = scatter(core_sum(*weight_grad(joined, grad_in_low)), False)
    grad_modulation = jnp.concatenate(
        [
            grad_normed_attn,
            grad_normed_attn * normal_first,
            grad_normed_ffn,
            grad_normed_ffn * normal_second,
        ],
        axis=1,
    ).astype(BF)
    total_time = scatter(core_sum(*weight_grad(features, grad_modulation)), True)
    grad_local = from_buckets(grad_in_low.reshape(micro_count, rows, width), span, mine)
    grad_local = grad_local.reshape(frames, width)
    shape = (micro_count, 1, rows, width)
    input_grad = dot(grad_local, w_skip[:width], DIMS_LAST).reshape(shape)
    skip_grad = dot(grad_local, w_skip[width:], DIMS_LAST).reshape(shape)
    return (
        output[:, None],
        input_grad,
        skip_grad,
        total_skip,
        total_time,
        total_qkv,
        total_out,
        total_up,
        total_down,
    )


def solution(mesh):
    frames_spec = P(None, "seq", "head", None)
    line_spec = P(None, "seq", "head")
    shard_spec = P(("head", "seq"), None)
    return jax.shard_map(
        per_device,
        mesh=mesh,
        in_specs=(frames_spec, frames_spec, line_spec, line_spec, line_spec, frames_spec)
        + (P(),) * 6,
        out_specs=(frames_spec,) * 3 + (shard_spec,) * 6,
        check_vma=False,
    )
```

```python
import functools
import math

import jax
import jax.numpy as jnp
from jax import lax
from jax.experimental import pallas as pl
from jax.experimental.pallas import tpu as pltpu
from jax.sharding import PartitionSpec as P

HD = 64
PAIR = 2 * HD
eps_norm = 1e-06
neg_fill = -1e30
BF = jnp.bfloat16
F32 = jnp.float32
DIMS_FIRST = (((0,), (0,)), ((), ()))
DIMS_LAST = (((1,), (1,)), ((), ()))
LOG2E = 1.4426950408889634
VMEM_BYTES = 52 * 1024 * 1024


def dot(left, right, dims=(((1,), (0,)), ((), ()))):
    return lax.dot_general(left, right, dims, preferred_element_type=F32)


def swap(values, axis_name, bits):
    size = lax.axis_size(axis_name)
    return lax.ppermute(values, axis_name, [(i, i ^ bits) for i in range(size)])


def pick(values, index, axis):
    return lax.dynamic_index_in_dim(values, index, axis, keepdims=False)


def together(*values):
    return lax.optimization_barrier(values)


def cut_parts(values, mine):
    return [pick(values, mine ^ step, 0) for step in range(values.shape[0])]


def send_parts(parts, span):
    return parts[:1] + [
        swap(part, "head", step * span) for step, part in enumerate(parts) if step > 0
    ]


def from_buckets(parts, span, mine):
    count = parts.shape[0]
    got = [parts[0]]
    for step in range(1, count):
        got.append(swap(parts[step], "head", step * span))
    got = jnp.stack(got)
    return jnp.stack([pick(got, mine ^ micro, 0) for micro in range(count)])


def add_low(terms):
    return functools.reduce(jnp.add, [term.astype(F32) for term in terms]).astype(BF)


class Rows:
    def __init__(self, arrays, bits, before=1, cols=None):
        self.order = sorted(bits, reverse=True)
        self.before, self.arrays = before, []
        self.start, self.size = cols or (0, arrays[0].shape[-1])
        self.chunk = arrays[0].size // arrays[0].shape[-1] // before // 2 ** len(bits)
        for array in arrays:
            self.join(array, self.start)

    def join(self, array, start=0):
        shape = [self.before] + [2] * len(self.order) + [self.chunk, array.shape[-1]]
        self.arrays.append((array.reshape(shape), tuple(self.order), {}, start))

    def read(self, bit=None, index=None):
        terms = []
        for array, bits, picks, start in self.arrays:
            picks = picks if bit is None else {**picks, bit: index}
            starts = [0] + [picks.get(b, 0) for b in bits] + [0, start]
            sizes = [self.before] + [1 if b in picks else 2 for b in bits] + [self.chunk, self.size]
            terms.append(lax.dynamic_slice(array, starts, sizes).reshape(-1, self.size))
        return add_low(terms)

    def away(self, bit):
        here = (place_of() >> bit) % 2
        sent = self.read(bit, 1 - here)
        self.order.remove(bit)
        for _, _, picks, _ in self.arrays:
            picks[bit] = here
        return sent


def place_of():
    return lax.axis_index("head") * lax.axis_size("seq") + lax.axis_index("seq")


def cross(rows, bit):
    seq_bits = lax.axis_size("seq").bit_length() - 1
    if bit < seq_bits:
        return swap(rows, "seq", 2**bit)
    return swap(rows, "head", 2 ** (bit - seq_bits))


def away_all(parts, bit):
    return jnp.concatenate([part.away(bit) for part in parts])


def join_all(parts, came):
    start = 0
    for part in parts:
        height = part.before * part.chunk * 2 ** len(part.order)
        part.join(came[start : start + height])
        start += height


def step_all(parts, bit):
    join_all(parts, cross(away_all(parts, bit), bit))


def last_sum(*rows):
    size = lax.axis_size("seq")
    narrow = min(part.shape[1] for part in rows)
    blocks, counts = [], []
    for part in rows:
        part = part.reshape(size, -1, part.shape[1])
        counts.append((part.shape[1], part.shape[2] // narrow))
        blocks += [part[:, :, i * narrow : (i + 1) * narrow] for i in range(counts[-1][1])]
    joint = jnp.concatenate(blocks, axis=1) if len(blocks) > 1 else blocks[0]
    joint = joint.reshape(-1, narrow)
    total = lax.psum_scatter(joint, "seq", scatter_dimension=0, tiled=True).astype(F32)
    results, start = [], 0
    for height, count in counts:
        parts = [total[start + i * height : start + (i + 1) * height] for i in range(count)]
        results.append(jnp.concatenate(parts, axis=1) if count > 1 else parts[0])
        start += height * count
    return results


def norm_stats(hidden):
    centred = hidden - jnp.mean(hidden, axis=-1, keepdims=True)
    rate = lax.rsqrt(jnp.mean(centred * centred, axis=-1, keepdims=True) + eps_norm)
    return centred * rate, rate


def norm_back(grad, normal, rate, scale_term):
    inner = grad * (1.0 + scale_term)
    return rate * (
        inner
        - jnp.mean(inner, axis=-1, keepdims=True)
        - normal * jnp.mean(inner * normal, axis=-1, keepdims=True)
    )


def time_features(times, feature_count):
    half = feature_count // 2
    steps = jnp.exp(jnp.arange(half, dtype=F32) * (-math.log(10000.0) / (half - 1)))
    angles = 1000.0 * times[:, None] * steps
    return jnp.concatenate([jnp.sin(angles), jnp.cos(angles)], axis=-1).astype(BF)


def params():
    return pltpu.CompilerParams(vmem_limit_bytes=VMEM_BYTES)


def cost(flops, moved, hard=0):
    return pl.CostEstimate(flops=int(flops), bytes_accessed=int(moved), transcendentals=int(hard))


def turn(values):
    lanes = lax.broadcasted_iota(jnp.int32, values.shape, 1)
    low = lax.rem(lanes, HD) < HD // 2
    return jnp.where(low, pltpu.roll(values, PAIR - HD // 2, 1), pltpu.roll(values, HD // 2, 1))


def project_kernel(tiles, x_ref, w_ref, cos_ref, sin_ref, q_ref, kv_ref):
    raw = dot(x_ref[...], w_ref[...])
    step = pl.program_id(0)

    def rotated(o_ref, factor):
        for first in range(0, raw.shape[1], PAIR):
            part = raw[:, first : first + PAIR]
            turned = part * cos_ref[...] + turn(part) * sin_ref[...]
            o_ref[:, first : first + PAIR] = (turned * factor).astype(BF)

    @pl.when(step < tiles)
    def _():
        rotated(q_ref, HD ** (-0.5) * LOG2E)

    @pl.when((step >= tiles) & (step < 2 * tiles))
    def _():
        rotated(kv_ref, 1.0)

    @pl.when(step >= 2 * tiles)
    def _():
        kv_ref[...] = raw.astype(BF)


def project(normed, w_qkv, cos_table, sin_table):
    frames, width = normed.shape
    tile = 512
    tiles = width // tile
    return pl.pallas_call(
        functools.partial(project_kernel, tiles),
        grid=(3 * tiles,),
        in_specs=[
            pl.BlockSpec((frames, width), lambda i: (0, 0)),
            pl.BlockSpec((width, tile), lambda i: (0, i)),
            pl.BlockSpec((frames, PAIR), lambda i: (0, 0)),
            pl.BlockSpec((frames, PAIR), lambda i: (0, 0)),
        ],
        out_specs=[
            pl.BlockSpec((frames, tile), lambda i: (0, jnp.minimum(i, tiles - 1))),
            pl.BlockSpec((frames, tile), lambda i: (0, jnp.maximum(i - tiles, 0))),
        ],
        out_shape=[
            jax.ShapeDtypeStruct((frames, width), BF),
            jax.ShapeDtypeStruct((frames, 2 * width), BF),
        ],
        compiler_params=params(),
        cost_estimate=cost(6 * frames * width * width, 6 * width * width + 8 * frames * width),
    )(normed, w_qkv, cos_table, sin_table)


def only_head(values, which):
    lanes = lax.broadcasted_iota(jnp.int32, values.shape, 1)
    mine = (lanes >= which * HD) & (lanes < (which + 1) * HD)
    return jnp.where(mine, values, jnp.zeros_like(values))


def attend_kernel(span, q_ref, *refs):
    k_refs, v_refs = refs[:span], refs[span : 2 * span]
    mk_ref, mq_ref, o_ref, p_ref, l_ref, bias_ref = refs[2 * span :]
    frames = q_ref.shape[0]

    @pl.when(pl.program_id(0) == 0)
    def _():
        seg_q, place_q = mq_ref[0:1, :], mq_ref[1:2, :]
        for index in range(span):
            rows = slice(index * frames, (index + 1) * frames)
            seg_k, place_k, live_k = mk_ref[rows, 0:1], mk_ref[rows, 1:2], mk_ref[rows, 2:3]
            allowed = (seg_q == seg_k) & ((live_k == 1) | (place_q == place_k))
            bias_ref[rows, :] = jnp.where(allowed, 0.0, neg_fill)

    values_t = [v[...].T for v in v_refs]
    ones = jnp.ones((16, frames), BF)
    results, inverses = [], []
    for which in range(2):
        queries = only_head(q_ref[...], which)
        scores = [
            dot(k[...], queries, DIMS_LAST) + bias_ref[i * frames : (i + 1) * frames, :]
            for i, k in enumerate(k_refs)
        ]
        top = functools.reduce(jnp.maximum, [jnp.max(s, axis=0, keepdims=True) for s in scores])
        result = None
        for index, part in enumerate(scores):
            powered = jnp.exp2(part - top).astype(BF)
            p_ref[which, index * frames : (index + 1) * frames, :] = powered
            lanes = values_t[index][which * HD : (which + 1) * HD]
            part = dot(jnp.concatenate([lanes, ones], axis=0), powered)
            result = part if result is None else result + part
        inverse = 1.0 / result[HD : HD + 1]
        results.append(result[:HD] * inverse)
        inverses.append(inverse)
    o_ref[...] = jnp.concatenate(results, axis=0).T.astype(BF)
    l_ref[0] = jnp.concatenate(inverses + [jnp.zeros((6, frames), F32)], axis=0)


def columns(frames, start=0):
    return pl.BlockSpec((frames, PAIR), lambda i: (0, start + i))


def attend(queries, pairs_kv, meta_k, meta_q):
    span = len(pairs_kv)
    frames, width = queries.shape
    pairs = width // PAIR
    keys = span * frames
    return pl.pallas_call(
        functools.partial(attend_kernel, span),
        grid=(pairs,),
        in_specs=[columns(frames)]
        + [columns(frames)] * span
        + [columns(frames, pairs)] * span
        + [
            pl.BlockSpec((keys, PAIR), lambda i: (0, 0)),
            pl.BlockSpec((8, frames), lambda i: (0, 0)),
        ],
        out_specs=[
            columns(frames),
            pl.BlockSpec((2, keys, frames), lambda i: (i, 0, 0)),
            pl.BlockSpec((1, 8, frames), lambda i: (i, 0, 0)),
        ],
        out_shape=[
            jax.ShapeDtypeStruct((frames, width), BF),
            jax.ShapeDtypeStruct((2 * pairs, keys, frames), BF),
            jax.ShapeDtypeStruct((pairs, 8, frames), F32),
        ],
        scratch_shapes=[pltpu.VMEM((keys, frames), F32)],
        compiler_params=params(),
        cost_estimate=cost(
            16 * pairs * frames * keys * PAIR,
            4 * pairs * frames * keys,
            2 * pairs * frames * keys,
        ),
    )(queries, *pairs_kv, *pairs_kv, meta_k, meta_q)


def middle_kernel(*refs):
    fed_ref, mid_ref, gx_ref, cot_ref, scale_ref, w_ref, a_ref, l_ref = refs[:8]
    out_ref, gm_ref, gl_ref, gs_ref, gc_ref, o_ref, c_ref = refs[8:]
    frames = mid_ref.shape[0]
    out_ref[...] = (mid_ref[...] + fed_ref[...]).astype(BF)
    normal, rate = norm_stats(mid_ref[...])
    grad = gx_ref[...]
    grad_mid = cot_ref[...].astype(F32) + norm_back(grad, normal, rate, scale_ref[...])
    gm_ref[...] = grad_mid
    gl_ref[...] = grad_mid.astype(BF)
    gs_ref[...] = grad.astype(BF)
    gc_ref[...] = (grad * normal).astype(BF)
    grads = dot(w_ref[...], grad_mid.astype(BF), DIMS_LAST)
    for pair in range(l_ref.shape[0]):
        lanes = slice(pair * PAIR, (pair + 1) * PAIR)
        scaled, centres = [], []
        results = a_ref[:, lanes].T
        for which in range(2):
            rows = slice(pair * PAIR + which * HD, pair * PAIR + (which + 1) * HD)
            scaled.append(grads[rows] * l_ref[pair, which : which + 1, :])
            product = scaled[-1] * results[which * HD : (which + 1) * HD].astype(F32)
            centres.append(jnp.sum(product, axis=0, keepdims=True))
        o_ref[:, lanes] = jnp.concatenate(scaled, axis=0).astype(BF).T
        c_ref[pair] = jnp.concatenate(centres + [jnp.zeros((6, frames), F32)], axis=0)


def middle(fed, resid_mid, grad_normed, cot_rows, modulation, w_out, attended, inverses):
    frames, width = resid_mid.shape
    pairs = width // PAIR
    tile = 256
    rows = pl.BlockSpec((tile, width), lambda i: (i, 0))
    heads = pl.BlockSpec((pairs, 8, tile), lambda i: (0, 0, i))
    low = jax.ShapeDtypeStruct((frames, width), BF)
    return pl.pallas_call(
        middle_kernel,
        grid=(frames // tile,),
        in_specs=[
            rows,
            rows,
            rows,
            rows,
            pl.BlockSpec((tile, width), lambda i: (i, 2)),
            pl.BlockSpec((width, width), lambda i: (0, 0)),
            rows,
            heads,
        ],
        out_specs=[rows] * 6 + [heads],
        out_shape=[low, jax.ShapeDtypeStruct((frames, width), F32), low, low, low, low]
        + [jax.ShapeDtypeStruct((pairs, 8, frames), F32)],
        compiler_params=params(),
        cost_estimate=cost(2 * frames * width * width, 2 * width * width + 30 * frames * width),
    )(fed, resid_mid, grad_normed, cot_rows, modulation, w_out, attended, inverses)


def attend_back_kernel(span, q_ref, *refs):
    k_refs, v_refs = refs[:span], refs[span : 2 * span]
    p_ref, c_ref, g_ref, cos_ref, sin_ref = refs[2 * span : 2 * span + 5]
    dq_ref, dkv_refs, ds_ref = refs[2 * span + 5], refs[2 * span + 6 : -1], refs[-1]
    frames = q_ref.shape[0]

    def unturn(grad, index):
        rows = slice(index * frames, (index + 1) * frames)
        return grad * cos_ref[rows, :] - turn(grad) * sin_ref[rows, :]

    keys_t = [k[...].T for k in k_refs]
    dk, dv, dq = [None] * span, [None] * span, []
    for which in range(2):
        centre = c_ref[0, which : which + 1, :]
        grads = only_head(g_ref[...], which)
        queries = only_head(q_ref[...], which)
        result = None
        for index in range(span):
            rows = slice(index * frames, (index + 1) * frames)
            grad_probs = dot(v_refs[index][...], grads, DIMS_LAST)
            soft = p_ref[which, rows, :]
            ds_ref[rows, :] = (soft.astype(F32) * (grad_probs - centre)).astype(BF)
            part = dot(soft, grads)
            dv[index] = part if dv[index] is None else dv[index] + part
            part = dot(ds_ref[rows, :], queries)
            dk[index] = part if dk[index] is None else dk[index] + part
            part = dot(keys_t[index][which * HD : (which + 1) * HD], ds_ref[rows, :])
            result = part if result is None else result + part
        dq.append(result)
    dq = jnp.concatenate(dq, axis=0).T
    dq_ref[...] = unturn(dq * HD ** (-0.5), 0).astype(BF)
    for index in range(span):
        dkv_refs[index][0] = unturn(dk[index] * (1.0 / LOG2E), index).astype(BF)
        dkv_refs[index][1] = dv[index].astype(BF)


def attend_back(queries, pairs_kv, probs, centres, grads, cos_keys, sin_keys):
    span = len(pairs_kv)
    frames, width = queries.shape
    pairs = width // PAIR
    keys = span * frames
    results = pl.pallas_call(
        functools.partial(attend_back_kernel, span),
        grid=(pairs,),
        in_specs=[columns(frames)]
        + [columns(frames)] * span
        + [columns(frames, pairs)] * span
        + [
            pl.BlockSpec((2, keys, frames), lambda i: (i, 0, 0)),
            pl.BlockSpec((1, 8, frames), lambda i: (i, 0, 0)),
            columns(frames),
            pl.BlockSpec((keys, PAIR), lambda i: (0, 0)),
            pl.BlockSpec((keys, PAIR), lambda i: (0, 0)),
        ],
        out_specs=[columns(frames)]
        + [pl.BlockSpec((2, frames, PAIR), lambda i: (0, 0, i))] * span,
        out_shape=[jax.ShapeDtypeStruct((frames, width), BF)]
        + [jax.ShapeDtypeStruct((2, frames, width), BF)] * span,
        scratch_shapes=[pltpu.VMEM((keys, frames), BF)],
        compiler_params=params(),
        cost_estimate=cost(32 * pairs * frames * keys * PAIR, 4 * pairs * frames * keys),
    )(queries, *pairs_kv, *pairs_kv, probs, centres, grads, cos_keys, sin_keys)
    return results[0], results[1:]


def split_rows(source, target, groups, low_bit):
    chunk = source.shape[0] // groups
    half = source.shape[0] // 2
    for index in range(groups // 2):
        for part, bit in ((0, 1 - low_bit), (1, low_bit)):
            first = pl.multiple_of((2 * index + bit) * chunk, chunk)
            start = part * half + index * chunk
            target[start : start + chunk, :] = source[pl.ds(first, chunk), :]


def feed_kernel(groups, started, x_ref, g_ref, up_ref, down_ref, *refs):
    if started:
        before_acc, before_gx, *refs = refs
    acc_ref, gx_ref, da_ref, dk_ref, ua_ref, uk_ref, t_ref, xt_ref = refs
    step = pl.program_id(0)
    low_bit = lax.axis_index("head") % 2

    @pl.when(step == 0)
    def _():
        t_ref[...] = x_ref[...].T
        split_rows(t_ref, xt_ref, groups, low_bit)
        acc_ref[...] = before_acc[...] if started else jnp.zeros_like(acc_ref)
        gx_ref[...] = before_gx[...] if started else jnp.zeros_like(gx_ref)

    up = dot(x_ref[...], up_ref[...])
    grad_hidden = dot(g_ref[...], down_ref[...], DIMS_LAST)
    root = math.sqrt(2.0 / math.pi)
    square = up * up
    bent = jnp.tanh(root * up * (1.0 + 0.044715 * square))
    half = 0.5 + 0.5 * bent
    slope = half + 0.5 * up * (1.0 - bent * bent) * (root * (1.0 + 3 * 0.044715 * square))
    hidden = (up * half).astype(BF)
    grad_up = (grad_hidden * slope).astype(BF)
    acc_ref[...] += dot(hidden, down_ref[...])
    gx_ref[...] += dot(grad_up, up_ref[...], DIMS_LAST)
    rows = dot(hidden, g_ref[...], DIMS_FIRST).astype(BF)

    @pl.when(step % 2 == low_bit)
    def _():
        dk_ref[...] = rows

    @pl.when(step % 2 != low_bit)
    def _():
        da_ref[...] = rows

    depth = x_ref.shape[1] // 2
    ua_ref[...] = dot(xt_ref[:depth, :], grad_up).astype(BF)
    uk_ref[...] = dot(xt_ref[depth:, :], grad_up).astype(BF)


def feed(normed, grads, w_up, w_down, first, count, *sums):
    groups = lax.axis_size("head")
    frames, width = normed.shape
    tile = w_up.shape[1] // groups
    inner = count * tile
    whole = pl.BlockSpec((frames, width), lambda i: (0, 0))
    rows = pl.BlockSpec((tile, width), lambda i: (i // 2, 0))
    cols = pl.BlockSpec((width // 2, tile), lambda i: (0, i))
    total = jax.ShapeDtypeStruct((frames, width), F32)
    down = jax.ShapeDtypeStruct((inner // 2, width), BF)
    up = jax.ShapeDtypeStruct((width // 2, inner), BF)
    return pl.pallas_call(
        functools.partial(feed_kernel, groups, bool(sums)),
        grid=(count,),
        in_specs=[
            whole,
            whole,
            pl.BlockSpec((width, tile), lambda i: (0, first + i)),
            pl.BlockSpec((tile, width), lambda i: (first + i, 0)),
        ]
        + [whole] * len(sums),
        out_specs=[whole, whole, rows, rows, cols, cols],
        out_shape=[total, total, down, down, up, up],
        scratch_shapes=[pltpu.VMEM((width, frames), BF), pltpu.VMEM((width, frames), BF)],
        compiler_params=params(),
        cost_estimate=cost(12 * frames * width * inner, 8 * width * inner, frames * inner),
    )(normed, grads, w_up, w_down, *sums)


def near_kernel(groups, span, *refs):
    dq_ref, dkv_refs, refs = refs[0], refs[1 : span + 1], refs[span + 1 :]
    w_ref, x_ref, a_ref, gl_ref, r_ref, scale_ref, gm_ref = refs[:7]
    away_ref, keep_ref, gi_ref, gs_ref, gc_ref = refs[7:12]
    t_ref, xt_ref, at_ref, acc_ref = refs[12:]
    step = pl.program_id(0)
    tiles = x_ref.shape[1] // dq_ref.shape[1]
    low_bit = lax.axis_index("head") % 2
    half = x_ref.shape[1] // 2

    @pl.when(step == 0)
    def _():
        for source, target in ((x_ref, xt_ref), (a_ref, at_ref)):
            t_ref[...] = source[...].T
            split_rows(t_ref, target, groups, low_bit)

    def one(left_ref, grads):
        away_ref[...] = dot(left_ref[:half, :], grads).astype(BF)
        keep_ref[...] = dot(left_ref[half:, :], grads).astype(BF)

    def projected(grads, first):
        one(xt_ref, grads)
        part = dot(grads, w_ref[...], DIMS_LAST)
        acc_ref[...] = part if first else acc_ref[...] + part

    @pl.when(step == 0)
    def _():
        projected(dq_ref[...], True)

    @pl.when((step > 0) & (step < tiles))
    def _():
        projected(dq_ref[...], False)

    @pl.when((step >= tiles) & (step < 3 * tiles))
    def _():
        grads = functools.reduce(jnp.add, [ref[0].astype(F32) for ref in dkv_refs])
        projected(grads.astype(BF), False)

    @pl.when(step >= 3 * tiles)
    def _():
        one(at_ref, gl_ref[...])

    @pl.when(step == 4 * tiles - 1)
    def _():
        normal, rate = norm_stats(r_ref[...].astype(F32))
        grad = acc_ref[...]
        gi_ref[...] = (gm_ref[...] + norm_back(grad, normal, rate, scale_ref[...])).astype(BF)
        gs_ref[...] = grad.astype(BF)
        gc_ref[...] = (grad * normal).astype(BF)


def near(dq, dkv, w_qkv, normed, attended, grad_low, resid_in, modulation, grad_mid):
    groups = lax.axis_size("head")
    frames, width = dq.shape
    tile = 512
    tiles = width // tile
    whole = pl.BlockSpec((frames, width), lambda i: (0, 0))

    def pair(i):
        index = jnp.clip(i - tiles, 0, 2 * tiles - 1)
        return (index // tiles, 0, index % tiles)

    grads = pl.BlockSpec((width // 2, tile), lambda i: (0, i))
    out = jax.ShapeDtypeStruct((width // 2, 4 * width), BF)
    low = jax.ShapeDtypeStruct((frames, width), BF)
    return pl.pallas_call(
        functools.partial(near_kernel, groups, len(dkv)),
        grid=(4 * tiles,),
        in_specs=[pl.BlockSpec((frames, tile), lambda i: (0, jnp.minimum(i, tiles - 1)))]
        + [pl.BlockSpec((1, frames, tile), pair)] * len(dkv)
        + [
            pl.BlockSpec((width, tile), lambda i: (0, jnp.minimum(i, 3 * tiles - 1))),
            whole,
            whole,
            pl.BlockSpec((frames, tile), lambda i: (0, jnp.maximum(i - 3 * tiles, 0))),
            whole,
            whole,
            whole,
        ],
        out_specs=[grads, grads, whole, whole, whole],
        out_shape=[out, out, low, low, low],
        scratch_shapes=[pltpu.VMEM((width, frames), BF)] * 3 + [pltpu.VMEM((frames, width), F32)],
        compiler_params=params(),
        cost_estimate=cost(14 * frames * width * width, 14 * width * width + 30 * frames * width),
    )(dq, *dkv, w_qkv, normed, attended, grad_low, resid_in, modulation, grad_mid)


def far_kernel(groups, count, *refs):
    pieces, refs = refs[:count], refs[count:]
    f_ref, gi_ref, m_refs = refs[0], refs[1], refs[2:6]
    sa_ref, sk_ref, ta_ref, tk_ref, t_ref, st_ref, u_ref, ft_ref = refs[6:]
    low_bit = lax.axis_index("head") % 2
    rows, width = pieces[0].shape[1], pieces[0].shape[2]

    @pl.when(pl.program_id(0) == 0)
    def _():
        for index, piece in enumerate(pieces):
            here = slice(index * rows, (index + 1) * rows)
            t_ref[:width, here] = piece[0].T
            t_ref[width:, here] = piece[1].T
        split_rows(t_ref, st_ref, groups, low_bit)
        u_ref[...] = f_ref[...].T
        split_rows(u_ref, ft_ref, groups, low_bit)

    half, few = width, u_ref.shape[0] // 2
    sa_ref[...] = dot(st_ref[:half, :], gi_ref[...]).astype(BF)
    sk_ref[...] = dot(st_ref[half:, :], gi_ref[...]).astype(BF)
    for index, m_ref in enumerate(m_refs):
        ta_ref[index] = dot(ft_ref[:few, :], m_ref[...]).astype(BF)
        tk_ref[index] = dot(ft_ref[few:, :], m_ref[...]).astype(BF)


def far(pieces, features, grad_in, grad_mods):
    groups = lax.axis_size("head")
    frames, width = grad_in.shape
    few = features.shape[1]
    tile = 512
    cols = pl.BlockSpec((frames, tile), lambda i: (0, i))
    big = pl.BlockSpec((width, tile), lambda i: (0, i))
    small = pl.BlockSpec((4, few // 2, tile), lambda i: (0, 0, i))
    return pl.pallas_call(
        functools.partial(far_kernel, groups, len(pieces)),
        grid=(width // tile,),
        in_specs=[pl.BlockSpec(piece.shape, lambda i: (0, 0, 0)) for piece in pieces]
        + [pl.BlockSpec((frames, few), lambda i: (0, 0))]
        + [cols] * 5,
        out_specs=[big, big, small, small],
        out_shape=[jax.ShapeDtypeStruct((width, width), BF)] * 2
        + [jax.ShapeDtypeStruct((4, few // 2, width), BF)] * 2,
        scratch_shapes=[pltpu.VMEM((2 * width, frames), BF)] * 2
        + [pltpu.VMEM((few, frames), BF)] * 2,
        compiler_params=params(),
        cost_estimate=cost(6 * frames * width * width, 6 * width * width + 20 * frames * width),
    )(*pieces, features, grad_in, *grad_mods)


def per_device(
    inputs,
    skips,
    flow_time,
    segment_ids,
    frame_mask,
    cotangent,
    w_skip,
    w_time,
    w_qkv,
    w_out,
    w_up,
    w_down,
):
    groups = lax.axis_size("head")
    micro_count, _, rows, width = inputs.shape
    span = groups // micro_count
    place = lax.axis_index("head")
    mine = place // span
    frames = micro_count * rows
    feature_count = w_time.shape[0]
    inputs, skips, cotangent = inputs[:, 0], skips[:, 0], cotangent[:, 0]

    resid_own = dot(inputs.reshape(frames, width), w_skip[:width]) + dot(
        skips.reshape(frames, width), w_skip[width:]
    )
    own_mod = dot(time_features(flow_time.reshape(-1), feature_count), w_time[:, : 2 * width])
    normed_own = norm_stats(resid_own)[0] * (1.0 + own_mod[:, width:]) + own_mod[:, :width]
    normed_own = cut_parts(normed_own.astype(BF).reshape(micro_count, rows, width), mine)

    meta = jnp.stack(
        [segment_ids[:, 0].astype(F32), frame_mask[:, 0].astype(F32), flow_time[:, 0]], axis=1
    )[None]
    for bit in range(groups.bit_length() - 1):
        meta = jnp.concatenate([meta, swap(meta, "head", 2**bit)])
    meta = pick(meta, mine, 1).reshape(micro_count, span, 3, rows)
    seg_keys, live_keys, times = [meta[:, :, i].swapaxes(0, 1).reshape(-1) for i in range(3)]
    order = jnp.stack(
        [place ^ other ^ (step * span) for other in range(span) for step in range(micro_count)]
    )
    place_keys = (order[:, None] * rows + jnp.arange(rows)[None, :]).reshape(-1).astype(F32)
    starts = jnp.sum((seg_keys[None, :] < seg_keys[:, None]).astype(F32), axis=1)
    positions = place_keys - starts
    inv_freq = jnp.exp(jnp.arange(HD // 2, dtype=F32) * (-2.0 * math.log(10000.0) / HD))
    turns = positions[:, None] * inv_freq
    cos_half, sin_half = jnp.cos(turns), jnp.sin(turns)
    cos_keys = jnp.concatenate([cos_half] * 4, axis=1)
    sin_keys = jnp.concatenate([-sin_half, sin_half] * 2, axis=1)
    meta_q = jnp.stack(
        [seg_keys[:frames], place_keys[:frames]] + [jnp.zeros((frames,), F32)] * 6
    )
    meta_k = jnp.stack([seg_keys, place_keys, live_keys], axis=1)
    meta_k = jnp.pad(meta_k, ((0, 0), (0, PAIR - 3)))
    features = time_features(times[:frames], feature_count)
    modulation = dot(features, w_time[:, width:])

    normed_attn = send_parts(normed_own, span)
    modulation, *normed_attn = together(modulation, *normed_attn)
    normed_attn = jnp.concatenate(normed_attn)
    second = jnp.stack(
        [cotangent, resid_own.astype(BF).reshape(micro_count, rows, width)], axis=1
    )
    second = cut_parts(second, mine)
    joined = cut_parts(jnp.stack([inputs, skips], axis=1), mine)
    normed_attn, *second = together(normed_attn, *second)
    second = send_parts(second, span)

    queries, keys_values = project(normed_attn, w_qkv, cos_keys[:frames], sin_keys[:frames])
    pairs_kv = [keys_values] + [swap(keys_values, "head", other) for other in range(1, span)]
    queries, *joined = together(queries, *joined)
    attended, probs, inverses = attend(queries, pairs_kv, meta_k, meta_q)
    attended, *second = together(attended, *second)
    cot_rows = jnp.concatenate([part[0] for part in second])
    resid_in = jnp.concatenate([part[1] for part in second])
    resid_mid = resid_in.astype(F32) + dot(attended, w_out)
    normal_second = norm_stats(resid_mid)[0]
    normed_ffn = (
        normal_second * (1.0 + modulation[:, 2 * width :]) + modulation[:, width : 2 * width]
    ).astype(BF)

    normed_ffn, *joined = together(normed_ffn, *joined)
    joined = send_parts(joined, span)
    half = groups // 2
    *sums, down_away, down_keep, up_away, up_keep = feed(
        normed_ffn, cot_rows, w_up, w_down, 0, half
    )
    down_away, up_away, normed_ffn, *rest = together(down_away, up_away, normed_ffn, *sums, *joined)
    sums, joined = rest[:2], rest[2:]
    down_came, up_came = swap(down_away, "head", 1), swap(up_away, "head", 1)
    *sums, down_away, down_keep_b, up_away_b, up_keep_b = feed(
        normed_ffn, cot_rows, w_up, w_down, half, half, *sums
    )
    *sums, down_came, up_came, down_away_b, up_away_b = together(
        *sums, down_came, up_came, down_away, up_away_b
    )
    seq_bits = lax.axis_size("seq").bit_length() - 1
    bits = list(range(seq_bits + 1, seq_bits + groups.bit_length() - 1))
    first, top = bits[0], bits[-1]
    down_a, up_a = Rows([down_keep, down_came], bits[:-1]), Rows([up_keep, up_came], bits)
    down_go, up_go, *sums = together(down_a.away(first), up_a.away(top), *sums)

    down_came, up_came = cross(down_go, first), cross(up_go, top)
    down_came_b, up_came_b = swap(down_away_b, "head", 1), swap(up_away_b, "head", 1)
    output, grad_mid, grad_mid_low, mod_shift, mod_scale, grads, centres = middle(
        sums[0], resid_mid, sums[1], cot_rows, modulation, w_out, attended, inverses
    )
    dq, dkv = attend_back(queries, pairs_kv, probs, centres, grads, cos_keys, sin_keys)
    dq, down_came, up_came, down_came_b, up_came_b, *dkv = together(
        dq, down_came, up_came, down_came_b, up_came_b, *dkv
    )
    down_a.join(down_came)
    up_a.join(up_came)
    down_b, up_b = Rows([down_keep_b, down_came_b], bits[:-1]), Rows([up_keep_b, up_came_b], bits)

    dkv[1:] = [swap(part, "head", other) for other, part in enumerate(dkv) if other > 0]
    dq, down_go, up_go = together(dq, down_b.away(first), up_b.away(top))
    down_came, up_came = cross(down_go, first), cross(up_go, top)
    near_away, near_keep, grad_in_low, first_shift, first_scale = near(
        dq, dkv, w_qkv, normed_attn, attended, grad_mid_low, resid_in, modulation, grad_mid
    )
    near_away, grad_in_low, down_came, up_came = together(
        near_away, grad_in_low, down_came, up_came
    )
    down_b.join(down_came)
    up_b.join(up_came)

    near_came = swap(near_away, "head", 1)
    for bit in bits[1:-1]:
        step_all([down_a, down_b], bit)
        step_all([up_a, up_b], bit)
    down_a, down_b = down_a.read(), down_b.read()
    upper = (place_of() >> top) % 2 == 1
    down_keep = jnp.where(upper, down_b, down_a)
    grad_in_low, down_go, up_go, up_go_b = together(
        grad_in_low, jnp.where(upper, down_a, down_b), up_a.away(first), up_b.away(first)
    )
    down_came = cross(down_go, top)
    up_came, up_came_b = cross(up_go, first), cross(up_go_b, first)
    skip_away, skip_keep, time_away, time_keep = far(
        joined, features, grad_in_low, [first_shift, first_scale, mod_shift, mod_scale]
    )
    skip_away, time_away, near_came, down_came, up_came, up_came_b = together(
        skip_away, time_away, near_came, down_came, up_came, up_came_b
    )
    up_a.join(up_came)
    up_b.join(up_came_b)

    skip_came, time_came = swap(skip_away, "head", 1), swap(time_away, "head", 1)
    middle_col = near_keep.shape[1] // 2
    wide = [[Rows([near_keep, near_came], bits, 1, (i * middle_col, middle_col))] for i in range(2)]

    def both_ways(pairs, index):
        return [(parts, order[index]) for parts, order in zip(pairs, (bits, bits[::-1]), strict=True)]

    def stage(steps, *values):
        sent = [cross(away_all(parts, bit), bit) for parts, bit in steps]
        *sent, values = together(*sent, values)
        for (parts, _), came in zip(steps, sent, strict=True):
            join_all(parts, came)
        return values

    total_down, total_up = last_sum(
        add_low([down_keep, down_came]), jnp.concatenate([up_a.read(), up_b.read()], axis=1)
    )
    skip_came, time_came = stage(both_ways(wide, 0), skip_came, time_came)
    narrow = [
        [
            Rows([skip_keep, skip_came], list(range(seq_bits)) + bits, 1, cols),
            Rows([time_keep, time_came], list(range(seq_bits)) + bits, 4, cols),
        ]
        for cols in ((0, width // 2), (width // 2, width // 2))
    ]
    for index in range(1, len(bits)):
        stage(both_ways(wide, index) + both_ways(narrow, index - 1))
    wide_sum = jnp.concatenate([wide[0][0].read(), wide[1][0].read()], axis=1)
    (near_sum,) = last_sum(wide_sum)
    wide_sum, output, grad_in_low = together(wide_sum, output, grad_in_low)
    output = from_buckets(output.reshape(micro_count, rows, width), span, mine)
    output, grad_in_low = stage(both_ways(narrow, len(bits) - 1), output, grad_in_low)
    grad_local = from_buckets(grad_in_low.reshape(micro_count, rows, width), span, mine)
    grad_local = grad_local.reshape(frames, width)
    total_qkv, total_out = near_sum[:, : 3 * width], near_sum[:, 3 * width :]
    for bit in range(seq_bits):
        for parts in narrow:
            step_all(parts, bit)
    total_skip = jnp.concatenate([parts[0].read() for parts in narrow], axis=1).astype(F32)
    total_time = jnp.concatenate([parts[1].read() for parts in narrow], axis=1).astype(F32)
    total_time = total_time.reshape(4, -1, width).swapaxes(0, 1).reshape(-1, 4 * width)
    shape = (micro_count, 1, rows, width)
    input_grad = dot(grad_local, w_skip[:width], DIMS_LAST).reshape(shape)
    skip_grad = dot(grad_local, w_skip[width:], DIMS_LAST).reshape(shape)
    return (
        output[:, None],
        input_grad,
        skip_grad,
        total_skip,
        total_time,
        total_qkv,
        total_out,
        total_up,
        total_down,
    )


def solution(mesh):
    frames_spec = P(None, "seq", "head", None)
    line_spec = P(None, "seq", "head")
    shard_spec = P(("head", "seq"), None)
    return jax.shard_map(
        per_device,
        mesh=mesh,
        in_specs=(frames_spec, frames_spec, line_spec, line_spec, line_spec, frames_spec)
        + (P(),) * 6,
        out_specs=(frames_spec,) * 3 + (shard_spec,) * 6,
        check_vma=False,
    )
```

```python
import functools
import math

import jax
import jax.numpy as jnp
from jax import lax
from jax.experimental import pallas as pl
from jax.experimental.pallas import tpu as pltpu
from jax.sharding import PartitionSpec as P

HD = 64
PAIR = 2 * HD
eps_norm = 1e-06
neg_fill = -1e30
BF = jnp.bfloat16
F32 = jnp.float32
DIMS_FIRST = (((0,), (0,)), ((), ()))
DIMS_LAST = (((1,), (1,)), ((), ()))
LOG2E = 1.4426950408889634


def dot(left, right, dims=(((1,), (0,)), ((), ()))):
    return lax.dot_general(left, right, dims, preferred_element_type=F32)


def swap(values, axis_name, bits):
    size = lax.axis_size(axis_name)
    return lax.ppermute(values, axis_name, [(i, i ^ bits) for i in range(size)])


def pick(values, index, axis):
    return lax.dynamic_index_in_dim(values, index, axis, keepdims=False)


def together(*values):
    return lax.optimization_barrier(values)


def cut_parts(values, mine):
    return [pick(values, mine ^ step, 0) for step in range(values.shape[0])]


def cut_pairs(left, right, mine):
    pairs = zip(cut_parts(left, mine), cut_parts(right, mine), strict=True)
    return [jnp.stack(pair) for pair in pairs]


def send_parts(parts, span):
    return parts[:1] + [
        swap(part, "head", step * span) for step, part in enumerate(parts) if step > 0
    ]


def by_micro(parts, mine):
    parts = jnp.stack(parts)
    return jnp.stack([pick(parts, mine ^ micro, 0) for micro in range(parts.shape[0])])


def add_low(terms):
    return functools.reduce(jnp.add, [term.astype(F32) for term in terms]).astype(BF)


class Rows:
    def __init__(self, arrays, bits, before=1, cols=None):
        self.order = sorted(bits, reverse=True)
        self.before, self.arrays = before, []
        self.start, self.size = cols or (0, arrays[0].shape[-1])
        self.chunk = arrays[0].size // arrays[0].shape[-1] // before // 2 ** len(bits)
        for array in arrays:
            self.join(array, self.start)

    def join(self, array, start=0):
        shape = [self.before] + [2] * len(self.order) + [self.chunk, array.shape[-1]]
        self.arrays.append((array.reshape(shape), tuple(self.order), {}, start))

    def read(self, bit=None, index=None):
        terms = []
        for array, bits, picks, start in self.arrays:
            picks = picks if bit is None else {**picks, bit: index}
            starts = [0] + [picks.get(b, 0) for b in bits] + [0, start]
            sizes = [self.before] + [1 if b in picks else 2 for b in bits] + [self.chunk, self.size]
            terms.append(lax.dynamic_slice(array, starts, sizes).reshape(-1, self.size))
        return add_low(terms)

    def away(self, bit):
        here = (place_of() >> bit) % 2
        sent = self.read(bit, 1 - here)
        self.order.remove(bit)
        for _, _, picks, _ in self.arrays:
            picks[bit] = here
        return sent


def place_of():
    return lax.axis_index("head") * lax.axis_size("seq") + lax.axis_index("seq")


def cross(rows, bit):
    seq_bits = lax.axis_size("seq").bit_length() - 1
    if bit < seq_bits:
        return swap(rows, "seq", 2**bit)
    return swap(rows, "head", 2 ** (bit - seq_bits))


def away_all(parts, bit):
    return jnp.concatenate([part.away(bit) for part in parts])


def join_all(parts, came):
    start = 0
    for part in parts:
        height = part.before * part.chunk * 2 ** len(part.order)
        part.join(came[start : start + height])
        start += height


def step_all(parts, bit):
    join_all(parts, cross(away_all(parts, bit), bit))


def seq_first(rows):
    size = lax.axis_size("seq")
    if seq_blocks(2 * rows.shape[0]) == 1:
        rows = rows.reshape(-1, size, rows.shape[0] * 2 // lax.axis_size("head") // size, rows.shape[1])
        rows = rows.swapaxes(0, 1).reshape(-1, rows.shape[-1])
    return lax.psum_scatter(rows, "seq", scatter_dimension=0, tiled=True)


def last_sum(*rows):
    size = lax.axis_size("seq")
    narrow = min(part.shape[1] for part in rows)
    blocks, counts = [], []
    for part in rows:
        part = part.reshape(size, -1, part.shape[1])
        counts.append((part.shape[1], part.shape[2] // narrow))
        blocks += [part[:, :, i * narrow : (i + 1) * narrow] for i in range(counts[-1][1])]
    joint = jnp.concatenate(blocks, axis=1) if len(blocks) > 1 else blocks[0]
    joint = joint.reshape(-1, narrow)
    total = lax.psum_scatter(joint, "seq", scatter_dimension=0, tiled=True)
    results, start = [], 0
    for height, count in counts:
        parts = [total[start + i * height : start + (i + 1) * height] for i in range(count)]
        results.append(jnp.concatenate(parts, axis=1) if count > 1 else parts[0])
        start += height * count
    return results


def norm_stats(hidden):
    centred = hidden - jnp.mean(hidden, axis=-1, keepdims=True)
    rate = lax.rsqrt(jnp.mean(centred * centred, axis=-1, keepdims=True) + eps_norm)
    return centred * rate, rate


def norm_back(grad, normal, rate, scale_term):
    inner = grad * (1.0 + scale_term)
    return rate * (
        inner
        - jnp.mean(inner, axis=-1, keepdims=True)
        - normal * jnp.mean(inner * normal, axis=-1, keepdims=True)
    )


def time_features(times, feature_count):
    half = feature_count // 2
    steps = jnp.exp(jnp.arange(half, dtype=F32) * (-math.log(10000.0) / (half - 1)))
    angles = 1000.0 * times[:, None] * steps
    return jnp.concatenate([jnp.sin(angles), jnp.cos(angles)], axis=-1).astype(BF)


def params(mebibytes):
    return pltpu.CompilerParams(vmem_limit_bytes=mebibytes * 1024 * 1024)


def once(shape, index_map=None):
    fixed = index_map or (lambda i: (0,) * len(shape))
    return pl.BlockSpec(shape, fixed, pipeline_mode=pl.Buffered(1))


def in_hbm(value):
    return pltpu.with_memory_space_constraint(value, pltpu.HBM)


def cost(flops, moved, hard=0):
    return pl.CostEstimate(flops=int(flops), bytes_accessed=int(moved), transcendentals=int(hard))


def turn(values):
    lanes = lax.broadcasted_iota(jnp.int32, values.shape, 1)
    low = lax.rem(lanes, HD) < HD // 2
    return jnp.where(low, pltpu.roll(values, PAIR - HD // 2, 1), pltpu.roll(values, HD // 2, 1))


def project_kernel(tiles, x_ref, w_ref, cos_ref, sin_ref, q_ref, kv_ref):
    raw = dot(x_ref[...], w_ref[...])
    step = pl.program_id(0)

    def rotated(o_ref, factor):
        for first in range(0, raw.shape[1], PAIR):
            part = raw[:, first : first + PAIR]
            turned = part * cos_ref[...] + turn(part) * sin_ref[...]
            o_ref[:, first : first + PAIR] = (turned * factor).astype(BF)

    @pl.when(step < tiles)
    def _():
        rotated(q_ref, HD ** (-0.5) * LOG2E)

    @pl.when((step >= tiles) & (step < 2 * tiles))
    def _():
        rotated(kv_ref, 1.0)

    @pl.when(step >= 2 * tiles)
    def _():
        kv_ref[...] = raw.astype(BF)


def project(normed, w_qkv, cos_table, sin_table):
    frames, width = normed.shape
    tile = 512
    tiles = width // tile
    return pl.pallas_call(
        functools.partial(project_kernel, tiles),
        grid=(3 * tiles,),
        in_specs=[
            once((frames, width)),
            pl.BlockSpec((width, tile), lambda i: (0, i)),
            once((frames, PAIR)),
            once((frames, PAIR)),
        ],
        out_specs=[
            pl.BlockSpec((frames, tile), lambda i: (0, jnp.minimum(i, tiles - 1))),
            pl.BlockSpec((frames, tile), lambda i: (0, jnp.maximum(i - tiles, 0))),
        ],
        out_shape=[
            jax.ShapeDtypeStruct((frames, width), BF),
            jax.ShapeDtypeStruct((frames, 2 * width), BF),
        ],
        compiler_params=params(52),
        cost_estimate=cost(6 * frames * width * width, 6 * width * width + 8 * frames * width),
    )(normed, w_qkv, cos_table, sin_table)


def only_head(values, which):
    lanes = lax.broadcasted_iota(jnp.int32, values.shape, 1)
    mine = (lanes >= which * HD) & (lanes < (which + 1) * HD)
    return jnp.where(mine, values, jnp.zeros_like(values))


def attend_kernel(span, q_ref, *refs):
    k_refs, v_refs = refs[:span], refs[span : 2 * span]
    mk_ref, mq_ref, o_ref, p_ref, l_ref, bias_ref = refs[2 * span :]
    frames = q_ref.shape[0]

    @pl.when(pl.program_id(0) == 0)
    def _():
        seg_q, place_q = mq_ref[0:1, :], mq_ref[1:2, :]
        for index in range(span):
            rows = slice(index * frames, (index + 1) * frames)
            seg_k, place_k, live_k = mk_ref[rows, 0:1], mk_ref[rows, 1:2], mk_ref[rows, 2:3]
            allowed = (seg_q == seg_k) & ((live_k == 1) | (place_q == place_k))
            bias_ref[rows, :] = jnp.where(allowed, 0.0, neg_fill)

    values_t = [v[...].T for v in v_refs]
    ones = jnp.ones((16, frames), BF)
    results, inverses = [], []
    for which in range(2):
        queries = only_head(q_ref[...], which)
        scores = [
            dot(k[...], queries, DIMS_LAST) + bias_ref[i * frames : (i + 1) * frames, :]
            for i, k in enumerate(k_refs)
        ]
        top = functools.reduce(jnp.maximum, [jnp.max(s, axis=0, keepdims=True) for s in scores])
        result = None
        for index, part in enumerate(scores):
            powered = jnp.exp2(part - top).astype(BF)
            p_ref[which, index * frames : (index + 1) * frames, :] = powered
            lanes = values_t[index][which * HD : (which + 1) * HD]
            part = dot(jnp.concatenate([lanes, ones], axis=0), powered)
            result = part if result is None else result + part
        inverse = 1.0 / result[HD : HD + 1]
        results.append(result[:HD] * inverse)
        inverses.append(inverse)
    o_ref[...] = jnp.concatenate(results, axis=0).T.astype(BF)
    l_ref[0] = jnp.concatenate(inverses + [jnp.zeros((6, frames), F32)], axis=0)


def columns(frames, start=0):
    return pl.BlockSpec((frames, PAIR), lambda i: (0, start + i))


def attend(queries, pairs_kv, meta_k, meta_q):
    span = len(pairs_kv)
    frames, width = queries.shape
    pairs = width // PAIR
    keys = span * frames
    return pl.pallas_call(
        functools.partial(attend_kernel, span),
        grid=(pairs,),
        in_specs=[columns(frames)]
        + [columns(frames)] * span
        + [columns(frames, pairs)] * span
        + [
            once((keys, PAIR)),
            once((8, frames)),
        ],
        out_specs=[
            columns(frames),
            pl.BlockSpec((2, keys, frames), lambda i: (i, 0, 0)),
            pl.BlockSpec((1, 8, frames), lambda i: (i, 0, 0)),
        ],
        out_shape=[
            jax.ShapeDtypeStruct((frames, width), BF),
            pltpu.HBM((2 * pairs, keys, frames), BF),
            jax.ShapeDtypeStruct((pairs, 8, frames), F32),
        ],
        scratch_shapes=[pltpu.VMEM((keys, frames), F32)],
        compiler_params=params(52),
        cost_estimate=cost(
            16 * pairs * frames * keys * PAIR,
            4 * pairs * frames * keys,
            2 * pairs * frames * keys,
        ),
    )(queries, *pairs_kv, *pairs_kv, meta_k, meta_q)


def attend_back_kernel(span, q_ref, *refs):
    k_refs, v_refs = refs[:span], refs[span : 2 * span]
    p_ref, c_ref, g_ref, cos_ref, sin_ref = refs[2 * span : 2 * span + 5]
    dq_ref, dkv_refs, ds_ref = refs[2 * span + 5], refs[2 * span + 6 : -1], refs[-1]
    frames = q_ref.shape[0]

    def unturn(grad, index):
        rows = slice(index * frames, (index + 1) * frames)
        return grad * cos_ref[rows, :] - turn(grad) * sin_ref[rows, :]

    keys_t = [k[...].T for k in k_refs]
    dk, dv, dq = [None] * span, [None] * span, []
    for which in range(2):
        centre = c_ref[0, which : which + 1, :]
        grads = only_head(g_ref[...], which)
        queries = only_head(q_ref[...], which)
        result = None
        for index in range(span):
            rows = slice(index * frames, (index + 1) * frames)
            grad_probs = dot(v_refs[index][...], grads, DIMS_LAST)
            soft = p_ref[which, rows, :]
            ds_ref[rows, :] = (soft.astype(F32) * (grad_probs - centre)).astype(BF)
            part = dot(soft, grads)
            dv[index] = part if dv[index] is None else dv[index] + part
            part = dot(ds_ref[rows, :], queries)
            dk[index] = part if dk[index] is None else dk[index] + part
            part = dot(keys_t[index][which * HD : (which + 1) * HD], ds_ref[rows, :])
            result = part if result is None else result + part
        dq.append(result)
    dq = jnp.concatenate(dq, axis=0).T
    dq_ref[...] = unturn(dq * HD ** (-0.5), 0).astype(BF)
    for index in range(span):
        dkv_refs[index][0] = unturn(dk[index] * (1.0 / LOG2E), index).astype(BF)
        dkv_refs[index][1] = dv[index].astype(BF)


def attend_back(queries, pairs_kv, probs, centres, grads, cos_keys, sin_keys):
    span = len(pairs_kv)
    frames, width = queries.shape
    pairs = width // PAIR
    keys = span * frames
    results = pl.pallas_call(
        functools.partial(attend_back_kernel, span),
        grid=(pairs,),
        in_specs=[columns(frames)]
        + [columns(frames)] * span
        + [columns(frames, pairs)] * span
        + [
            pl.BlockSpec((2, keys, frames), lambda i: (i, 0, 0)),
            pl.BlockSpec((1, 8, frames), lambda i: (i, 0, 0)),
            columns(frames),
            once((keys, PAIR)),
            once((keys, PAIR)),
        ],
        out_specs=[columns(frames)]
        + [pl.BlockSpec((2, frames, PAIR), lambda i: (0, 0, i))] * span,
        out_shape=[jax.ShapeDtypeStruct((frames, width), BF)]
        + [jax.ShapeDtypeStruct((2, frames, width), BF)] * span,
        scratch_shapes=[pltpu.VMEM((keys, frames), BF)],
        compiler_params=params(52),
        cost_estimate=cost(32 * pairs * frames * keys * PAIR, 4 * pairs * frames * keys),
    )(queries, *pairs_kv, *pairs_kv, in_hbm(probs), centres, grads, cos_keys, sin_keys)
    return results[0], results[1:]


def seq_blocks(rows):
    size = lax.axis_size("seq")
    return size if rows // lax.axis_size("head") // size % 16 == 0 else 1


def split_rows(source, target, groups, low_bit, blocks=1):
    chunk = source.shape[0] // groups // blocks
    half = source.shape[0] // 2
    for index in range(groups // 2):
        for part, bit in ((0, 1 - low_bit), (1, low_bit)):
            for block in range(blocks):
                first = pl.multiple_of(((2 * index + bit) * blocks + block) * chunk, chunk)
                start = part * half + (block * (groups // 2) + index) * chunk
                target[start : start + chunk, :] = source[pl.ds(first, chunk), :]


def fetches(pairs, sems):
    return [
        pltpu.make_async_copy(source, target, sems.at[index])
        for index, (source, target) in enumerate(pairs)
    ]


def feed_kernel(groups, blocks, x_ref, g_ref, up_ref, down_ref, l_ref, *refs):
    later, refs = refs[:4], refs[4:]
    da_ref, dk_ref, ua_ref, uk_ref = refs[:4]
    out_ref, gl_ref, gs_ref, gc_ref, o_ref, c_ref = refs[4:10]
    acc_ref, gx_ref, t_ref, xt_ref, mid_ref, scale_ref, w_ref, a_ref, sems = refs[10:]
    step = pl.program_id(0)
    low_bit = lax.axis_index("head") % 2
    copies = fetches(zip(later, (mid_ref, scale_ref, w_ref, a_ref), strict=True), sems)

    @pl.when(step == 0)
    def _():
        for copy in copies:
            copy.start()
        t_ref[...] = x_ref[...].T
        split_rows(t_ref, xt_ref, groups, low_bit, blocks)
        acc_ref[...] = jnp.zeros_like(acc_ref)
        gx_ref[...] = jnp.zeros_like(gx_ref)

    @pl.when(step < groups)
    def _():
        up = dot(x_ref[...], up_ref[...])
        grad_hidden = dot(g_ref[...], down_ref[...], DIMS_LAST)
        root = math.sqrt(2.0 / math.pi)
        square = up * up
        bent = jnp.tanh(root * up * (1.0 + 0.044715 * square))
        half = 0.5 + 0.5 * bent
        slope = half + 0.5 * up * (1.0 - bent * bent) * (root * (1.0 + 3 * 0.044715 * square))
        hidden = (up * half).astype(BF)
        grad_up = (grad_hidden * slope).astype(BF)
        acc_ref[...] += dot(hidden, down_ref[...])
        gx_ref[...] += dot(grad_up, up_ref[...], DIMS_LAST)
        rows = dot(hidden, g_ref[...], DIMS_FIRST).astype(BF)

        @pl.when(step % 2 == low_bit)
        def _():
            dk_ref[...] = rows

        @pl.when(step % 2 != low_bit)
        def _():
            da_ref[...] = rows

        depth = x_ref.shape[1] // 2
        ua_ref[...] = dot(xt_ref[:depth, :], grad_up).astype(BF)
        uk_ref[...] = dot(xt_ref[depth:, :], grad_up).astype(BF)

    @pl.when(step == groups)
    def _():
        for copy in copies:
            copy.wait()

    @pl.when(step >= groups)
    def _():
        few = out_ref.shape[0]
        here = pl.ds(pl.multiple_of((step - groups) * few, few), few)
        mid, grad = mid_ref[here, :], gx_ref[here, :]
        out_ref[...] = (mid + acc_ref[here, :]).astype(BF)
        normal, rate = norm_stats(mid)
        grad_mid = g_ref[here, :].astype(F32) + norm_back(grad, normal, rate, scale_ref[here, :])
        grad_low = grad_mid.astype(BF)
        gl_ref[...] = grad_low
        gs_ref[...] = grad.astype(BF)
        gc_ref[...] = (grad * normal).astype(BF)
        heads = dot(w_ref[...], grad_low, DIMS_LAST)
        for pair in range(l_ref.shape[0]):
            lanes = slice(pair * PAIR, (pair + 1) * PAIR)
            scaled, centres = [], []
            results = a_ref[here, lanes].T
            for which in range(2):
                rows = slice(pair * PAIR + which * HD, pair * PAIR + (which + 1) * HD)
                scaled.append(heads[rows] * l_ref[pair, which : which + 1, :])
                product = scaled[-1] * results[which * HD : (which + 1) * HD].astype(F32)
                centres.append(jnp.sum(product, axis=0, keepdims=True))
            o_ref[:, lanes] = jnp.concatenate(scaled, axis=0).astype(BF).T
            c_ref[pair] = jnp.concatenate(centres + [jnp.zeros((6, few), F32)], axis=0)


def feed(normed, cot_resid, w_up, w_down, resid_mid, scale, w_out, attended, inverses):
    groups = lax.axis_size("head")
    frames, width = normed.shape
    pairs = width // PAIR
    tile = w_up.shape[1] // groups
    inner = groups * tile
    few = 128
    whole = once((frames, width))
    last = groups - 1
    rows = pl.BlockSpec((tile, width), lambda i: (jnp.minimum(i, last) // 2, 0))
    cols = pl.BlockSpec((width // 2, tile), lambda i: (0, jnp.minimum(i, last)))
    part = pl.BlockSpec((few, width), lambda i: (jnp.maximum(i - groups, 0), 0))
    heads = pl.BlockSpec((pairs, 8, few), lambda i: (0, 0, jnp.maximum(i - groups, 0)))
    low = jax.ShapeDtypeStruct((frames, width), BF)
    anywhere = pl.BlockSpec(memory_space=pl.ANY)
    return pl.pallas_call(
        functools.partial(feed_kernel, groups, seq_blocks(width)),
        grid=(groups + frames // few,),
        in_specs=[
            whole,
            whole,
            pl.BlockSpec((width, tile), lambda i: (0, jnp.minimum(i, last))),
            pl.BlockSpec((tile, width), lambda i: (jnp.minimum(i, last), 0)),
            heads,
        ]
        + [anywhere] * 4,
        out_specs=[rows, rows, cols, cols] + [part] * 5 + [heads],
        out_shape=[
            jax.ShapeDtypeStruct((inner // 2, width), BF),
            pltpu.HBM((inner // 2, width), BF),
            jax.ShapeDtypeStruct((width // 2, inner), BF),
            pltpu.HBM((width // 2, inner), BF),
        ]
        + [low] * 5
        + [jax.ShapeDtypeStruct((pairs, 8, frames), F32)],
        scratch_shapes=[
            pltpu.VMEM((frames, width), F32),
            pltpu.VMEM((frames, width), F32),
            pltpu.VMEM((width, frames), BF),
            pltpu.VMEM((width, frames), BF),
            pltpu.VMEM((frames, width), F32),
            pltpu.VMEM((frames, width), F32),
            pltpu.VMEM((width, width), BF),
            pltpu.VMEM((frames, width), BF),
            pltpu.SemaphoreType.DMA((4,)),
        ],
        compiler_params=params(52),
        cost_estimate=cost(12 * frames * width * inner, 8 * width * inner, frames * inner),
    )(
        normed,
        cot_resid,
        in_hbm(w_up),
        in_hbm(w_down),
        inverses,
        resid_mid,
        scale,
        w_out,
        attended,
    )


def near_kernel(groups, span, *refs):
    dq_ref, dkv_refs, refs = refs[0], refs[1 : span + 1], refs[span + 1 :]
    w_ref, x_ref, gl_ref = refs[:3]
    attended, second, scale, grad_mid = refs[3:7]
    away_ref, keep_ref, gi_ref, gs_ref, gc_ref = refs[7:12]
    t_ref, xt_ref, acc_ref, a_ref, r_ref, scale_ref, gm_ref, sems = refs[12:]
    step = pl.program_id(0)
    tiles = x_ref.shape[1] // dq_ref.shape[1]
    low_bit = lax.axis_index("head") % 2
    width = x_ref.shape[1]
    half = width // 2
    first, *rest = fetches(
        [
            (attended, a_ref),
            (second.at[:, pl.ds(width, width)], r_ref),
            (scale, scale_ref),
            (grad_mid, gm_ref),
        ],
        sems,
    )

    @pl.when(step == 0)
    def _():
        for copy in (first, *rest):
            copy.start()
        t_ref[...] = x_ref[...].T
        split_rows(t_ref, xt_ref, groups, low_bit)

    @pl.when(step == 3 * tiles)
    def _():
        first.wait()
        t_ref[...] = a_ref[...].T
        split_rows(t_ref, xt_ref, groups, low_bit)

    def one(grads):
        away_ref[...] = dot(xt_ref[:half, :], grads).astype(BF)
        keep_ref[...] = dot(xt_ref[half:, :], grads).astype(BF)

    def projected(grads, start):
        one(grads)
        part = dot(grads, w_ref[...], DIMS_LAST)
        acc_ref[...] = part if start else acc_ref[...] + part

    @pl.when(step == 0)
    def _():
        projected(dq_ref[...], True)

    @pl.when((step > 0) & (step < tiles))
    def _():
        projected(dq_ref[...], False)

    @pl.when((step >= tiles) & (step < 3 * tiles))
    def _():
        grads = functools.reduce(jnp.add, [ref[0].astype(F32) for ref in dkv_refs])
        projected(grads.astype(BF), False)

    @pl.when((step >= 3 * tiles) & (step < 4 * tiles))
    def _():
        one(gl_ref[...])

    @pl.when(step == 4 * tiles)
    def _():
        for copy in rest:
            copy.wait()

    @pl.when(step >= 4 * tiles)
    def _():
        few = gi_ref.shape[0]
        here = pl.ds(pl.multiple_of((step - 4 * tiles) * few, few), few)
        normal, rate = norm_stats(r_ref[here, :].astype(F32))
        grad = acc_ref[here, :]
        grad_in = gm_ref[here, :].astype(F32) + norm_back(grad, normal, rate, scale_ref[here, :])
        gi_ref[...] = grad_in.astype(BF)
        gs_ref[...] = grad.astype(BF)
        gc_ref[...] = (grad * normal).astype(BF)


def near(dq, dkv, w_qkv, normed, attended, grad_low, cot_resid, scale):
    groups = lax.axis_size("head")
    frames, width = dq.shape
    tile = 512
    few = 128
    tiles = width // tile

    def pair(i):
        index = jnp.clip(i - tiles, 0, 2 * tiles - 1)
        return (index // tiles, 0, index % tiles)

    grads = pl.BlockSpec((width // 2, tile), lambda i: (0, jnp.minimum(i, 4 * tiles - 1)))
    part = pl.BlockSpec((few, width), lambda i: (jnp.maximum(i - 4 * tiles, 0), 0))
    out = pltpu.HBM((width // 2, 4 * width), BF)
    low = jax.ShapeDtypeStruct((frames, width), BF)
    return pl.pallas_call(
        functools.partial(near_kernel, groups, len(dkv)),
        grid=(4 * tiles + frames // few,),
        in_specs=[pl.BlockSpec((frames, tile), lambda i: (0, jnp.minimum(i, tiles - 1)))]
        + [pl.BlockSpec((1, frames, tile), pair)] * len(dkv)
        + [
            pl.BlockSpec((width, tile), lambda i: (0, jnp.minimum(i, 3 * tiles - 1))),
            once((frames, width)),
            pl.BlockSpec((frames, tile), lambda i: (0, jnp.clip(i - 3 * tiles, 0, tiles - 1))),
        ]
        + [pl.BlockSpec(memory_space=pl.ANY)] * 4,
        out_specs=[grads, grads, part, part, part],
        out_shape=[out, out, low, low, low],
        scratch_shapes=[
            pltpu.VMEM((width, frames), BF),
            pltpu.VMEM((width, frames), BF),
            pltpu.VMEM((frames, width), F32),
            pltpu.VMEM((frames, width), BF),
            pltpu.VMEM((frames, width), BF),
            pltpu.VMEM((frames, width), F32),
            pltpu.VMEM((frames, width), BF),
            pltpu.SemaphoreType.DMA((4,)),
        ],
        compiler_params=params(52),
        cost_estimate=cost(14 * frames * width * width, 14 * width * width + 30 * frames * width),
    )(dq, *dkv, w_qkv, normed, grad_low, attended, cot_resid, scale, grad_low)


def far_kernel(groups, count, *refs):
    pieces, refs = refs[:count], refs[count:]
    f_ref, gi_ref, m_refs = refs[0], refs[1], refs[2:6]
    away_ref, keep_ref, t_ref, st_ref, u_ref, ft_ref = refs[6:]
    low_bit = lax.axis_index("head") % 2
    rows, width = pieces[0].shape[1], pieces[0].shape[2]

    @pl.when(pl.program_id(0) == 0)
    def _():
        for index, piece in enumerate(pieces):
            here = slice(index * rows, (index + 1) * rows)
            t_ref[:width, here] = piece[0].T
            t_ref[width:, here] = piece[1].T
        split_rows(t_ref, st_ref, groups, low_bit)
        u_ref[...] = f_ref[...].T
        split_rows(u_ref, ft_ref, groups, low_bit)

    many, few = 2 * width // groups, u_ref.shape[0] // groups
    for part, out_ref in enumerate((away_ref, keep_ref)):
        big = dot(st_ref[part * width : (part + 1) * width, :], gi_ref[...]).astype(BF)
        half = u_ref.shape[0] // 2
        here = ft_ref[part * half : (part + 1) * half, :]
        small = [dot(here, m_ref[...]).astype(BF) for m_ref in m_refs]
        for index in range(groups // 2):
            start = index * (many + 4 * few)
            out_ref[start : start + many, :] = big[index * many : (index + 1) * many]
            for block in range(4):
                first = start + many + block * few
                out_ref[first : first + few, :] = small[block][index * few : (index + 1) * few]


def far(pieces, features, grad_in, grad_mods):
    groups = lax.axis_size("head")
    frames, width = grad_in.shape
    few = features.shape[1]
    tile = 512
    cols = pl.BlockSpec((frames, tile), lambda i: (0, i))
    out = pl.BlockSpec((width + 2 * few, tile), lambda i: (0, i))
    return pl.pallas_call(
        functools.partial(far_kernel, groups, len(pieces)),
        grid=(width // tile,),
        in_specs=[once(piece.shape) for piece in pieces] + [once((frames, few))] + [cols] * 5,
        out_specs=[out, out],
        out_shape=[pltpu.HBM((width + 2 * few, width), BF)] * 2,
        scratch_shapes=[pltpu.VMEM((2 * width, frames), BF)] * 2
        + [pltpu.VMEM((few, frames), BF)] * 2,
        compiler_params=params(52),
        cost_estimate=cost(6 * frames * width * width, 6 * width * width + 20 * frames * width),
    )(*pieces, features, grad_in, *grad_mods)


def per_device(
    inputs,
    skips,
    flow_time,
    segment_ids,
    frame_mask,
    cotangent,
    w_skip,
    w_time,
    w_qkv,
    w_out,
    w_up,
    w_down,
):
    groups = lax.axis_size("head")
    micro_count, _, rows, width = inputs.shape
    span = groups // micro_count
    place = lax.axis_index("head")
    mine = place // span
    frames = micro_count * rows
    feature_count = w_time.shape[0]
    inputs, skips, cotangent = inputs[:, 0], skips[:, 0], cotangent[:, 0]

    resid_own = dot(inputs.reshape(frames, width), w_skip[:width]) + dot(
        skips.reshape(frames, width), w_skip[width:]
    )
    own_mod = dot(time_features(flow_time.reshape(-1), feature_count), w_time[:, : 2 * width])
    normed_own = norm_stats(resid_own)[0] * (1.0 + own_mod[:, width:]) + own_mod[:, :width]
    normed_own = cut_parts(normed_own.astype(BF).reshape(micro_count, rows, width), mine)

    meta = jnp.stack(
        [segment_ids[:, 0].astype(F32), frame_mask[:, 0].astype(F32), flow_time[:, 0]], axis=1
    )[None]
    meta = jnp.concatenate([meta, swap(meta, "head", 1)])
    meta, *normed_own = together(meta, *normed_own)
    normed_attn = send_parts(normed_own, span)
    for bit in range(1, groups.bit_length() - 1):
        meta = jnp.concatenate([meta, swap(meta, "head", 2**bit)])
    resid_low = resid_own.astype(BF).reshape(micro_count, rows, width)
    second = [
        jnp.concatenate(pair, axis=1)
        for pair in zip(cut_parts(cotangent, mine), cut_parts(resid_low, mine), strict=True)
    ]
    meta, *rest = together(meta, *normed_attn, *second)
    normed_attn, second = jnp.concatenate(rest[:micro_count]), rest[micro_count:]
    meta = pick(meta, mine, 1).reshape(micro_count, span, 3, rows)
    seg_keys, live_keys, times = [meta[:, :, i].swapaxes(0, 1).reshape(-1) for i in range(3)]
    order = jnp.stack(
        [place ^ other ^ (step * span) for other in range(span) for step in range(micro_count)]
    )
    place_keys = (order[:, None] * rows + jnp.arange(rows)[None, :]).reshape(-1).astype(F32)
    starts = jnp.sum((seg_keys[None, :] < seg_keys[:, None]).astype(F32), axis=1)
    positions = place_keys - starts
    inv_freq = jnp.exp(jnp.arange(HD // 2, dtype=F32) * (-2.0 * math.log(10000.0) / HD))
    turns = positions[:, None] * inv_freq
    cos_half, sin_half = jnp.cos(turns), jnp.sin(turns)
    cos_keys = jnp.concatenate([cos_half] * 4, axis=1)
    sin_keys = jnp.concatenate([-sin_half, sin_half] * 2, axis=1)

    queries, keys_values = project(normed_attn, w_qkv, cos_keys[:frames], sin_keys[:frames])
    keys_values, seg_keys, live_keys, place_keys, times = together(
        keys_values, seg_keys, live_keys, place_keys, times
    )
    features = time_features(times[:frames], feature_count)
    scale_first, shift_second, scale_second = [
        dot(features, w_time[:, i * width : (i + 1) * width]) for i in range(1, 4)
    ]
    pairs_kv = [keys_values] + [swap(keys_values, "head", other) for other in range(1, span)]
    meta_q = jnp.stack(
        [seg_keys[:frames], place_keys[:frames]] + [jnp.zeros((frames,), F32)] * 6
    )
    meta_k = jnp.stack([seg_keys, place_keys, live_keys], axis=1)
    meta_k = jnp.pad(meta_k, ((0, 0), (0, PAIR - 3)))
    queries, meta_k, meta_q, scale_first, shift_second, scale_second, *pairs_kv = together(
        queries, meta_k, meta_q, scale_first, shift_second, scale_second, *pairs_kv
    )

    second = send_parts(second, span)
    attended, probs, inverses = attend(queries, pairs_kv, meta_k, meta_q)
    attended, inputs, skips = together(attended, inputs, skips)
    joined = cut_pairs(inputs, skips, mine)
    attended, *rest = together(attended, *second, *joined)
    second, joined = rest[:micro_count], rest[micro_count:]
    second = jnp.concatenate(second)
    resid_mid = second[:, width:].astype(F32) + dot(attended, w_out)
    normal_second = norm_stats(resid_mid)[0]
    normed_ffn = (normal_second * (1.0 + scale_second) + shift_second).astype(BF)

    normed_ffn, *joined = together(normed_ffn, *joined)
    joined = send_parts(joined, span)
    (
        down_away, down_keep, up_away, up_keep, output, grad_mid, mod_shift, mod_scale, grads, centres
    ) = feed(
        normed_ffn, second, w_up, w_down, resid_mid, scale_second, w_out, attended, inverses
    )
    grads, down_away, up_away, output, *joined = together(
        grads, down_away, up_away, output, *joined
    )
    seq_bits = lax.axis_size("seq").bit_length() - 1
    bits = list(range(seq_bits + 1, seq_bits + groups.bit_length() - 1))
    orders = (bits, bits[::-1])

    def two_ways(*arrays):
        middle_col = arrays[0].shape[1] // 2
        return [Rows(list(arrays), bits, 1, (i * middle_col, middle_col)) for i in range(2)]

    def begin(*pairs, index):
        return [
            away_all([pair[side] for pair in pairs], order[index])
            for side, order in enumerate(orders)
        ]

    def send(away, index):
        return [cross(rows, order[index]) for rows, order in zip(away, orders, strict=True)]

    def end(*pairs, came):
        for side, rows in enumerate(came):
            join_all([pair[side] for pair in pairs], rows)

    down_came, up_came = swap(down_away, "head", 1), swap(up_away, "head", 1)
    output = send_parts(list(output.reshape(micro_count, rows, width)), span)
    dq, dkv = attend_back(queries, pairs_kv, probs, centres, grads, cos_keys, sin_keys)
    dq, down_came, up_came, *rest = together(dq, down_came, up_came, *dkv, *output)
    dkv, output = rest[:span], rest[span:]

    dkv[1:] = [swap(part, "head", other) for other, part in enumerate(dkv) if other > 0]
    down = two_ways(down_keep, down_came)
    half = up_keep.shape[1] // 2
    up_0 = add_low([up_keep[:, :half], up_came[:, :half]])
    up_1 = add_low([up_keep[:, half:], up_came[:, half:]])
    dq, up_0, up_1, *rest = together(dq, up_0, up_1, *begin(down, index=0), *dkv)
    away, dkv = rest[:2], rest[2:]
    up_0 = seq_first(up_0)
    came = send(away, 0)
    near_away, near_keep, grad_in_low, first_shift, first_scale = near(
        dq, dkv, w_qkv, normed_attn, attended, grad_mid, second, scale_first
    )
    near_away, grad_in_low, *came = together(near_away, grad_in_low, *came)
    end(down, came=came)

    near_came = swap(near_away, "head", 1)
    for index in range(1, len(bits) - 1):
        end(down, came=send(begin(down, index=index), index))
    last_index = len(bits) - 1
    grad_in_low, *away = together(grad_in_low, *begin(down, index=last_index))
    came = send(away, last_index)
    far_away, far_keep = far(
        joined, features, grad_in_low, [first_shift, first_scale, mod_shift, mod_scale]
    )
    wide = two_ways(near_keep, near_came)
    far_away, up_0, *rest = together(far_away, up_0, *begin(wide, index=0), *came)
    wide_away, came = rest[:2], rest[2:]
    end(down, came=came)

    far_came = swap(far_away, "head", 1)
    wide_came = send(wide_away, 0)
    grad_local = send_parts(list(grad_in_low.reshape(micro_count, rows, width)), span)
    narrow = two_ways(far_keep, far_came)
    up_1 = seq_first(up_1)
    down_rows = jnp.concatenate([part.read() for part in down], axis=1)
    rest = together(*begin(narrow, index=0), up_1, *wide_came, down_rows, *grad_local)
    narrow_away, up_1, wide_came = rest[:2], rest[2], rest[3:5]
    down_rows, grad_local = rest[5], rest[6:]
    end(wide, came=wide_came)
    (down_sum,) = last_sum(down_rows)
    narrow_came = send(narrow_away, 0)
    for index in range(1, len(bits)):
        wide_came = send(begin(wide, index=index), index)
        if index < last_index:
            rest = together(*narrow_came, *wide_came)
            end(narrow, came=rest[:2])
            end(wide, came=rest[2:])
            narrow_came = send(begin(narrow, index=index), index)
    end(wide, came=wide_came)
    ups = [Rows([up_0], bits), Rows([up_1], bits)]
    wide_sum = jnp.concatenate([wide[0].read(), wide[1].read()], axis=1)
    wide_sum, down_sum, *rest = together(
        wide_sum, down_sum, *begin(ups, index=0), *narrow_came
    )
    up_away = rest[:2]
    end(narrow, came=rest[2:])
    narrow_came = send(begin(narrow, index=last_index), last_index)
    (near_sum,) = last_sum(wide_sum)
    end(narrow, came=together(*narrow_came))
    far_sum = jnp.concatenate([narrow[0].read(), narrow[1].read()], axis=1)
    many = w_skip.shape[0] // groups
    last = [
        Rows([far_sum[:many]], list(range(seq_bits))),
        Rows([far_sum[many:]], list(range(seq_bits)), 4),
    ]
    for index in range(max(seq_bits, len(bits))):
        came, up_came = [], []
        if index < seq_bits:
            came = [cross(away_all(last, index), index)]
        if index < len(bits):
            up_came = send(up_away, index)
        near_sum, *rest = together(near_sum, *came, *up_came)
        if index < seq_bits:
            join_all(last, rest[0])
        if index < len(bits):
            end(ups, came=rest[len(came) :])
        if index + 1 < len(bits):
            up_away = begin(ups, index=index + 1)
    output = by_micro(output, mine)
    grad_local = by_micro(grad_local, mine).reshape(frames, width)
    total_down, near_sum = down_sum.astype(F32), near_sum.astype(F32)
    total_up = jnp.concatenate([part.read() for part in ups], axis=1).astype(F32)
    total_qkv, total_out = near_sum[:, : 3 * width], near_sum[:, 3 * width :]
    total_skip = last[0].read().astype(F32)
    total_time = last[1].read().astype(F32)
    total_time = total_time.reshape(4, -1, width).swapaxes(0, 1).reshape(-1, 4 * width)
    shape = (micro_count, 1, rows, width)
    input_grad = dot(grad_local, w_skip[:width], DIMS_LAST).reshape(shape)
    skip_grad = dot(grad_local, w_skip[width:], DIMS_LAST).reshape(shape)
    return (
        output[:, None],
        input_grad,
        skip_grad,
        total_skip,
        total_time,
        total_qkv,
        total_out,
        total_up,
        total_down,
    )


def solution(mesh):
    frames_spec = P(None, "seq", "head", None)
    line_spec = P(None, "seq", "head")
    shard_spec = P(("head", "seq"), None)
    return jax.shard_map(
        per_device,
        mesh=mesh,
        in_specs=(frames_spec, frames_spec, line_spec, line_spec, line_spec, frames_spec)
        + (P(),) * 6,
        out_specs=(frames_spec,) * 3 + (shard_spec,) * 6,
        check_vma=False,
    )
```

```python
import functools
import math

import jax
import jax.numpy as jnp
from jax import lax
from jax.experimental import pallas as pl
from jax.experimental.pallas import tpu as pltpu
from jax.sharding import PartitionSpec as P

HD = 64
PAIR = 2 * HD
eps_norm = 1e-06
neg_fill = -1e30
SEGMENTS = 8
PADDING = 64
BF = jnp.bfloat16
F32 = jnp.float32
DIMS_FIRST = (((0,), (0,)), ((), ()))
DIMS_LAST = (((1,), (1,)), ((), ()))
LOG2E = 1.4426950408889634


def dot(left, right, dims=(((1,), (0,)), ((), ()))):
    return lax.dot_general(left, right, dims, preferred_element_type=F32)


def swap(values, axis_name, bits):
    size = lax.axis_size(axis_name)
    return lax.ppermute(values, axis_name, [(i, i ^ bits) for i in range(size)])


def pick(values, index, axis):
    return lax.dynamic_index_in_dim(values, index, axis, keepdims=False)


def together(*values):
    return lax.optimization_barrier(values)


def cut_parts(values, mine):
    return [pick(values, mine ^ step, 0) for step in range(values.shape[0])]


def cut_pairs(left, right, mine):
    pairs = zip(cut_parts(left, mine), cut_parts(right, mine), strict=True)
    return [jnp.stack(pair) for pair in pairs]


def send_parts(parts, span):
    return parts[:1] + [
        swap(part, "head", step * span) for step, part in enumerate(parts) if step > 0
    ]


def by_micro(parts, mine):
    parts = jnp.stack(parts)
    return jnp.stack([pick(parts, mine ^ micro, 0) for micro in range(parts.shape[0])])


def add_low(terms):
    return functools.reduce(jnp.add, [term.astype(F32) for term in terms]).astype(BF)


class Rows:
    def __init__(self, arrays, bits, before=1, cols=None):
        self.order = sorted(bits, reverse=True)
        self.before, self.arrays = before, []
        self.start, self.size = cols or (0, arrays[0].shape[-1])
        self.chunk = arrays[0].size // arrays[0].shape[-1] // before // 2 ** len(bits)
        for array in arrays:
            self.join(array, self.start)

    def join(self, array, start=0):
        shape = [self.before] + [2] * len(self.order) + [self.chunk, array.shape[-1]]
        self.arrays.append((array.reshape(shape), tuple(self.order), {}, start))

    def read(self, bit=None, index=None):
        terms = []
        for array, bits, picks, start in self.arrays:
            picks = picks if bit is None else {**picks, bit: index}
            starts = [0] + [picks.get(b, 0) for b in bits] + [0, start]
            sizes = [self.before] + [1 if b in picks else 2 for b in bits] + [self.chunk, self.size]
            terms.append(lax.dynamic_slice(array, starts, sizes).reshape(-1, self.size))
        return add_low(terms)

    def away(self, bit):
        here = (place_of() >> bit) % 2
        sent = self.read(bit, 1 - here)
        self.order.remove(bit)
        for _, _, picks, _ in self.arrays:
            picks[bit] = here
        return sent


def place_of():
    return lax.axis_index("head") * lax.axis_size("seq") + lax.axis_index("seq")


def cross(rows, bit):
    seq_bits = lax.axis_size("seq").bit_length() - 1
    if bit < seq_bits:
        return swap(rows, "seq", 2**bit)
    return swap(rows, "head", 2 ** (bit - seq_bits))


def away_all(parts, bit):
    return jnp.concatenate([part.away(bit) for part in parts])


def join_all(parts, came):
    start = 0
    for part in parts:
        height = part.before * part.chunk * 2 ** len(part.order)
        part.join(came[start : start + height])
        start += height


def step_all(parts, bit):
    join_all(parts, cross(away_all(parts, bit), bit))


def seq_first(rows):
    size = lax.axis_size("seq")
    if seq_blocks(2 * rows.shape[0]) == 1:
        rows = rows.reshape(-1, size, rows.shape[0] * 2 // lax.axis_size("head") // size, rows.shape[1])
        rows = rows.swapaxes(0, 1).reshape(-1, rows.shape[-1])
    return lax.psum_scatter(rows, "seq", scatter_dimension=0, tiled=True)


def last_sum(*rows):
    size = lax.axis_size("seq")
    narrow = min(part.shape[1] for part in rows)
    blocks, counts = [], []
    for part in rows:
        part = part.reshape(size, -1, part.shape[1])
        counts.append((part.shape[1], part.shape[2] // narrow))
        blocks += [part[:, :, i * narrow : (i + 1) * narrow] for i in range(counts[-1][1])]
    joint = jnp.concatenate(blocks, axis=1) if len(blocks) > 1 else blocks[0]
    joint = joint.reshape(-1, narrow)
    total = lax.psum_scatter(joint, "seq", scatter_dimension=0, tiled=True)
    results, start = [], 0
    for height, count in counts:
        parts = [total[start + i * height : start + (i + 1) * height] for i in range(count)]
        results.append(jnp.concatenate(parts, axis=1) if count > 1 else parts[0])
        start += height * count
    return results


def norm_stats(hidden):
    centred = hidden - jnp.mean(hidden, axis=-1, keepdims=True)
    rate = lax.rsqrt(jnp.mean(centred * centred, axis=-1, keepdims=True) + eps_norm)
    return centred * rate, rate


def norm_back(grad, normal, rate, scale_term):
    inner = grad * (1.0 + scale_term)
    return rate * (
        inner
        - jnp.mean(inner, axis=-1, keepdims=True)
        - normal * jnp.mean(inner * normal, axis=-1, keepdims=True)
    )


def time_features(times, feature_count):
    half = feature_count // 2
    steps = jnp.exp(jnp.arange(half, dtype=F32) * (-math.log(10000.0) / (half - 1)))
    angles = 1000.0 * times[:, None] * steps
    return jnp.concatenate([jnp.sin(angles), jnp.cos(angles)], axis=-1).astype(BF)


def params(mebibytes):
    return pltpu.CompilerParams(vmem_limit_bytes=mebibytes * 1024 * 1024)


def once(shape, index_map=None):
    fixed = index_map or (lambda i: (0,) * len(shape))
    return pl.BlockSpec(shape, fixed, pipeline_mode=pl.Buffered(1))


def in_hbm(value):
    return pltpu.with_memory_space_constraint(value, pltpu.HBM)


def cost(flops, moved, hard=0):
    return pl.CostEstimate(flops=int(flops), bytes_accessed=int(moved), transcendentals=int(hard))


def turn(values):
    lanes = lax.broadcasted_iota(jnp.int32, values.shape, 1)
    low = lax.rem(lanes, HD) < HD // 2
    return jnp.where(low, pltpu.roll(values, PAIR - HD // 2, 1), pltpu.roll(values, HD // 2, 1))


def project_kernel(tiles, x_ref, w_ref, cos_ref, sin_ref, q_ref, kv_ref):
    raw = dot(x_ref[...], w_ref[...])
    step = pl.program_id(0)

    def rotated(o_ref, factor):
        for first in range(0, raw.shape[1], PAIR):
            part = raw[:, first : first + PAIR]
            turned = part * cos_ref[...] + turn(part) * sin_ref[...]
            o_ref[:, first : first + PAIR] = (turned * factor).astype(BF)

    @pl.when(step < tiles)
    def _():
        rotated(q_ref, HD ** (-0.5) * LOG2E)

    @pl.when((step >= tiles) & (step < 2 * tiles))
    def _():
        rotated(kv_ref, 1.0)

    @pl.when(step >= 2 * tiles)
    def _():
        kv_ref[...] = raw.astype(BF)


def project(normed, w_qkv, cos_table, sin_table):
    frames, width = normed.shape
    tile = 512
    tiles = width // tile
    return pl.pallas_call(
        functools.partial(project_kernel, tiles),
        grid=(3 * tiles,),
        in_specs=[
            once((frames, width)),
            pl.BlockSpec((width, tile), lambda i: (0, i)),
            once((frames, PAIR)),
            once((frames, PAIR)),
        ],
        out_specs=[
            pl.BlockSpec((frames, tile), lambda i: (0, jnp.minimum(i, tiles - 1))),
            pl.BlockSpec((frames, tile), lambda i: (0, jnp.maximum(i - tiles, 0))),
        ],
        out_shape=[
            jax.ShapeDtypeStruct((frames, width), BF),
            jax.ShapeDtypeStruct((frames, 2 * width), BF),
        ],
        compiler_params=params(20),
        cost_estimate=cost(6 * frames * width * width, 6 * width * width + 8 * frames * width),
    )(normed, pltpu.with_memory_space_constraint(w_qkv, pltpu.VMEM), cos_table, sin_table)


def only_head(values, which):
    lanes = lax.broadcasted_iota(jnp.int32, values.shape, 1)
    mine = (lanes >= which * HD) & (lanes < (which + 1) * HD)
    return jnp.where(mine, values, jnp.zeros_like(values))


def attend_kernel(span, q_ref, *refs):
    k_refs, v_refs = refs[:span], refs[span : 2 * span]
    mk_ref, mq_ref, o_ref, p_ref, l_ref = refs[2 * span :]
    frames = q_ref.shape[0]
    values_t = [v[...].T for v in v_refs]
    ones = jnp.ones((16, frames), BF)
    keys = [
        jnp.concatenate([k[...], mk_ref[i * frames : (i + 1) * frames, :]], axis=1)
        for i, k in enumerate(k_refs)
    ]
    both = []
    for which in range(2):
        queries = jnp.concatenate([only_head(q_ref[...], which), mq_ref[...]], axis=1)
        both.append([dot(k, queries, DIMS_LAST) for k in keys])
    results, inverses = [], []
    for which, scores in enumerate(both):
        top = functools.reduce(jnp.maximum, [jnp.max(s, axis=0, keepdims=True) for s in scores])
        result = None
        for index, part in enumerate(scores):
            powered = jnp.exp2(part - top).astype(BF)
            p_ref[which, index * frames : (index + 1) * frames, :] = powered
            lanes = values_t[index][which * HD : (which + 1) * HD]
            part = dot(jnp.concatenate([lanes, ones], axis=0), powered)
            result = part if result is None else result + part
        inverse = 1.0 / result[HD : HD + 1]
        results.append(result[:HD] * inverse)
        inverses.append(inverse)
    o_ref[...] = jnp.concatenate(results, axis=0).T.astype(BF)
    l_ref[0] = jnp.concatenate(inverses + [jnp.zeros((6, frames), F32)], axis=0)


def mask_lanes(segments, live, places, bucket_len):
    lanes = jnp.arange(PAIR)[None, :]
    segment = (lanes < SEGMENTS) & (segments[:, None] == lanes)
    place = places[:, None] - (bucket_len - PADDING) == lanes - SEGMENTS
    place = place & (lanes >= SEGMENTS) & (lanes < SEGMENTS + PADDING)
    keys = (segment | (place & (live[:, None] == 0))).astype(BF)
    fill = (lanes < SEGMENTS + PADDING) & ~(segment | place)
    return keys, jnp.where(fill, neg_fill, 0.0).astype(BF)


def columns(frames, start=0):
    return pl.BlockSpec((frames, PAIR), lambda i: (0, start + i))


def attend(queries, pairs_kv, mask_keys, mask_queries):
    span = len(pairs_kv)
    frames, width = queries.shape
    pairs = width // PAIR
    keys = span * frames
    return pl.pallas_call(
        functools.partial(attend_kernel, span),
        grid=(pairs,),
        in_specs=[columns(frames)]
        + [columns(frames)] * span
        + [columns(frames, pairs)] * span
        + [
            once((keys, PAIR)),
            once((frames, PAIR)),
        ],
        out_specs=[
            columns(frames),
            pl.BlockSpec((2, keys, frames), lambda i: (i, 0, 0)),
            pl.BlockSpec((1, 8, frames), lambda i: (i, 0, 0)),
        ],
        out_shape=[
            jax.ShapeDtypeStruct((frames, width), BF),
            pltpu.HBM((2 * pairs, keys, frames), BF),
            jax.ShapeDtypeStruct((pairs, 8, frames), F32),
        ],
        compiler_params=params(28),
        cost_estimate=cost(
            16 * pairs * frames * keys * PAIR,
            4 * pairs * frames * keys,
            2 * pairs * frames * keys,
        ),
    )(queries, *pairs_kv, *pairs_kv, mask_keys, mask_queries)


def attend_back_kernel(span, q_ref, *refs):
    k_refs, v_refs = refs[:span], refs[span : 2 * span]
    p_ref, c_ref, g_ref, cos_ref, sin_ref = refs[2 * span : 2 * span + 5]
    dq_ref, dkv_refs, ds_ref = refs[2 * span + 5], refs[2 * span + 6 : -1], refs[-1]
    frames = q_ref.shape[0]

    def unturn(grad, index):
        rows = slice(index * frames, (index + 1) * frames)
        return grad * cos_ref[rows, :] - turn(grad) * sin_ref[rows, :]

    keys_t = [k[...].T for k in k_refs]
    dk, dv, dq = [None] * span, [None] * span, []
    for which in range(2):
        centre = c_ref[0, which : which + 1, :]
        grads = only_head(g_ref[...], which)
        queries = only_head(q_ref[...], which)
        result = None
        for index in range(span):
            rows = slice(index * frames, (index + 1) * frames)
            grad_probs = dot(v_refs[index][...], grads, DIMS_LAST)
            soft = p_ref[which, rows, :]
            ds_ref[rows, :] = (soft.astype(F32) * (grad_probs - centre)).astype(BF)
            part = dot(soft, grads)
            dv[index] = part if dv[index] is None else dv[index] + part
            part = dot(ds_ref[rows, :], queries)
            dk[index] = part if dk[index] is None else dk[index] + part
            part = dot(keys_t[index][which * HD : (which + 1) * HD], ds_ref[rows, :])
            result = part if result is None else result + part
        dq.append(result)
    dq = jnp.concatenate(dq, axis=0).T
    dq_ref[...] = unturn(dq * HD ** (-0.5), 0).astype(BF)
    for index in range(span):
        dkv_refs[index][0] = unturn(dk[index] * (1.0 / LOG2E), index).astype(BF)
        dkv_refs[index][1] = dv[index].astype(BF)


def attend_back(queries, pairs_kv, probs, centres, grads, cos_keys, sin_keys):
    span = len(pairs_kv)
    frames, width = queries.shape
    pairs = width // PAIR
    keys = span * frames
    results = pl.pallas_call(
        functools.partial(attend_back_kernel, span),
        grid=(pairs,),
        in_specs=[columns(frames)]
        + [columns(frames)] * span
        + [columns(frames, pairs)] * span
        + [
            pl.BlockSpec((2, keys, frames), lambda i: (i, 0, 0)),
            pl.BlockSpec((1, 8, frames), lambda i: (i, 0, 0)),
            columns(frames),
            once((keys, PAIR)),
            once((keys, PAIR)),
        ],
        out_specs=[columns(frames)]
        + [pl.BlockSpec((2, frames, PAIR), lambda i: (0, 0, i))] * span,
        out_shape=[jax.ShapeDtypeStruct((frames, width), BF)]
        + [jax.ShapeDtypeStruct((2, frames, width), BF)] * span,
        scratch_shapes=[pltpu.VMEM((keys, frames), BF)],
        compiler_params=params(52),
        cost_estimate=cost(32 * pairs * frames * keys * PAIR, 4 * pairs * frames * keys),
    )(queries, *pairs_kv, *pairs_kv, in_hbm(probs), centres, grads, cos_keys, sin_keys)
    return results[0], results[1:]


def seq_blocks(rows):
    size = lax.axis_size("seq")
    return size if rows // lax.axis_size("head") // size % 16 == 0 else 1


def split_rows(source, target, groups, low_bit, blocks=1):
    chunk = source.shape[0] // groups // blocks
    half = source.shape[0] // 2
    for index in range(groups // 2):
        for part, bit in ((0, 1 - low_bit), (1, low_bit)):
            for block in range(blocks):
                first = pl.multiple_of(((2 * index + bit) * blocks + block) * chunk, chunk)
                start = part * half + (block * (groups // 2) + index) * chunk
                target[start : start + chunk, :] = source[pl.ds(first, chunk), :]


def fetches(pairs, sems):
    return [
        pltpu.make_async_copy(source, target, sems.at[index])
        for index, (source, target) in enumerate(pairs)
    ]


def feed_kernel(groups, blocks, x_ref, g_ref, up_ref, down_ref, l_ref, *refs):
    later, refs = refs[:4], refs[4:]
    da_ref, dk_ref, ua_ref, uk_ref = refs[:4]
    out_ref, gl_ref, gs_ref, gc_ref, o_ref, c_ref = refs[4:10]
    acc_ref, gx_ref, t_ref, xt_ref, mid_ref, scale_ref, w_ref, a_ref, sems = refs[10:]
    step = pl.program_id(0)
    low_bit = lax.axis_index("head") % 2
    copies = fetches(zip(later, (mid_ref, scale_ref, w_ref, a_ref), strict=True), sems)

    @pl.when(step == 0)
    def _():
        for copy in copies:
            copy.start()
        t_ref[...] = x_ref[...].T
        split_rows(t_ref, xt_ref, groups, low_bit, blocks)
        acc_ref[...] = jnp.zeros_like(acc_ref)
        gx_ref[...] = jnp.zeros_like(gx_ref)

    @pl.when(step < groups)
    def _():
        up = dot(x_ref[...], up_ref[...])
        grad_hidden = dot(g_ref[...], down_ref[...], DIMS_LAST)
        root = math.sqrt(2.0 / math.pi)
        square = up * up
        bent = jnp.tanh(root * up * (1.0 + 0.044715 * square))
        half = 0.5 + 0.5 * bent
        slope = half + 0.5 * up * (1.0 - bent * bent) * (root * (1.0 + 3 * 0.044715 * square))
        hidden = (up * half).astype(BF)
        grad_up = (grad_hidden * slope).astype(BF)
        acc_ref[...] += dot(hidden, down_ref[...])
        gx_ref[...] += dot(grad_up, up_ref[...], DIMS_LAST)
        rows = dot(hidden, g_ref[...], DIMS_FIRST).astype(BF)

        @pl.when(step % 2 == low_bit)
        def _():
            dk_ref[...] = rows

        @pl.when(step % 2 != low_bit)
        def _():
            da_ref[...] = rows

        depth = x_ref.shape[1] // 2
        ua_ref[...] = dot(xt_ref[:depth, :], grad_up).astype(BF)
        uk_ref[...] = dot(xt_ref[depth:, :], grad_up).astype(BF)

    @pl.when(step == groups)
    def _():
        for copy in copies:
            copy.wait()

    @pl.when(step >= groups)
    def _():
        few = out_ref.shape[0]
        here = pl.ds(pl.multiple_of((step - groups) * few, few), few)
        mid, grad = mid_ref[here, :], gx_ref[here, :]
        out_ref[...] = (mid + acc_ref[here, :]).astype(BF)
        normal, rate = norm_stats(mid)
        grad_mid = g_ref[here, :].astype(F32) + norm_back(grad, normal, rate, scale_ref[here, :])
        grad_low = grad_mid.astype(BF)
        gl_ref[...] = grad_low
        gs_ref[...] = grad.astype(BF)
        gc_ref[...] = (grad * normal).astype(BF)
        heads = dot(w_ref[...], grad_low, DIMS_LAST)
        for pair in range(l_ref.shape[0]):
            lanes = slice(pair * PAIR, (pair + 1) * PAIR)
            scaled, centres = [], []
            results = a_ref[here, lanes].T
            for which in range(2):
                rows = slice(pair * PAIR + which * HD, pair * PAIR + (which + 1) * HD)
                scaled.append(heads[rows] * l_ref[pair, which : which + 1, :])
                product = scaled[-1] * results[which * HD : (which + 1) * HD].astype(F32)
                centres.append(jnp.sum(product, axis=0, keepdims=True))
            o_ref[:, lanes] = jnp.concatenate(scaled, axis=0).astype(BF).T
            c_ref[pair] = jnp.concatenate(centres + [jnp.zeros((6, few), F32)], axis=0)


def feed(normed, cot_resid, w_up, w_down, resid_mid, scale, w_out, attended, inverses):
    groups = lax.axis_size("head")
    frames, width = normed.shape
    pairs = width // PAIR
    tile = w_up.shape[1] // groups
    inner = groups * tile
    few = 128
    whole = once((frames, width))
    last = groups - 1
    rows = pl.BlockSpec((tile, width), lambda i: (jnp.minimum(i, last) // 2, 0))
    cols = pl.BlockSpec((width // 2, tile), lambda i: (0, jnp.minimum(i, last)))
    part = pl.BlockSpec((few, width), lambda i: (jnp.maximum(i - groups, 0), 0))
    heads = pl.BlockSpec((pairs, 8, few), lambda i: (0, 0, jnp.maximum(i - groups, 0)))
    low = jax.ShapeDtypeStruct((frames, width), BF)
    anywhere = pl.BlockSpec(memory_space=pl.ANY)
    return pl.pallas_call(
        functools.partial(feed_kernel, groups, seq_blocks(width)),
        grid=(groups + frames // few,),
        in_specs=[
            whole,
            whole,
            pl.BlockSpec((width, tile), lambda i: (0, jnp.minimum(i, last))),
            pl.BlockSpec((tile, width), lambda i: (jnp.minimum(i, last), 0)),
            heads,
        ]
        + [anywhere] * 4,
        out_specs=[rows, rows, cols, cols] + [part] * 5 + [heads],
        out_shape=[
            jax.ShapeDtypeStruct((inner // 2, width), BF),
            pltpu.HBM((inner // 2, width), BF),
            jax.ShapeDtypeStruct((width // 2, inner), BF),
            pltpu.HBM((width // 2, inner), BF),
        ]
        + [low] * 5
        + [jax.ShapeDtypeStruct((pairs, 8, frames), F32)],
        scratch_shapes=[
            pltpu.VMEM((frames, width), F32),
            pltpu.VMEM((frames, width), F32),
            pltpu.VMEM((width, frames), BF),
            pltpu.VMEM((width, frames), BF),
            pltpu.VMEM((frames, width), F32),
            pltpu.VMEM((frames, width), F32),
            pltpu.VMEM((width, width), BF),
            pltpu.VMEM((frames, width), BF),
            pltpu.SemaphoreType.DMA((4,)),
        ],
        compiler_params=params(52),
        cost_estimate=cost(12 * frames * width * inner, 8 * width * inner, frames * inner),
    )(
        normed,
        cot_resid,
        in_hbm(w_up),
        in_hbm(w_down),
        inverses,
        resid_mid,
        scale,
        w_out,
        attended,
    )


def near_kernel(groups, span, *refs):
    dq_ref, dkv_refs, refs = refs[0], refs[1 : span + 1], refs[span + 1 :]
    w_ref, x_ref, gl_ref = refs[:3]
    attended, second, scale, grad_mid = refs[3:7]
    away_ref, keep_ref, gi_ref, gs_ref, gc_ref = refs[7:12]
    t_ref, xt_ref, acc_ref, a_ref, r_ref, scale_ref, gm_ref, sems = refs[12:]
    step = pl.program_id(0)
    tiles = x_ref.shape[1] // dq_ref.shape[1]
    low_bit = lax.axis_index("head") % 2
    width = x_ref.shape[1]
    half = width // 2
    first, *rest = fetches(
        [
            (attended, a_ref),
            (second.at[:, pl.ds(width, width)], r_ref),
            (scale, scale_ref),
            (grad_mid, gm_ref),
        ],
        sems,
    )

    @pl.when(step == 0)
    def _():
        for copy in (first, *rest):
            copy.start()
        t_ref[...] = x_ref[...].T
        split_rows(t_ref, xt_ref, groups, low_bit)

    @pl.when(step == 3 * tiles)
    def _():
        first.wait()
        t_ref[...] = a_ref[...].T
        split_rows(t_ref, xt_ref, groups, low_bit)

    def one(grads):
        away_ref[...] = dot(xt_ref[:half, :], grads).astype(BF)
        keep_ref[...] = dot(xt_ref[half:, :], grads).astype(BF)

    def projected(grads, start):
        one(grads)
        part = dot(grads, w_ref[...], DIMS_LAST)
        acc_ref[...] = part if start else acc_ref[...] + part

    @pl.when(step == 0)
    def _():
        projected(dq_ref[...], True)

    @pl.when((step > 0) & (step < tiles))
    def _():
        projected(dq_ref[...], False)

    @pl.when((step >= tiles) & (step < 3 * tiles))
    def _():
        grads = functools.reduce(jnp.add, [ref[0].astype(F32) for ref in dkv_refs])
        projected(grads.astype(BF), False)

    @pl.when((step >= 3 * tiles) & (step < 4 * tiles))
    def _():
        one(gl_ref[...])

    @pl.when(step == 4 * tiles)
    def _():
        for copy in rest:
            copy.wait()

    @pl.when(step >= 4 * tiles)
    def _():
        few = gi_ref.shape[0]
        here = pl.ds(pl.multiple_of((step - 4 * tiles) * few, few), few)
        normal, rate = norm_stats(r_ref[here, :].astype(F32))
        grad = acc_ref[here, :]
        grad_in = gm_ref[here, :].astype(F32) + norm_back(grad, normal, rate, scale_ref[here, :])
        gi_ref[...] = grad_in.astype(BF)
        gs_ref[...] = grad.astype(BF)
        gc_ref[...] = (grad * normal).astype(BF)


def near(dq, dkv, w_qkv, normed, attended, grad_low, cot_resid, scale):
    groups = lax.axis_size("head")
    frames, width = dq.shape
    tile = 512
    few = 128
    tiles = width // tile

    def pair(i):
        index = jnp.clip(i - tiles, 0, 2 * tiles - 1)
        return (index // tiles, 0, index % tiles)

    grads = pl.BlockSpec((width // 2, tile), lambda i: (0, jnp.minimum(i, 4 * tiles - 1)))
    part = pl.BlockSpec((few, width), lambda i: (jnp.maximum(i - 4 * tiles, 0), 0))
    out = pltpu.HBM((width // 2, 4 * width), BF)
    low = jax.ShapeDtypeStruct((frames, width), BF)
    return pl.pallas_call(
        functools.partial(near_kernel, groups, len(dkv)),
        grid=(4 * tiles + frames // few,),
        in_specs=[pl.BlockSpec((frames, tile), lambda i: (0, jnp.minimum(i, tiles - 1)))]
        + [pl.BlockSpec((1, frames, tile), pair)] * len(dkv)
        + [
            pl.BlockSpec((width, tile), lambda i: (0, jnp.minimum(i, 3 * tiles - 1))),
            once((frames, width)),
            pl.BlockSpec((frames, tile), lambda i: (0, jnp.clip(i - 3 * tiles, 0, tiles - 1))),
        ]
        + [pl.BlockSpec(memory_space=pl.ANY)] * 4,
        out_specs=[grads, grads, part, part, part],
        out_shape=[out, out, low, low, low],
        scratch_shapes=[
            pltpu.VMEM((width, frames), BF),
            pltpu.VMEM((width, frames), BF),
            pltpu.VMEM((frames, width), F32),
            pltpu.VMEM((frames, width), BF),
            pltpu.VMEM((frames, width), BF),
            pltpu.VMEM((frames, width), F32),
            pltpu.VMEM((frames, width), BF),
            pltpu.SemaphoreType.DMA((4,)),
        ],
        compiler_params=params(52),
        cost_estimate=cost(14 * frames * width * width, 14 * width * width + 30 * frames * width),
    )(dq, *dkv, w_qkv, normed, grad_low, attended, cot_resid, scale, grad_low)


def far_kernel(groups, x_ref, y_ref, f_ref, gi_ref, *refs):
    m_refs, (away_ref, keep_ref, t_ref, st_ref, u_ref, ft_ref) = refs[:4], refs[4:]
    low_bit = lax.axis_index("head") % 2
    width = x_ref.shape[1]

    @pl.when(pl.program_id(0) == 0)
    def _():
        t_ref[:width, :] = x_ref[...].T
        t_ref[width:, :] = y_ref[...].T
        split_rows(t_ref, st_ref, groups, low_bit)
        u_ref[...] = f_ref[...].T
        split_rows(u_ref, ft_ref, groups, low_bit)

    many, few = 2 * width // groups, u_ref.shape[0] // groups
    for part, out_ref in enumerate((away_ref, keep_ref)):
        big = dot(st_ref[part * width : (part + 1) * width, :], gi_ref[...]).astype(BF)
        half = u_ref.shape[0] // 2
        here = ft_ref[part * half : (part + 1) * half, :]
        small = [dot(here, m_ref[...]).astype(BF) for m_ref in m_refs]
        for index in range(groups // 2):
            start = index * (many + 4 * few)
            out_ref[start : start + many, :] = big[index * many : (index + 1) * many]
            for block in range(4):
                first = start + many + block * few
                out_ref[first : first + few, :] = small[block][index * few : (index + 1) * few]


def far(inputs, skips, features, grad_in, grad_mods):
    groups = lax.axis_size("head")
    frames, width = grad_in.shape
    few = features.shape[1]
    tile = 512
    cols = pl.BlockSpec((frames, tile), lambda i: (0, i))
    out = pl.BlockSpec((width + 2 * few, tile), lambda i: (0, i))
    return pl.pallas_call(
        functools.partial(far_kernel, groups),
        grid=(width // tile,),
        in_specs=[once((frames, width)), once((frames, width)), once((frames, few))] + [cols] * 5,
        out_specs=[out, out],
        out_shape=[pltpu.HBM((width + 2 * few, width), BF)] * 2,
        scratch_shapes=[pltpu.VMEM((2 * width, frames), BF)] * 2
        + [pltpu.VMEM((few, frames), BF)] * 2,
        compiler_params=params(52),
        cost_estimate=cost(6 * frames * width * width, 6 * width * width + 20 * frames * width),
    )(inputs, skips, features, grad_in, *grad_mods)


def per_device(
    inputs,
    skips,
    flow_time,
    segment_ids,
    frame_mask,
    cotangent,
    w_skip,
    w_time,
    w_qkv,
    w_out,
    w_up,
    w_down,
):
    groups = lax.axis_size("head")
    micro_count, _, rows, width = inputs.shape
    span = groups // micro_count
    place = lax.axis_index("head")
    mine = place // span
    frames = micro_count * rows
    feature_count = w_time.shape[0]
    inputs, skips, cotangent = inputs[:, 0], skips[:, 0], cotangent[:, 0]

    resid_own = dot(inputs.reshape(frames, width), w_skip[:width]) + dot(
        skips.reshape(frames, width), w_skip[width:]
    )
    own_mod = dot(time_features(flow_time.reshape(-1), feature_count), w_time[:, : 2 * width])
    normed_own = norm_stats(resid_own)[0] * (1.0 + own_mod[:, width:]) + own_mod[:, :width]
    normed_own = cut_parts(normed_own.astype(BF).reshape(micro_count, rows, width), mine)

    meta = jnp.stack(
        [segment_ids[:, 0].astype(F32), frame_mask[:, 0].astype(F32), flow_time[:, 0]], axis=1
    )[None]
    meta = jnp.concatenate([meta, swap(meta, "head", 1)])
    meta, *normed_own = together(meta, *normed_own)
    normed_attn = send_parts(normed_own, span)
    for bit in range(1, groups.bit_length() - 1):
        meta = jnp.concatenate([meta, swap(meta, "head", 2**bit)])
    resid_low = resid_own.astype(BF).reshape(micro_count, rows, width)
    second = [
        jnp.concatenate(pair, axis=1)
        for pair in zip(cut_parts(cotangent, mine), cut_parts(resid_low, mine), strict=True)
    ]
    meta, *rest = together(meta, *normed_attn, *second)
    normed_attn, second = jnp.concatenate(rest[:micro_count]), rest[micro_count:]
    meta = pick(meta, mine, 1).reshape(micro_count, span, 3, rows)
    seg_keys, live_keys, times = [meta[:, :, i].swapaxes(0, 1).reshape(-1) for i in range(3)]
    order = jnp.stack(
        [place ^ other ^ (step * span) for other in range(span) for step in range(micro_count)]
    )
    place_keys = (order[:, None] * rows + jnp.arange(rows)[None, :]).reshape(-1).astype(F32)
    starts = jnp.sum((seg_keys[None, :] < seg_keys[:, None]).astype(F32), axis=1)
    positions = place_keys - starts
    inv_freq = jnp.exp(jnp.arange(HD // 2, dtype=F32) * (-2.0 * math.log(10000.0) / HD))
    turns = positions[:, None] * inv_freq
    cos_half, sin_half = jnp.cos(turns), jnp.sin(turns)
    cos_keys = jnp.concatenate([cos_half] * 4, axis=1)
    sin_keys = jnp.concatenate([-sin_half, sin_half] * 2, axis=1)

    queries, keys_values = project(normed_attn, w_qkv, cos_keys[:frames], sin_keys[:frames])
    keys_values, seg_keys, live_keys, place_keys, times = together(
        keys_values, seg_keys, live_keys, place_keys, times
    )
    pairs_kv = [keys_values] + [swap(keys_values, "head", other) for other in range(1, span)]
    mask_keys, mask_queries = mask_lanes(seg_keys, live_keys, place_keys, groups * rows)
    queries, mask_keys, mask_queries, *pairs_kv = together(
        queries, mask_keys, mask_queries[:frames], *pairs_kv
    )

    second = send_parts(second, span)
    attended, probs, inverses = attend(queries, pairs_kv, mask_keys, mask_queries)
    attended, times = together(attended, times)
    features = time_features(times[:frames], feature_count)
    scale_first, shift_second, scale_second = [
        dot(features, w_time[:, i * width : (i + 1) * width]) for i in range(1, 4)
    ]
    attended, scale_first, shift_second, scale_second, *second = together(
        attended, scale_first, shift_second, scale_second, *second
    )
    second = jnp.concatenate(second)
    resid_mid = second[:, width:].astype(F32) + dot(attended, w_out)
    normal_second = norm_stats(resid_mid)[0]
    normed_ffn = (normal_second * (1.0 + scale_second) + shift_second).astype(BF)

    (
        down_away, down_keep, up_away, up_keep, output, grad_mid, mod_shift, mod_scale, grads, centres
    ) = feed(
        normed_ffn, second, w_up, w_down, resid_mid, scale_second, w_out, attended, inverses
    )
    grads, down_away, up_away, output = together(grads, down_away, up_away, output)
    seq_bits = lax.axis_size("seq").bit_length() - 1
    bits = list(range(seq_bits + 1, seq_bits + groups.bit_length() - 1))
    orders = (bits, bits[::-1])

    def two_ways(*arrays):
        middle_col = arrays[0].shape[1] // 2
        return [Rows(list(arrays), bits, 1, (i * middle_col, middle_col)) for i in range(2)]

    def begin(*pairs, index):
        return [
            away_all([pair[side] for pair in pairs], order[index])
            for side, order in enumerate(orders)
        ]

    def send(away, index):
        return [cross(rows, order[index]) for rows, order in zip(away, orders, strict=True)]

    def end(*pairs, came):
        for side, rows in enumerate(came):
            join_all([pair[side] for pair in pairs], rows)

    down_came, up_came = swap(down_away, "head", 1), swap(up_away, "head", 1)
    output = send_parts(list(output.reshape(micro_count, rows, width)), span)
    dq, dkv = attend_back(queries, pairs_kv, probs, centres, grads, cos_keys, sin_keys)
    dq, down_came, up_came, *rest = together(dq, down_came, up_came, *dkv, *output)
    dkv, output = rest[:span], rest[span:]

    dkv[1:] = [swap(part, "head", other) for other, part in enumerate(dkv) if other > 0]
    down = two_ways(down_keep, down_came)
    half = up_keep.shape[1] // 2
    up_0 = add_low([up_keep[:, :half], up_came[:, :half]])
    up_1 = add_low([up_keep[:, half:], up_came[:, half:]])
    dq, up_0, up_1, down_came, *dkv = together(dq, up_0, up_1, down_came, *dkv)
    up_0 = seq_first(up_0)
    down = two_ways(down_keep, down_came)
    dq, *away = together(dq, *begin(down, index=0))
    came = send(away, 0)
    near_away, near_keep, grad_in_low, first_shift, first_scale = near(
        dq, dkv, w_qkv, normed_attn, attended, grad_mid, second, scale_first
    )
    near_away, grad_in_low, *came = together(near_away, grad_in_low, *came)
    end(down, came=came)

    near_came = swap(near_away, "head", 1)
    for index in range(1, len(bits) - 1):
        end(down, came=send(begin(down, index=index), index))
    last_index = len(bits) - 1
    grad_in_low, *away = together(grad_in_low, *begin(down, index=last_index))
    came = send(away, last_index)
    grad_local = send_parts(list(grad_in_low.reshape(micro_count, rows, width)), span)
    wide = two_ways(near_keep, near_came)
    up_0, *rest = together(up_0, *begin(wide, index=0), *came, *grad_local)
    wide_away, came, grad_local = rest[:2], rest[2:4], rest[4:]
    end(down, came=came)

    wide_came = send(wide_away, 0)
    grad_local = by_micro(grad_local, mine).reshape(frames, width)
    far_away, far_keep = far(
        inputs.reshape(frames, width),
        skips.reshape(frames, width),
        features,
        grad_local,
        [first_shift, first_scale, mod_shift, mod_scale],
    )
    up_1 = seq_first(up_1)
    down_rows = jnp.concatenate([part.read() for part in down], axis=1)
    far_away, down_rows, *wide_came = together(far_away, down_rows, *wide_came)
    end(wide, came=wide_came)

    far_came = swap(far_away, "head", 1)
    narrow = two_ways(far_keep, far_came)
    for index in range(1, len(bits)):
        wide_came = send(begin(wide, index=index), index)
        if index < last_index:
            end(wide, came=together(*wide_came))
    (down_sum,) = last_sum(down_rows)
    up_1, *rest = together(up_1, *begin(narrow, index=0), *wide_came)
    narrow_away, wide_came = rest[:2], rest[2:]
    end(wide, came=wide_came)

    narrow_came = send(narrow_away, 0)
    wide_sum = jnp.concatenate([wide[0].read(), wide[1].read()], axis=1)
    ups = [Rows([up_0], bits), Rows([up_1], bits)]
    rest = together(wide_sum, down_sum, *begin(ups, index=0), *narrow_came)
    wide_sum, down_sum, up_away = rest[0], rest[1], rest[2:4]
    end(narrow, came=rest[4:])

    (near_sum,) = last_sum(wide_sum)
    for index in range(1, len(bits)):
        end(narrow, came=together(*send(begin(narrow, index=index), index)))
    far_sum = jnp.concatenate([narrow[0].read(), narrow[1].read()], axis=1)
    many = w_skip.shape[0] // groups
    last = [
        Rows([far_sum[:many]], list(range(seq_bits))),
        Rows([far_sum[many:]], list(range(seq_bits)), 4),
    ]
    for index in range(max(seq_bits, len(bits))):
        came, up_came = [], []
        if index < seq_bits:
            came = [cross(away_all(last, index), index)]
        if index < len(bits):
            up_came = send(up_away, index)
        if index == 0:
            near_sum, *rest = together(near_sum, *came, *up_came)
            done = [
                by_micro(output, mine),
                near_sum[:, : 3 * width].astype(F32),
                near_sum[:, 3 * width :].astype(F32),
                down_sum.astype(F32),
            ]
        else:
            *done, rest = together(*done, [*came, *up_came])
        if index < seq_bits:
            join_all(last, rest[0])
        if index < len(bits):
            end(ups, came=rest[len(came) :])
        if index + 1 < len(bits):
            up_away = begin(ups, index=index + 1)
    output, total_qkv, total_out, total_down = done
    total_up = jnp.concatenate([part.read() for part in ups], axis=1).astype(F32)
    total_skip = last[0].read().astype(F32)
    total_time = last[1].read().astype(F32)
    total_time = total_time.reshape(4, -1, width).swapaxes(0, 1).reshape(-1, 4 * width)
    shape = (micro_count, 1, rows, width)
    input_grad = dot(grad_local, w_skip[:width], DIMS_LAST).reshape(shape)
    skip_grad = dot(grad_local, w_skip[width:], DIMS_LAST).reshape(shape)
    return (
        output[:, None],
        input_grad,
        skip_grad,
        total_skip,
        total_time,
        total_qkv,
        total_out,
        total_up,
        total_down,
    )


def solution(mesh):
    frames_spec = P(None, "seq", "head", None)
    line_spec = P(None, "seq", "head")
    shard_spec = P(("head", "seq"), None)
    return jax.shard_map(
        per_device,
        mesh=mesh,
        in_specs=(frames_spec, frames_spec, line_spec, line_spec, line_spec, frames_spec)
        + (P(),) * 6,
        out_specs=(frames_spec,) * 3 + (shard_spec,) * 6,
        check_vma=False,
    )
```

```python
import functools
import math

import jax
import jax.numpy as jnp
from jax import lax
from jax.experimental import pallas as pl
from jax.experimental.pallas import tpu as pltpu
from jax.sharding import PartitionSpec as P

HD = 64
PAIR = 2 * HD
eps_norm = 1e-06
neg_fill = -1e30
SEGMENTS = 8
PADDING = 64
BF = jnp.bfloat16
F32 = jnp.float32
DIMS_FIRST = (((0,), (0,)), ((), ()))
DIMS_LAST = (((1,), (1,)), ((), ()))
LOG2E = 1.4426950408889634


def dot(left, right, dims=(((1,), (0,)), ((), ()))):
    return lax.dot_general(left, right, dims, preferred_element_type=F32)


def swap(values, axis_name, bits):
    size = lax.axis_size(axis_name)
    return lax.ppermute(values, axis_name, [(i, i ^ bits) for i in range(size)])


def pick(values, index, axis):
    return lax.dynamic_index_in_dim(values, index, axis, keepdims=False)


def together(*values):
    return lax.optimization_barrier(values)


def cut_parts(values, mine):
    return [pick(values, mine ^ step, 0) for step in range(values.shape[0])]


def cut_pairs(left, right, mine):
    pairs = zip(cut_parts(left, mine), cut_parts(right, mine), strict=True)
    return [jnp.stack(pair) for pair in pairs]


def send_parts(parts, span):
    return parts[:1] + [
        swap(part, "head", step * span) for step, part in enumerate(parts) if step > 0
    ]


def by_micro(parts, mine):
    parts = jnp.stack(parts)
    return jnp.stack([pick(parts, mine ^ micro, 0) for micro in range(parts.shape[0])])


def add_low(terms):
    return functools.reduce(jnp.add, [term.astype(F32) for term in terms]).astype(BF)


class Rows:
    def __init__(self, arrays, bits, before=1, cols=None):
        self.order = sorted(bits, reverse=True)
        self.before, self.arrays = before, []
        self.start, self.size = cols or (0, arrays[0].shape[-1])
        self.chunk = arrays[0].size // arrays[0].shape[-1] // before // 2 ** len(bits)
        for array in arrays:
            self.join(array, self.start)

    def join(self, array, start=0):
        shape = [self.before] + [2] * len(self.order) + [self.chunk, array.shape[-1]]
        self.arrays.append((array.reshape(shape), tuple(self.order), {}, start))

    def read(self, bit=None, index=None):
        terms = []
        for array, bits, picks, start in self.arrays:
            picks = picks if bit is None else {**picks, bit: index}
            starts = [0] + [picks.get(b, 0) for b in bits] + [0, start]
            sizes = [self.before] + [1 if b in picks else 2 for b in bits] + [self.chunk, self.size]
            terms.append(lax.dynamic_slice(array, starts, sizes).reshape(-1, self.size))
        return add_low(terms)

    def away(self, bit):
        here = (place_of() >> bit) % 2
        sent = self.read(bit, 1 - here)
        self.order.remove(bit)
        for _, _, picks, _ in self.arrays:
            picks[bit] = here
        return sent


def place_of():
    return lax.axis_index("head") * lax.axis_size("seq") + lax.axis_index("seq")


def cross(rows, bit):
    seq_bits = lax.axis_size("seq").bit_length() - 1
    if bit < seq_bits:
        return swap(rows, "seq", 2**bit)
    return swap(rows, "head", 2 ** (bit - seq_bits))


def away_all(parts, bit):
    return jnp.concatenate([part.away(bit) for part in parts])


def join_all(parts, came):
    start = 0
    for part in parts:
        height = part.before * part.chunk * 2 ** len(part.order)
        part.join(came[start : start + height])
        start += height


def step_all(parts, bit):
    join_all(parts, cross(away_all(parts, bit), bit))


def seq_first(rows):
    size = lax.axis_size("seq")
    if seq_blocks(2 * rows.shape[0]) == 1:
        rows = rows.reshape(-1, size, rows.shape[0] * 2 // lax.axis_size("head") // size, rows.shape[1])
        rows = rows.swapaxes(0, 1).reshape(-1, rows.shape[-1])
    return lax.psum_scatter(rows, "seq", scatter_dimension=0, tiled=True)


def last_sum(*rows):
    size = lax.axis_size("seq")
    narrow = min(part.shape[1] for part in rows)
    blocks, counts = [], []
    for part in rows:
        part = part.reshape(size, -1, part.shape[1])
        counts.append((part.shape[1], part.shape[2] // narrow))
        blocks += [part[:, :, i * narrow : (i + 1) * narrow] for i in range(counts[-1][1])]
    joint = jnp.concatenate(blocks, axis=1) if len(blocks) > 1 else blocks[0]
    joint = joint.reshape(-1, narrow)
    total = lax.psum_scatter(joint, "seq", scatter_dimension=0, tiled=True)
    results, start = [], 0
    for height, count in counts:
        parts = [total[start + i * height : start + (i + 1) * height] for i in range(count)]
        results.append(jnp.concatenate(parts, axis=1) if count > 1 else parts[0])
        start += height * count
    return results


def norm_stats(hidden):
    centred = hidden - jnp.mean(hidden, axis=-1, keepdims=True)
    rate = lax.rsqrt(jnp.mean(centred * centred, axis=-1, keepdims=True) + eps_norm)
    return centred * rate, rate


def norm_back(grad, normal, rate, scale_term):
    inner = grad * (1.0 + scale_term)
    return rate * (
        inner
        - jnp.mean(inner, axis=-1, keepdims=True)
        - normal * jnp.mean(inner * normal, axis=-1, keepdims=True)
    )


def time_features(times, feature_count):
    half = feature_count // 2
    steps = jnp.exp(jnp.arange(half, dtype=F32) * (-math.log(10000.0) / (half - 1)))
    angles = 1000.0 * times[:, None] * steps
    return jnp.concatenate([jnp.sin(angles), jnp.cos(angles)], axis=-1).astype(BF)


def params(mebibytes):
    return pltpu.CompilerParams(vmem_limit_bytes=mebibytes * 1024 * 1024)


def once(shape, index_map=None):
    fixed = index_map or (lambda i: (0,) * len(shape))
    return pl.BlockSpec(shape, fixed, pipeline_mode=pl.Buffered(1))


def in_hbm(value):
    return pltpu.with_memory_space_constraint(value, pltpu.HBM)


def cost(flops, moved, hard=0):
    return pl.CostEstimate(flops=int(flops), bytes_accessed=int(moved), transcendentals=int(hard))


def turn(values):
    lanes = lax.broadcasted_iota(jnp.int32, values.shape, 1)
    low = lax.rem(lanes, HD) < HD // 2
    return jnp.where(low, pltpu.roll(values, PAIR - HD // 2, 1), pltpu.roll(values, HD // 2, 1))


def project_kernel(tiles, x_ref, w_ref, cos_ref, sin_ref, q_ref, kv_ref):
    raw = dot(x_ref[...], w_ref[...])
    step = pl.program_id(0)

    def rotated(o_ref, factor):
        for first in range(0, raw.shape[1], PAIR):
            part = raw[:, first : first + PAIR]
            turned = part * cos_ref[...] + turn(part) * sin_ref[...]
            o_ref[:, first : first + PAIR] = (turned * factor).astype(BF)

    @pl.when(step < tiles)
    def _():
        rotated(q_ref, HD ** (-0.5) * LOG2E)

    @pl.when((step >= tiles) & (step < 2 * tiles))
    def _():
        rotated(kv_ref, 1.0)

    @pl.when(step >= 2 * tiles)
    def _():
        kv_ref[...] = raw.astype(BF)


def project(normed, w_qkv, cos_table, sin_table):
    frames, width = normed.shape
    tile = 512
    tiles = width // tile
    return pl.pallas_call(
        functools.partial(project_kernel, tiles),
        grid=(3 * tiles,),
        in_specs=[
            once((frames, width)),
            pl.BlockSpec((width, tile), lambda i: (0, i)),
            once((frames, PAIR)),
            once((frames, PAIR)),
        ],
        out_specs=[
            pl.BlockSpec((frames, tile), lambda i: (0, jnp.minimum(i, tiles - 1))),
            pl.BlockSpec((frames, tile), lambda i: (0, jnp.maximum(i - tiles, 0))),
        ],
        out_shape=[
            jax.ShapeDtypeStruct((frames, width), BF),
            jax.ShapeDtypeStruct((frames, 2 * width), BF),
        ],
        compiler_params=params(20),
        cost_estimate=cost(6 * frames * width * width, 6 * width * width + 8 * frames * width),
    )(normed, pltpu.with_memory_space_constraint(w_qkv, pltpu.VMEM), cos_table, sin_table)


def only_head(values, which):
    lanes = lax.broadcasted_iota(jnp.int32, values.shape, 1)
    mine = (lanes >= which * HD) & (lanes < (which + 1) * HD)
    return jnp.where(mine, values, jnp.zeros_like(values))


def attend_kernel(span, q_ref, *refs):
    k_refs, v_refs = refs[:span], refs[span : 2 * span]
    mk_ref, mq_ref, o_ref, p_ref, l_ref = refs[2 * span :]
    frames = q_ref.shape[0]
    values_t = [v[...].T for v in v_refs]
    ones = jnp.ones((16, frames), BF)
    keys = [
        jnp.concatenate([k[...], mk_ref[i * frames : (i + 1) * frames, :]], axis=1)
        for i, k in enumerate(k_refs)
    ]
    both = []
    for which in range(2):
        queries = jnp.concatenate([only_head(q_ref[...], which), mq_ref[...]], axis=1)
        both.append([dot(k, queries, DIMS_LAST) for k in keys])
    results, inverses = [], []
    for which, scores in enumerate(both):
        top = functools.reduce(jnp.maximum, [jnp.max(s, axis=0, keepdims=True) for s in scores])
        result = None
        for index, part in enumerate(scores):
            powered = jnp.exp2(part - top).astype(BF)
            p_ref[which, index * frames : (index + 1) * frames, :] = powered
            lanes = values_t[index][which * HD : (which + 1) * HD]
            part = dot(jnp.concatenate([lanes, ones], axis=0), powered)
            result = part if result is None else result + part
        inverse = 1.0 / result[HD : HD + 1]
        results.append(result[:HD] * inverse)
        inverses.append(inverse)
    o_ref[...] = jnp.concatenate(results, axis=0).T.astype(BF)
    l_ref[0] = jnp.concatenate(inverses + [jnp.zeros((6, frames), F32)], axis=0)


def mask_lanes(segments, live, places, bucket_len):
    lanes = jnp.arange(PAIR)[None, :]
    segment = (lanes < SEGMENTS) & (segments[:, None] == lanes)
    place = places[:, None] - (bucket_len - PADDING) == lanes - SEGMENTS
    place = place & (lanes >= SEGMENTS) & (lanes < SEGMENTS + PADDING)
    keys = (segment | (place & (live[:, None] == 0))).astype(BF)
    fill = (lanes < SEGMENTS + PADDING) & ~(segment | place)
    return keys, jnp.where(fill, neg_fill, 0.0).astype(BF)


def columns(frames, start=0):
    return pl.BlockSpec((frames, PAIR), lambda i: (0, start + i))


def attend(queries, pairs_kv, mask_keys, mask_queries):
    span = len(pairs_kv)
    frames, width = queries.shape
    pairs = width // PAIR
    keys = span * frames
    return pl.pallas_call(
        functools.partial(attend_kernel, span),
        grid=(pairs,),
        in_specs=[columns(frames)]
        + [columns(frames)] * span
        + [columns(frames, pairs)] * span
        + [
            once((keys, PAIR)),
            once((frames, PAIR)),
        ],
        out_specs=[
            columns(frames),
            pl.BlockSpec((2, keys, frames), lambda i: (i, 0, 0)),
            pl.BlockSpec((1, 8, frames), lambda i: (i, 0, 0)),
        ],
        out_shape=[
            jax.ShapeDtypeStruct((frames, width), BF),
            pltpu.HBM((2 * pairs, keys, frames), BF),
            jax.ShapeDtypeStruct((pairs, 8, frames), F32),
        ],
        compiler_params=params(28),
        cost_estimate=cost(
            16 * pairs * frames * keys * PAIR,
            4 * pairs * frames * keys,
            2 * pairs * frames * keys,
        ),
    )(queries, *pairs_kv, *pairs_kv, mask_keys, mask_queries)


def attend_back_kernel(span, q_ref, *refs):
    k_refs, v_refs = refs[:span], refs[span : 2 * span]
    p_ref, c_ref, g_ref, cos_ref, sin_ref = refs[2 * span : 2 * span + 5]
    dq_ref, dkv_refs, ds_ref = refs[2 * span + 5], refs[2 * span + 6 : -1], refs[-1]
    frames = q_ref.shape[0]

    def unturn(grad, index):
        rows = slice(index * frames, (index + 1) * frames)
        return grad * cos_ref[rows, :] - turn(grad) * sin_ref[rows, :]

    keys_t = [k[...].T for k in k_refs]
    dk, dv, dq = [None] * span, [None] * span, []
    for which in range(2):
        centre = c_ref[0, which : which + 1, :]
        grads = only_head(g_ref[...], which)
        queries = only_head(q_ref[...], which)
        result = None
        for index in range(span):
            rows = slice(index * frames, (index + 1) * frames)
            grad_probs = dot(v_refs[index][...], grads, DIMS_LAST)
            soft = p_ref[which, rows, :]
            ds_ref[rows, :] = (soft.astype(F32) * (grad_probs - centre)).astype(BF)
            part = dot(soft, grads)
            dv[index] = part if dv[index] is None else dv[index] + part
            part = dot(ds_ref[rows, :], queries)
            dk[index] = part if dk[index] is None else dk[index] + part
            part = dot(keys_t[index][which * HD : (which + 1) * HD], ds_ref[rows, :])
            result = part if result is None else result + part
        dq.append(result)
    dq = jnp.concatenate(dq, axis=0).T
    dq_ref[...] = unturn(dq * HD ** (-0.5), 0).astype(BF)
    for index in range(span):
        dkv_refs[index][0] = unturn(dk[index] * (1.0 / LOG2E), index).astype(BF)
        dkv_refs[index][1] = dv[index].astype(BF)


def attend_back(queries, pairs_kv, probs, centres, grads, cos_keys, sin_keys):
    span = len(pairs_kv)
    frames, width = queries.shape
    pairs = width // PAIR
    keys = span * frames
    results = pl.pallas_call(
        functools.partial(attend_back_kernel, span),
        grid=(pairs,),
        in_specs=[columns(frames)]
        + [columns(frames)] * span
        + [columns(frames, pairs)] * span
        + [
            pl.BlockSpec((2, keys, frames), lambda i: (i, 0, 0)),
            pl.BlockSpec((1, 8, frames), lambda i: (i, 0, 0)),
            columns(frames),
            once((keys, PAIR)),
            once((keys, PAIR)),
        ],
        out_specs=[columns(frames)]
        + [pl.BlockSpec((2, frames, PAIR), lambda i: (0, 0, i))] * span,
        out_shape=[jax.ShapeDtypeStruct((frames, width), BF)]
        + [jax.ShapeDtypeStruct((2, frames, width), BF)] * span,
        scratch_shapes=[pltpu.VMEM((keys, frames), BF)],
        compiler_params=params(52),
        cost_estimate=cost(32 * pairs * frames * keys * PAIR, 4 * pairs * frames * keys),
    )(queries, *pairs_kv, *pairs_kv, in_hbm(probs), centres, grads, cos_keys, sin_keys)
    return results[0], results[1:]


def seq_blocks(rows):
    size = lax.axis_size("seq")
    return size if rows // lax.axis_size("head") // size % 16 == 0 else 1


def split_rows(source, target, groups, low_bit, blocks=1):
    chunk = source.shape[0] // groups // blocks
    half = source.shape[0] // 2
    for index in range(groups // 2):
        for part, bit in ((0, 1 - low_bit), (1, low_bit)):
            for block in range(blocks):
                first = pl.multiple_of(((2 * index + bit) * blocks + block) * chunk, chunk)
                start = part * half + (block * (groups // 2) + index) * chunk
                target[start : start + chunk, :] = source[pl.ds(first, chunk), :]


def fetches(pairs, sems):
    return [
        pltpu.make_async_copy(source, target, sems.at[index])
        for index, (source, target) in enumerate(pairs)
    ]


def feed_kernel(groups, blocks, x_ref, g_ref, up_ref, down_ref, l_ref, *refs):
    later, refs = refs[:4], refs[4:]
    da_ref, dk_ref, ua_ref, uk_ref = refs[:4]
    out_ref, gl_ref, gs_ref, gc_ref, o_ref, c_ref = refs[4:10]
    acc_ref, gx_ref, t_ref, xt_ref, mid_ref, scale_ref, w_ref, a_ref, sems = refs[10:]
    step = pl.program_id(0)
    low_bit = lax.axis_index("head") % 2
    copies = fetches(zip(later, (mid_ref, scale_ref, w_ref, a_ref), strict=True), sems)

    @pl.when(step == 0)
    def _():
        for copy in copies:
            copy.start()
        t_ref[...] = x_ref[...].T
        split_rows(t_ref, xt_ref, groups, low_bit, blocks)
        acc_ref[...] = jnp.zeros_like(acc_ref)
        gx_ref[...] = jnp.zeros_like(gx_ref)

    @pl.when(step < groups)
    def _():
        up = dot(x_ref[...], up_ref[...])
        grad_hidden = dot(g_ref[...], down_ref[...], DIMS_LAST)
        root = math.sqrt(2.0 / math.pi)
        square = up * up
        bent = jnp.tanh(root * up * (1.0 + 0.044715 * square))
        half = 0.5 + 0.5 * bent
        slope = half + 0.5 * up * (1.0 - bent * bent) * (root * (1.0 + 3 * 0.044715 * square))
        hidden = (up * half).astype(BF)
        grad_up = (grad_hidden * slope).astype(BF)
        acc_ref[...] += dot(hidden, down_ref[...])
        gx_ref[...] += dot(grad_up, up_ref[...], DIMS_LAST)
        rows = dot(hidden, g_ref[...], DIMS_FIRST).astype(BF)

        @pl.when(step % 2 == low_bit)
        def _():
            dk_ref[...] = rows

        @pl.when(step % 2 != low_bit)
        def _():
            da_ref[...] = rows

        depth = x_ref.shape[1] // 2
        ua_ref[...] = dot(xt_ref[:depth, :], grad_up).astype(BF)
        uk_ref[...] = dot(xt_ref[depth:, :], grad_up).astype(BF)

    @pl.when(step == groups)
    def _():
        for copy in copies:
            copy.wait()

    @pl.when(step >= groups)
    def _():
        few = out_ref.shape[0]
        here = pl.ds(pl.multiple_of((step - groups) * few, few), few)
        mid, grad = mid_ref[here, :], gx_ref[here, :]
        out_ref[...] = (mid + acc_ref[here, :]).astype(BF)
        normal, rate = norm_stats(mid)
        grad_mid = g_ref[here, :].astype(F32) + norm_back(grad, normal, rate, scale_ref[here, :])
        grad_low = grad_mid.astype(BF)
        gl_ref[...] = grad_low
        gs_ref[...] = grad.astype(BF)
        gc_ref[...] = (grad * normal).astype(BF)
        heads = dot(w_ref[...], grad_low, DIMS_LAST)
        for pair in range(l_ref.shape[0]):
            lanes = slice(pair * PAIR, (pair + 1) * PAIR)
            scaled, centres = [], []
            results = a_ref[here, lanes].T
            for which in range(2):
                rows = slice(pair * PAIR + which * HD, pair * PAIR + (which + 1) * HD)
                scaled.append(heads[rows] * l_ref[pair, which : which + 1, :])
                product = scaled[-1] * results[which * HD : (which + 1) * HD].astype(F32)
                centres.append(jnp.sum(product, axis=0, keepdims=True))
            o_ref[:, lanes] = jnp.concatenate(scaled, axis=0).astype(BF).T
            c_ref[pair] = jnp.concatenate(centres + [jnp.zeros((6, few), F32)], axis=0)


def feed(normed, cot_resid, w_up, w_down, resid_mid, scale, w_out, attended, inverses):
    groups = lax.axis_size("head")
    frames, width = normed.shape
    pairs = width // PAIR
    tile = w_up.shape[1] // groups
    inner = groups * tile
    few = 128
    whole = once((frames, width))
    last = groups - 1
    rows = pl.BlockSpec((tile, width), lambda i: (jnp.minimum(i, last) // 2, 0))
    cols = pl.BlockSpec((width // 2, tile), lambda i: (0, jnp.minimum(i, last)))
    part = pl.BlockSpec((few, width), lambda i: (jnp.maximum(i - groups, 0), 0))
    heads = pl.BlockSpec((pairs, 8, few), lambda i: (0, 0, jnp.maximum(i - groups, 0)))
    low = jax.ShapeDtypeStruct((frames, width), BF)
    anywhere = pl.BlockSpec(memory_space=pl.ANY)
    return pl.pallas_call(
        functools.partial(feed_kernel, groups, seq_blocks(width)),
        grid=(groups + frames // few,),
        in_specs=[
            whole,
            whole,
            pl.BlockSpec((width, tile), lambda i: (0, jnp.minimum(i, last))),
            pl.BlockSpec((tile, width), lambda i: (jnp.minimum(i, last), 0)),
            heads,
        ]
        + [anywhere] * 4,
        out_specs=[rows, rows, cols, cols] + [part] * 5 + [heads],
        out_shape=[
            jax.ShapeDtypeStruct((inner // 2, width), BF),
            pltpu.HBM((inner // 2, width), BF),
            jax.ShapeDtypeStruct((width // 2, inner), BF),
            pltpu.HBM((width // 2, inner), BF),
        ]
        + [low]
        + [pltpu.HBM((frames, width), BF)] * 3
        + [low]
        + [jax.ShapeDtypeStruct((pairs, 8, frames), F32)],
        scratch_shapes=[
            pltpu.VMEM((frames, width), F32),
            pltpu.VMEM((frames, width), F32),
            pltpu.VMEM((width, frames), BF),
            pltpu.VMEM((width, frames), BF),
            pltpu.VMEM((frames, width), F32),
            pltpu.VMEM((frames, width), F32),
            pltpu.VMEM((width, width), BF),
            pltpu.VMEM((frames, width), BF),
            pltpu.SemaphoreType.DMA((4,)),
        ],
        compiler_params=params(40),
        cost_estimate=cost(12 * frames * width * inner, 8 * width * inner, frames * inner),
    )(
        normed,
        cot_resid,
        in_hbm(w_up),
        in_hbm(w_down),
        inverses,
        resid_mid,
        scale,
        w_out,
        attended,
    )


def near_kernel(groups, span, *refs):
    dq_ref, dkv_refs, refs = refs[0], refs[1 : span + 1], refs[span + 1 :]
    w_ref, x_ref, gl_ref = refs[:3]
    attended, second, scale, grad_mid = refs[3:7]
    away_ref, keep_ref, gi_ref, gs_ref, gc_ref = refs[7:12]
    t_ref, xt_ref, acc_ref, a_ref, r_ref, scale_ref, gm_ref, sems = refs[12:]
    step = pl.program_id(0)
    tiles = x_ref.shape[1] // dq_ref.shape[1]
    low_bit = lax.axis_index("head") % 2
    width = x_ref.shape[1]
    half = width // 2
    first, *rest = fetches(
        [
            (attended, a_ref),
            (second.at[:, pl.ds(width, width)], r_ref),
            (scale, scale_ref),
            (grad_mid, gm_ref),
        ],
        sems,
    )

    @pl.when(step == 0)
    def _():
        for copy in (first, *rest):
            copy.start()
        t_ref[...] = x_ref[...].T
        split_rows(t_ref, xt_ref, groups, low_bit)

    @pl.when(step == 3 * tiles)
    def _():
        first.wait()
        t_ref[...] = a_ref[...].T
        split_rows(t_ref, xt_ref, groups, low_bit)

    def one(grads):
        away_ref[...] = dot(xt_ref[:half, :], grads).astype(BF)
        keep_ref[...] = dot(xt_ref[half:, :], grads).astype(BF)

    def projected(grads, start):
        one(grads)
        part = dot(grads, w_ref[...], DIMS_LAST)
        acc_ref[...] = part if start else acc_ref[...] + part

    @pl.when(step == 0)
    def _():
        projected(dq_ref[...], True)

    @pl.when((step > 0) & (step < tiles))
    def _():
        projected(dq_ref[...], False)

    @pl.when((step >= tiles) & (step < 3 * tiles))
    def _():
        grads = functools.reduce(jnp.add, [ref[0].astype(F32) for ref in dkv_refs])
        projected(grads.astype(BF), False)

    @pl.when((step >= 3 * tiles) & (step < 4 * tiles))
    def _():
        one(gl_ref[...])

    @pl.when(step == 4 * tiles)
    def _():
        for copy in rest:
            copy.wait()

    @pl.when(step >= 4 * tiles)
    def _():
        few = gi_ref.shape[0]
        here = pl.ds(pl.multiple_of((step - 4 * tiles) * few, few), few)
        normal, rate = norm_stats(r_ref[here, :].astype(F32))
        grad = acc_ref[here, :]
        grad_in = gm_ref[here, :].astype(F32) + norm_back(grad, normal, rate, scale_ref[here, :])
        gi_ref[...] = grad_in.astype(BF)
        gs_ref[...] = grad.astype(BF)
        gc_ref[...] = (grad * normal).astype(BF)


def near(dq, dkv, w_qkv, normed, attended, grad_low, cot_resid, scale):
    groups = lax.axis_size("head")
    frames, width = dq.shape
    tile = 512
    few = 128
    tiles = width // tile

    def pair(i):
        index = jnp.clip(i - tiles, 0, 2 * tiles - 1)
        return (index // tiles, 0, index % tiles)

    grads = pl.BlockSpec((width // 2, tile), lambda i: (0, jnp.minimum(i, 4 * tiles - 1)))
    part = pl.BlockSpec((few, width), lambda i: (jnp.maximum(i - 4 * tiles, 0), 0))
    out = pltpu.HBM((width // 2, 4 * width), BF)
    low = jax.ShapeDtypeStruct((frames, width), BF)
    return pl.pallas_call(
        functools.partial(near_kernel, groups, len(dkv)),
        grid=(4 * tiles + frames // few,),
        in_specs=[pl.BlockSpec((frames, tile), lambda i: (0, jnp.minimum(i, tiles - 1)))]
        + [pl.BlockSpec((1, frames, tile), pair)] * len(dkv)
        + [
            pl.BlockSpec((width, tile), lambda i: (0, jnp.minimum(i, 3 * tiles - 1))),
            once((frames, width)),
            pl.BlockSpec((frames, tile), lambda i: (0, jnp.clip(i - 3 * tiles, 0, tiles - 1))),
        ]
        + [pl.BlockSpec(memory_space=pl.ANY)] * 4,
        out_specs=[grads, grads, part, part, part],
        out_shape=[out, out, low, low, low],
        scratch_shapes=[
            pltpu.VMEM((width, frames), BF),
            pltpu.VMEM((width, frames), BF),
            pltpu.VMEM((frames, width), F32),
            pltpu.VMEM((frames, width), BF),
            pltpu.VMEM((frames, width), BF),
            pltpu.VMEM((frames, width), F32),
            pltpu.VMEM((frames, width), BF),
            pltpu.SemaphoreType.DMA((4,)),
        ],
        compiler_params=params(52),
        cost_estimate=cost(14 * frames * width * width, 14 * width * width + 30 * frames * width),
    )(dq, *dkv, w_qkv, normed, grad_low, attended, cot_resid, scale, grad_low)


def far_kernel(groups, x_ref, y_ref, f_ref, gi_ref, *refs):
    m_refs, (away_ref, keep_ref, t_ref, st_ref, u_ref, ft_ref) = refs[:4], refs[4:]
    low_bit = lax.axis_index("head") % 2
    width = x_ref.shape[1]

    @pl.when(pl.program_id(0) == 0)
    def _():
        t_ref[:width, :] = x_ref[...].T
        t_ref[width:, :] = y_ref[...].T
        split_rows(t_ref, st_ref, groups, low_bit)
        u_ref[...] = f_ref[...].T
        split_rows(u_ref, ft_ref, groups, low_bit)

    many, few = 2 * width // groups, u_ref.shape[0] // groups
    for part, out_ref in enumerate((away_ref, keep_ref)):
        big = dot(st_ref[part * width : (part + 1) * width, :], gi_ref[...]).astype(BF)
        half = u_ref.shape[0] // 2
        here = ft_ref[part * half : (part + 1) * half, :]
        small = [dot(here, m_ref[...]).astype(BF) for m_ref in m_refs]
        for index in range(groups // 2):
            start = index * (many + 4 * few)
            out_ref[start : start + many, :] = big[index * many : (index + 1) * many]
            for block in range(4):
                first = start + many + block * few
                out_ref[first : first + few, :] = small[block][index * few : (index + 1) * few]


def far(inputs, skips, features, grad_in, grad_mods):
    groups = lax.axis_size("head")
    frames, width = grad_in.shape
    few = features.shape[1]
    tile = 512
    cols = pl.BlockSpec((frames, tile), lambda i: (0, i))
    out = pl.BlockSpec((width + 2 * few, tile), lambda i: (0, i))
    return pl.pallas_call(
        functools.partial(far_kernel, groups),
        grid=(width // tile,),
        in_specs=[once((frames, width)), once((frames, width)), once((frames, few))] + [cols] * 5,
        out_specs=[out, out],
        out_shape=[pltpu.HBM((width + 2 * few, width), BF)] * 2,
        scratch_shapes=[pltpu.VMEM((2 * width, frames), BF)] * 2
        + [pltpu.VMEM((few, frames), BF)] * 2,
        compiler_params=params(52),
        cost_estimate=cost(6 * frames * width * width, 6 * width * width + 20 * frames * width),
    )(inputs, skips, features, grad_in, *grad_mods)


def per_device(
    inputs,
    skips,
    flow_time,
    segment_ids,
    frame_mask,
    cotangent,
    w_skip,
    w_time,
    w_qkv,
    w_out,
    w_up,
    w_down,
):
    groups = lax.axis_size("head")
    micro_count, _, rows, width = inputs.shape
    span = groups // micro_count
    place = lax.axis_index("head")
    mine = place // span
    frames = micro_count * rows
    feature_count = w_time.shape[0]
    inputs, skips, cotangent = inputs[:, 0], skips[:, 0], cotangent[:, 0]

    resid_own = dot(inputs.reshape(frames, width), w_skip[:width]) + dot(
        skips.reshape(frames, width), w_skip[width:]
    )
    own_mod = dot(time_features(flow_time.reshape(-1), feature_count), w_time[:, : 2 * width])
    normed_own = norm_stats(resid_own)[0] * (1.0 + own_mod[:, width:]) + own_mod[:, :width]
    normed_own = cut_parts(normed_own.astype(BF).reshape(micro_count, rows, width), mine)

    meta = jnp.stack(
        [segment_ids[:, 0].astype(F32), frame_mask[:, 0].astype(F32), flow_time[:, 0]], axis=1
    )[None]
    meta = jnp.concatenate([meta, swap(meta, "head", 1)])
    meta, *normed_own = together(meta, *normed_own)
    normed_attn = send_parts(normed_own, span)
    resid_low = resid_own.astype(BF).reshape(micro_count, rows, width)
    for bit in range(1, groups.bit_length() - 1):
        meta = jnp.concatenate([meta, swap(meta, "head", 2**bit)])
        if bit == 1:
            meta, cotangent, resid_low = together(meta, cotangent, resid_low)
    second = [
        jnp.concatenate(pair, axis=1)
        for pair in zip(cut_parts(cotangent, mine), cut_parts(resid_low, mine), strict=True)
    ]
    meta, *rest = together(meta, *normed_attn, *second)
    normed_attn, second = jnp.concatenate(rest[:micro_count]), rest[micro_count:]
    meta = pick(meta, mine, 1).reshape(micro_count, span, 3, rows)
    seg_keys, live_keys, times = [meta[:, :, i].swapaxes(0, 1).reshape(-1) for i in range(3)]
    order = jnp.stack(
        [place ^ other ^ (step * span) for other in range(span) for step in range(micro_count)]
    )
    place_keys = (order[:, None] * rows + jnp.arange(rows)[None, :]).reshape(-1).astype(F32)
    starts = jnp.sum((seg_keys[None, :] < seg_keys[:, None]).astype(F32), axis=1)
    positions = place_keys - starts
    inv_freq = jnp.exp(jnp.arange(HD // 2, dtype=F32) * (-2.0 * math.log(10000.0) / HD))
    turns = positions[:, None] * inv_freq
    cos_half, sin_half = jnp.cos(turns), jnp.sin(turns)
    cos_keys = jnp.concatenate([cos_half] * 4, axis=1)
    sin_keys = jnp.concatenate([-sin_half, sin_half] * 2, axis=1)

    queries, keys_values = project(normed_attn, w_qkv, cos_keys[:frames], sin_keys[:frames])
    keys_values, seg_keys, live_keys, place_keys, times = together(
        keys_values, seg_keys, live_keys, place_keys, times
    )
    pairs_kv = [keys_values] + [swap(keys_values, "head", other) for other in range(1, span)]
    mask_keys, mask_queries = mask_lanes(seg_keys, live_keys, place_keys, groups * rows)
    queries, mask_keys, mask_queries, *pairs_kv = together(
        queries, mask_keys, mask_queries[:frames], *pairs_kv
    )

    second = send_parts(second, span)
    attended, probs, inverses = attend(queries, pairs_kv, mask_keys, mask_queries)
    attended, times = together(attended, times)
    features = time_features(times[:frames], feature_count)
    scale_first, shift_second, scale_second = [
        dot(features, w_time[:, i * width : (i + 1) * width]) for i in range(1, 4)
    ]
    attended, scale_first, shift_second, scale_second, *second = together(
        attended, scale_first, shift_second, scale_second, *second
    )
    second = jnp.concatenate(second)
    resid_mid = second[:, width:].astype(F32) + dot(attended, w_out)
    normal_second = norm_stats(resid_mid)[0]
    normed_ffn = (normal_second * (1.0 + scale_second) + shift_second).astype(BF)

    (
        down_away, down_keep, up_away, up_keep, output, grad_mid, mod_shift, mod_scale, grads, centres
    ) = feed(
        normed_ffn, second, w_up, w_down, resid_mid, scale_second, w_out, attended, inverses
    )
    grads, down_away, up_away, output = together(grads, down_away, up_away, output)
    seq_bits = lax.axis_size("seq").bit_length() - 1
    bits = list(range(seq_bits + 1, seq_bits + groups.bit_length() - 1))
    orders = (bits, bits[::-1])

    def two_ways(*arrays):
        middle_col = arrays[0].shape[1] // 2
        return [Rows(list(arrays), bits, 1, (i * middle_col, middle_col)) for i in range(2)]

    def begin(*pairs, index):
        return [
            away_all([pair[side] for pair in pairs], order[index])
            for side, order in enumerate(orders)
        ]

    def send(away, index):
        return [cross(rows, order[index]) for rows, order in zip(away, orders, strict=True)]

    def end(*pairs, came):
        for side, rows in enumerate(came):
            join_all([pair[side] for pair in pairs], rows)

    down_came, up_came = swap(down_away, "head", 1), swap(up_away, "head", 1)
    output = send_parts(list(output.reshape(micro_count, rows, width)), span)
    dq, dkv = attend_back(queries, pairs_kv, probs, centres, grads, cos_keys, sin_keys)
    dq, down_came, up_came, *rest = together(dq, down_came, up_came, *dkv, *output)
    dkv, output = rest[:span], rest[span:]

    dkv[1:] = [swap(part, "head", other) for other, part in enumerate(dkv) if other > 0]
    down = two_ways(down_keep, down_came)
    half = up_keep.shape[1] // 2
    up_0 = add_low([up_keep[:, :half], up_came[:, :half]])
    up_1 = add_low([up_keep[:, half:], up_came[:, half:]])
    dq, up_0, up_1, down_came, *dkv = together(dq, up_0, up_1, down_came, *dkv)
    up_0 = seq_first(up_0)
    down = two_ways(down_keep, down_came)
    dq, *away = together(dq, *begin(down, index=0))
    came = send(away, 0)
    near_away, near_keep, grad_in_low, first_shift, first_scale = near(
        dq, dkv, w_qkv, normed_attn, attended, grad_mid, second, scale_first
    )
    near_away, grad_in_low, *came = together(near_away, grad_in_low, *came)
    end(down, came=came)

    near_came = swap(near_away, "head", 1)
    for index in range(1, len(bits) - 1):
        end(down, came=send(begin(down, index=index), index))
    last_index = len(bits) - 1
    grad_in_low, *away = together(grad_in_low, *begin(down, index=last_index))
    came = send(away, last_index)
    grad_local = send_parts(list(grad_in_low.reshape(micro_count, rows, width)), span)
    wide = two_ways(near_keep, near_came)
    up_0, *rest = together(up_0, *begin(wide, index=0), *came, *grad_local, *output)
    wide_away, came, rest = rest[:2], rest[2:4], rest[4:]
    grad_local, output = rest[:micro_count], rest[micro_count:]
    end(down, came=came)

    wide_came = send(wide_away, 0)
    grad_local = by_micro(grad_local, mine).reshape(frames, width)
    far_away, far_keep = far(
        inputs.reshape(frames, width),
        skips.reshape(frames, width),
        features,
        grad_local,
        [first_shift, first_scale, mod_shift, mod_scale],
    )
    up_1 = seq_first(up_1)
    down_rows = jnp.concatenate([part.read() for part in down], axis=1)
    far_away, down_rows, *wide_came = together(far_away, down_rows, *wide_came)
    end(wide, came=wide_came)

    far_came = swap(far_away, "head", 1)
    narrow = two_ways(far_keep, far_came)
    for index in range(1, len(bits)):
        wide_came = send(begin(wide, index=index), index)
        if index < last_index:
            end(wide, came=together(*wide_came))
    (down_sum,) = last_sum(down_rows)
    up_1, *rest = together(up_1, *begin(narrow, index=0), *wide_came)
    narrow_away, wide_came = rest[:2], rest[2:]
    end(wide, came=wide_came)

    narrow_came = send(narrow_away, 0)
    wide_sum = jnp.concatenate([wide[0].read(), wide[1].read()], axis=1)
    ups = [Rows([up_0], bits), Rows([up_1], bits)]
    rest = together(wide_sum, down_sum, *begin(ups, index=0), *narrow_came)
    wide_sum, down_sum, up_away = rest[0], rest[1], rest[2:4]
    end(narrow, came=rest[4:])

    (near_sum,) = last_sum(wide_sum)
    for index in range(1, len(bits)):
        end(narrow, came=together(*send(begin(narrow, index=index), index)))
    far_sum = jnp.concatenate([narrow[0].read(), narrow[1].read()], axis=1)
    many = w_skip.shape[0] // groups
    last = [
        Rows([far_sum[:many]], list(range(seq_bits))),
        Rows([far_sum[many:]], list(range(seq_bits)), 4),
    ]
    for index in range(max(seq_bits, len(bits))):
        came, up_came = [], []
        if index < seq_bits:
            came = [cross(away_all(last, index), index)]
        if index < len(bits):
            up_came = send(up_away, index)
        if index == 0:
            near_sum, *rest = together(near_sum, *came, *up_came)
            done = [
                by_micro(output, mine),
                near_sum[:, : 3 * width].astype(F32),
                near_sum[:, 3 * width :].astype(F32),
                down_sum.astype(F32),
            ]
        else:
            *done, rest = together(*done, [*came, *up_came])
        if index < seq_bits:
            join_all(last, rest[0])
        if index < len(bits):
            end(ups, came=rest[len(came) :])
        if index + 1 < len(bits):
            up_away = begin(ups, index=index + 1)
    output, total_qkv, total_out, total_down = done
    total_up = jnp.concatenate([part.read() for part in ups], axis=1).astype(F32)
    total_skip = last[0].read().astype(F32)
    total_time = last[1].read().astype(F32)
    total_time = total_time.reshape(4, -1, width).swapaxes(0, 1).reshape(-1, 4 * width)
    shape = (micro_count, 1, rows, width)
    input_grad = dot(grad_local, w_skip[:width], DIMS_LAST).reshape(shape)
    skip_grad = dot(grad_local, w_skip[width:], DIMS_LAST).reshape(shape)
    return (
        output[:, None],
        input_grad,
        skip_grad,
        total_skip,
        total_time,
        total_qkv,
        total_out,
        total_up,
        total_down,
    )


def solution(mesh):
    frames_spec = P(None, "seq", "head", None)
    line_spec = P(None, "seq", "head")
    shard_spec = P(("head", "seq"), None)
    return jax.shard_map(
        per_device,
        mesh=mesh,
        in_specs=(frames_spec, frames_spec, line_spec, line_spec, line_spec, frames_spec)
        + (P(),) * 6,
        out_specs=(frames_spec,) * 3 + (shard_spec,) * 6,
        check_vma=False,
    )
```

```python
import functools
import math

import jax
import jax.numpy as jnp
from jax import lax
from jax.experimental import pallas as pl
from jax.experimental.pallas import tpu as pltpu
from jax.sharding import PartitionSpec as P

HD = 64
PAIR = 2 * HD
eps_norm = 1e-06
neg_fill = -1e30
SEGMENTS = 8
PADDING = 64
BF = jnp.bfloat16
F32 = jnp.float32
DIMS_FIRST = (((0,), (0,)), ((), ()))
DIMS_LAST = (((1,), (1,)), ((), ()))
LOG2E = 1.4426950408889634


def dot(left, right, dims=(((1,), (0,)), ((), ()))):
    return lax.dot_general(left, right, dims, preferred_element_type=F32)


def swap(values, axis_name, bits):
    size = lax.axis_size(axis_name)
    return lax.ppermute(values, axis_name, [(i, i ^ bits) for i in range(size)])


def pick(values, index, axis):
    return lax.dynamic_index_in_dim(values, index, axis, keepdims=False)


def together(*values):
    return lax.optimization_barrier(values)


def cut_parts(values, mine):
    return [pick(values, mine ^ step, 0) for step in range(values.shape[0])]


def cut_pairs(left, right, mine):
    pairs = zip(cut_parts(left, mine), cut_parts(right, mine), strict=True)
    return [jnp.stack(pair) for pair in pairs]


def send_parts(parts, span):
    return parts[:1] + [
        swap(part, "head", step * span) for step, part in enumerate(parts) if step > 0
    ]


def by_micro(parts, mine):
    parts = jnp.stack(parts)
    return jnp.stack([pick(parts, mine ^ micro, 0) for micro in range(parts.shape[0])])


def add_low(terms):
    return functools.reduce(jnp.add, [term.astype(F32) for term in terms]).astype(BF)


class Rows:
    def __init__(self, arrays, bits, before=1, cols=None):
        self.order = sorted(bits, reverse=True)
        self.before, self.arrays = before, []
        self.start, self.size = cols or (0, arrays[0].shape[-1])
        self.chunk = arrays[0].size // arrays[0].shape[-1] // before // 2 ** len(bits)
        for array in arrays:
            self.join(array, self.start)

    def join(self, array, start=0):
        shape = [self.before] + [2] * len(self.order) + [self.chunk, array.shape[-1]]
        self.arrays.append((array.reshape(shape), tuple(self.order), {}, start))

    def read(self, bit=None, index=None):
        terms = []
        for array, bits, picks, start in self.arrays:
            picks = picks if bit is None else {**picks, bit: index}
            starts = [0] + [picks.get(b, 0) for b in bits] + [0, start]
            sizes = [self.before] + [1 if b in picks else 2 for b in bits] + [self.chunk, self.size]
            terms.append(lax.dynamic_slice(array, starts, sizes).reshape(-1, self.size))
        return add_low(terms)

    def away(self, bit):
        here = (place_of() >> bit) % 2
        sent = self.read(bit, 1 - here)
        self.order.remove(bit)
        for _, _, picks, _ in self.arrays:
            picks[bit] = here
        return sent


def place_of():
    return lax.axis_index("head") * lax.axis_size("seq") + lax.axis_index("seq")


def cross(rows, bit):
    seq_bits = lax.axis_size("seq").bit_length() - 1
    if bit < seq_bits:
        return swap(rows, "seq", 2**bit)
    return swap(rows, "head", 2 ** (bit - seq_bits))


def away_all(parts, bit):
    return jnp.concatenate([part.away(bit) for part in parts])


def join_all(parts, came):
    start = 0
    for part in parts:
        height = part.before * part.chunk * 2 ** len(part.order)
        part.join(came[start : start + height])
        start += height


def step_all(parts, bit):
    join_all(parts, cross(away_all(parts, bit), bit))


def seq_first(rows):
    size = lax.axis_size("seq")
    if seq_blocks(2 * rows.shape[0]) == 1:
        rows = rows.reshape(-1, size, rows.shape[0] * 2 // lax.axis_size("head") // size, rows.shape[1])
        rows = rows.swapaxes(0, 1).reshape(-1, rows.shape[-1])
    return lax.psum_scatter(rows, "seq", scatter_dimension=0, tiled=True)


def last_sum(*rows):
    size = lax.axis_size("seq")
    narrow = min(part.shape[1] for part in rows)
    blocks, counts = [], []
    for part in rows:
        part = part.reshape(size, -1, part.shape[1])
        counts.append((part.shape[1], part.shape[2] // narrow))
        blocks += [part[:, :, i * narrow : (i + 1) * narrow] for i in range(counts[-1][1])]
    joint = jnp.concatenate(blocks, axis=1) if len(blocks) > 1 else blocks[0]
    joint = joint.reshape(-1, narrow)
    total = lax.psum_scatter(joint, "seq", scatter_dimension=0, tiled=True)
    results, start = [], 0
    for height, count in counts:
        parts = [total[start + i * height : start + (i + 1) * height] for i in range(count)]
        results.append(jnp.concatenate(parts, axis=1) if count > 1 else parts[0])
        start += height * count
    return results


def norm_stats(hidden):
    centred = hidden - jnp.mean(hidden, axis=-1, keepdims=True)
    rate = lax.rsqrt(jnp.mean(centred * centred, axis=-1, keepdims=True) + eps_norm)
    return centred * rate, rate


def norm_back(grad, normal, rate, scale_term):
    inner = grad * (1.0 + scale_term)
    return rate * (
        inner
        - jnp.mean(inner, axis=-1, keepdims=True)
        - normal * jnp.mean(inner * normal, axis=-1, keepdims=True)
    )


def time_features(times, feature_count):
    half = feature_count // 2
    steps = jnp.exp(jnp.arange(half, dtype=F32) * (-math.log(10000.0) / (half - 1)))
    angles = 1000.0 * times[:, None] * steps
    return jnp.concatenate([jnp.sin(angles), jnp.cos(angles)], axis=-1).astype(BF)


def params(mebibytes):
    return pltpu.CompilerParams(vmem_limit_bytes=mebibytes * 1024 * 1024)


def once(shape, index_map=None):
    fixed = index_map or (lambda i: (0,) * len(shape))
    return pl.BlockSpec(shape, fixed, pipeline_mode=pl.Buffered(1))


def in_hbm(value):
    return pltpu.with_memory_space_constraint(value, pltpu.HBM)


def cost(flops, moved, hard=0):
    return pl.CostEstimate(flops=int(flops), bytes_accessed=int(moved), transcendentals=int(hard))


def turn(values):
    lanes = lax.broadcasted_iota(jnp.int32, values.shape, 1)
    low = lax.rem(lanes, HD) < HD // 2
    return jnp.where(low, pltpu.roll(values, PAIR - HD // 2, 1), pltpu.roll(values, HD // 2, 1))


def project_kernel(tiles, x_ref, w_ref, cos_ref, sin_ref, q_ref, kv_ref):
    raw = dot(x_ref[...], w_ref[...])
    step = pl.program_id(0)

    def rotated(o_ref, factor):
        for first in range(0, raw.shape[1], PAIR):
            part = raw[:, first : first + PAIR]
            turned = part * cos_ref[...] + turn(part) * sin_ref[...]
            o_ref[:, first : first + PAIR] = (turned * factor).astype(BF)

    @pl.when(step < tiles)
    def _():
        rotated(q_ref, HD ** (-0.5) * LOG2E)

    @pl.when((step >= tiles) & (step < 2 * tiles))
    def _():
        rotated(kv_ref, 1.0)

    @pl.when(step >= 2 * tiles)
    def _():
        kv_ref[...] = raw.astype(BF)


def project(normed, w_qkv, cos_table, sin_table):
    frames, width = normed.shape
    tile = 512
    tiles = width // tile
    return pl.pallas_call(
        functools.partial(project_kernel, tiles),
        grid=(3 * tiles,),
        in_specs=[
            once((frames, width)),
            pl.BlockSpec((width, tile), lambda i: (0, i)),
            once((frames, PAIR)),
            once((frames, PAIR)),
        ],
        out_specs=[
            pl.BlockSpec((frames, tile), lambda i: (0, jnp.minimum(i, tiles - 1))),
            pl.BlockSpec((frames, tile), lambda i: (0, jnp.maximum(i - tiles, 0))),
        ],
        out_shape=[
            jax.ShapeDtypeStruct((frames, width), BF),
            jax.ShapeDtypeStruct((frames, 2 * width), BF),
        ],
        compiler_params=params(20),
        cost_estimate=cost(6 * frames * width * width, 6 * width * width + 8 * frames * width),
    )(normed, pltpu.with_memory_space_constraint(w_qkv, pltpu.VMEM), cos_table, sin_table)


def only_head(values, which):
    lanes = lax.broadcasted_iota(jnp.int32, values.shape, 1)
    mine = (lanes >= which * HD) & (lanes < (which + 1) * HD)
    return jnp.where(mine, values, jnp.zeros_like(values))


def attend_kernel(span, q_ref, *refs):
    k_refs, v_refs = refs[:span], refs[span : 2 * span]
    mk_ref, mq_ref, o_ref, p_ref, l_ref = refs[2 * span :]
    frames = q_ref.shape[0]
    values_t = [v[...].T for v in v_refs]
    ones = jnp.ones((16, frames), BF)
    keys = [
        jnp.concatenate([k[...], mk_ref[i * frames : (i + 1) * frames, :]], axis=1)
        for i, k in enumerate(k_refs)
    ]
    both = []
    for which in range(2):
        queries = jnp.concatenate([only_head(q_ref[...], which), mq_ref[...]], axis=1)
        both.append([dot(k, queries, DIMS_LAST) for k in keys])
    results, inverses = [], []
    for which, scores in enumerate(both):
        top = functools.reduce(jnp.maximum, [jnp.max(s, axis=0, keepdims=True) for s in scores])
        result = None
        for index, part in enumerate(scores):
            powered = jnp.exp2(part - top).astype(BF)
            p_ref[which, index * frames : (index + 1) * frames, :] = powered
            lanes = values_t[index][which * HD : (which + 1) * HD]
            part = dot(jnp.concatenate([lanes, ones], axis=0), powered)
            result = part if result is None else result + part
        inverse = 1.0 / result[HD : HD + 1]
        results.append(result[:HD] * inverse)
        inverses.append(inverse)
    o_ref[...] = jnp.concatenate(results, axis=0).T.astype(BF)
    l_ref[0] = jnp.concatenate(inverses + [jnp.zeros((6, frames), F32)], axis=0)


def mask_lanes(segments, live, places, bucket_len):
    lanes = jnp.arange(PAIR)[None, :]
    segment = (lanes < SEGMENTS) & (segments[:, None] == lanes)
    place = places[:, None] - (bucket_len - PADDING) == lanes - SEGMENTS
    place = place & (lanes >= SEGMENTS) & (lanes < SEGMENTS + PADDING)
    keys = (segment | (place & (live[:, None] == 0))).astype(BF)
    fill = (lanes < SEGMENTS + PADDING) & ~(segment | place)
    return keys, jnp.where(fill, neg_fill, 0.0).astype(BF)


def columns(frames, start=0):
    return pl.BlockSpec((frames, PAIR), lambda i: (0, start + i))


def attend(queries, pairs_kv, mask_keys, mask_queries):
    span = len(pairs_kv)
    frames, width = queries.shape
    pairs = width // PAIR
    keys = span * frames
    return pl.pallas_call(
        functools.partial(attend_kernel, span),
        grid=(pairs,),
        in_specs=[columns(frames)]
        + [columns(frames)] * span
        + [columns(frames, pairs)] * span
        + [
            once((keys, PAIR)),
            once((frames, PAIR)),
        ],
        out_specs=[
            columns(frames),
            pl.BlockSpec((2, keys, frames), lambda i: (i, 0, 0)),
            pl.BlockSpec((1, 8, frames), lambda i: (i, 0, 0)),
        ],
        out_shape=[
            jax.ShapeDtypeStruct((frames, width), BF),
            pltpu.HBM((2 * pairs, keys, frames), BF),
            jax.ShapeDtypeStruct((pairs, 8, frames), F32),
        ],
        compiler_params=params(28),
        cost_estimate=cost(
            16 * pairs * frames * keys * PAIR,
            4 * pairs * frames * keys,
            2 * pairs * frames * keys,
        ),
    )(queries, *pairs_kv, *pairs_kv, mask_keys, mask_queries)


def attend_back_kernel(span, q_ref, *refs):
    k_refs, v_refs = refs[:span], refs[span : 2 * span]
    p_ref, c_ref, g_ref, cos_ref, sin_ref = refs[2 * span : 2 * span + 5]
    dq_ref, dkv_refs, ds_ref = refs[2 * span + 5], refs[2 * span + 6 : -1], refs[-1]
    frames = q_ref.shape[0]

    def unturn(grad, index):
        rows = slice(index * frames, (index + 1) * frames)
        return grad * cos_ref[rows, :] - turn(grad) * sin_ref[rows, :]

    keys_t = [k[...].T for k in k_refs]
    dk, dv, dq = [None] * span, [None] * span, []
    for which in range(2):
        centre = c_ref[0, which : which + 1, :]
        grads = only_head(g_ref[...], which)
        queries = only_head(q_ref[...], which)
        result = None
        for index in range(span):
            rows = slice(index * frames, (index + 1) * frames)
            grad_probs = dot(v_refs[index][...], grads, DIMS_LAST)
            soft = p_ref[which, rows, :]
            ds_ref[rows, :] = (soft.astype(F32) * (grad_probs - centre)).astype(BF)
            part = dot(soft, grads)
            dv[index] = part if dv[index] is None else dv[index] + part
            part = dot(ds_ref[rows, :], queries)
            dk[index] = part if dk[index] is None else dk[index] + part
            part = dot(keys_t[index][which * HD : (which + 1) * HD], ds_ref[rows, :])
            result = part if result is None else result + part
        dq.append(result)
    dq = jnp.concatenate(dq, axis=0).T
    dq_ref[...] = unturn(dq * HD ** (-0.5), 0).astype(BF)
    for index in range(span):
        dkv_refs[index][0] = unturn(dk[index] * (1.0 / LOG2E), index).astype(BF)
        dkv_refs[index][1] = dv[index].astype(BF)


def attend_back(queries, pairs_kv, probs, centres, grads, cos_keys, sin_keys):
    span = len(pairs_kv)
    frames, width = queries.shape
    pairs = width // PAIR
    keys = span * frames
    results = pl.pallas_call(
        functools.partial(attend_back_kernel, span),
        grid=(pairs,),
        in_specs=[columns(frames)]
        + [columns(frames)] * span
        + [columns(frames, pairs)] * span
        + [
            pl.BlockSpec((2, keys, frames), lambda i: (i, 0, 0)),
            pl.BlockSpec((1, 8, frames), lambda i: (i, 0, 0)),
            columns(frames),
            once((keys, PAIR)),
            once((keys, PAIR)),
        ],
        out_specs=[columns(frames)]
        + [pl.BlockSpec((2, frames, PAIR), lambda i: (0, 0, i))] * span,
        out_shape=[jax.ShapeDtypeStruct((frames, width), BF)]
        + [jax.ShapeDtypeStruct((2, frames, width), BF)] * span,
        scratch_shapes=[pltpu.VMEM((keys, frames), BF)],
        compiler_params=params(52),
        cost_estimate=cost(32 * pairs * frames * keys * PAIR, 4 * pairs * frames * keys),
    )(queries, *pairs_kv, *pairs_kv, in_hbm(probs), centres, grads, cos_keys, sin_keys)
    return results[0], results[1:]


def seq_blocks(rows):
    size = lax.axis_size("seq")
    return size if rows // lax.axis_size("head") // size % 16 == 0 else 1


def split_rows(source, target, groups, low_bit, blocks=1):
    chunk = source.shape[0] // groups // blocks
    half = source.shape[0] // 2
    for index in range(groups // 2):
        for part, bit in ((0, 1 - low_bit), (1, low_bit)):
            for block in range(blocks):
                first = pl.multiple_of(((2 * index + bit) * blocks + block) * chunk, chunk)
                start = part * half + (block * (groups // 2) + index) * chunk
                target[start : start + chunk, :] = source[pl.ds(first, chunk), :]


def fetches(pairs, sems):
    return [
        pltpu.make_async_copy(source, target, sems.at[index])
        for index, (source, target) in enumerate(pairs)
    ]


def feed_kernel(groups, blocks, x_ref, g_ref, up_ref, down_ref, l_ref, *refs):
    later, refs = refs[:4], refs[4:]
    da_ref, dk_ref, ua_ref, uk_ref = refs[:4]
    out_ref, gl_ref, gs_ref, gc_ref, o_ref, c_ref = refs[4:10]
    acc_ref, gx_ref, t_ref, xt_ref, mid_ref, scale_ref, w_ref, a_ref, sems = refs[10:]
    step = pl.program_id(0)
    low_bit = lax.axis_index("head") % 2
    copies = fetches(zip(later, (mid_ref, scale_ref, w_ref, a_ref), strict=True), sems)

    @pl.when(step == 0)
    def _():
        for copy in copies:
            copy.start()
        t_ref[...] = x_ref[...].T
        split_rows(t_ref, xt_ref, groups, low_bit, blocks)
        acc_ref[...] = jnp.zeros_like(acc_ref)
        gx_ref[...] = jnp.zeros_like(gx_ref)

    @pl.when(step < groups)
    def _():
        up = dot(x_ref[...], up_ref[...])
        grad_hidden = dot(g_ref[...], down_ref[...], DIMS_LAST)
        root = math.sqrt(2.0 / math.pi)
        square = up * up
        bent = jnp.tanh(root * up * (1.0 + 0.044715 * square))
        half = 0.5 + 0.5 * bent
        slope = half + 0.5 * up * (1.0 - bent * bent) * (root * (1.0 + 3 * 0.044715 * square))
        hidden = (up * half).astype(BF)
        grad_up = (grad_hidden * slope).astype(BF)
        acc_ref[...] += dot(hidden, down_ref[...])
        gx_ref[...] += dot(grad_up, up_ref[...], DIMS_LAST)
        rows = dot(hidden, g_ref[...], DIMS_FIRST).astype(BF)

        @pl.when(step % 2 == low_bit)
        def _():
            dk_ref[...] = rows

        @pl.when(step % 2 != low_bit)
        def _():
            da_ref[...] = rows

        depth = x_ref.shape[1] // 2
        ua_ref[...] = dot(xt_ref[:depth, :], grad_up).astype(BF)
        uk_ref[...] = dot(xt_ref[depth:, :], grad_up).astype(BF)

    @pl.when(step == groups)
    def _():
        for copy in copies:
            copy.wait()

    @pl.when(step >= groups)
    def _():
        few = out_ref.shape[0]
        here = pl.ds(pl.multiple_of((step - groups) * few, few), few)
        mid, grad = mid_ref[here, :], gx_ref[here, :]
        out_ref[...] = (mid + acc_ref[here, :]).astype(BF)
        normal, rate = norm_stats(mid)
        grad_mid = g_ref[here, :].astype(F32) + norm_back(grad, normal, rate, scale_ref[here, :])
        grad_low = grad_mid.astype(BF)
        gl_ref[...] = grad_low
        gs_ref[...] = grad.astype(BF)
        gc_ref[...] = (grad * normal).astype(BF)
        heads = dot(w_ref[...], grad_low, DIMS_LAST)
        for pair in range(l_ref.shape[0]):
            lanes = slice(pair * PAIR, (pair + 1) * PAIR)
            scaled, centres = [], []
            results = a_ref[here, lanes].T
            for which in range(2):
                rows = slice(pair * PAIR + which * HD, pair * PAIR + (which + 1) * HD)
                scaled.append(heads[rows] * l_ref[pair, which : which + 1, :])
                product = scaled[-1] * results[which * HD : (which + 1) * HD].astype(F32)
                centres.append(jnp.sum(product, axis=0, keepdims=True))
            o_ref[:, lanes] = jnp.concatenate(scaled, axis=0).astype(BF).T
            c_ref[pair] = jnp.concatenate(centres + [jnp.zeros((6, few), F32)], axis=0)


def feed(normed, cot_resid, w_up, w_down, resid_mid, scale, w_out, attended, inverses):
    groups = lax.axis_size("head")
    frames, width = normed.shape
    pairs = width // PAIR
    tile = w_up.shape[1] // groups
    inner = groups * tile
    few = 128
    whole = once((frames, width))
    last = groups - 1
    rows = pl.BlockSpec((tile, width), lambda i: (jnp.minimum(i, last) // 2, 0))
    cols = pl.BlockSpec((width // 2, tile), lambda i: (0, jnp.minimum(i, last)))
    part = pl.BlockSpec((few, width), lambda i: (jnp.maximum(i - groups, 0), 0))
    heads = pl.BlockSpec((pairs, 8, few), lambda i: (0, 0, jnp.maximum(i - groups, 0)))
    low = jax.ShapeDtypeStruct((frames, width), BF)
    anywhere = pl.BlockSpec(memory_space=pl.ANY)
    return pl.pallas_call(
        functools.partial(feed_kernel, groups, seq_blocks(width)),
        grid=(groups + frames // few,),
        in_specs=[
            whole,
            whole,
            pl.BlockSpec((width, tile), lambda i: (0, jnp.minimum(i, last))),
            pl.BlockSpec((tile, width), lambda i: (jnp.minimum(i, last), 0)),
            heads,
        ]
        + [anywhere] * 4,
        out_specs=[rows, rows, cols, cols] + [part] * 5 + [heads],
        out_shape=[
            jax.ShapeDtypeStruct((inner // 2, width), BF),
            pltpu.HBM((inner // 2, width), BF),
            jax.ShapeDtypeStruct((width // 2, inner), BF),
            pltpu.HBM((width // 2, inner), BF),
        ]
        + [low]
        + [pltpu.HBM((frames, width), BF)] * 3
        + [low]
        + [jax.ShapeDtypeStruct((pairs, 8, frames), F32)],
        scratch_shapes=[
            pltpu.VMEM((frames, width), F32),
            pltpu.VMEM((frames, width), F32),
            pltpu.VMEM((width, frames), BF),
            pltpu.VMEM((width, frames), BF),
            pltpu.VMEM((frames, width), F32),
            pltpu.VMEM((frames, width), F32),
            pltpu.VMEM((width, width), BF),
            pltpu.VMEM((frames, width), BF),
            pltpu.SemaphoreType.DMA((4,)),
        ],
        compiler_params=params(40),
        cost_estimate=cost(12 * frames * width * inner, 8 * width * inner, frames * inner),
    )(
        normed,
        cot_resid,
        in_hbm(w_up),
        in_hbm(w_down),
        inverses,
        resid_mid,
        scale,
        w_out,
        attended,
    )


def near_kernel(groups, span, *refs):
    dq_ref, dkv_refs, refs = refs[0], refs[1 : span + 1], refs[span + 1 :]
    w_ref, x_ref, gl_ref = refs[:3]
    attended, second, scale, grad_mid = refs[3:7]
    away_ref, keep_ref, gi_ref, gs_ref, gc_ref = refs[7:12]
    t_ref, xt_ref, acc_ref, a_ref, r_ref, scale_ref, gm_ref, sems = refs[12:]
    step = pl.program_id(0)
    tiles = x_ref.shape[1] // dq_ref.shape[1]
    low_bit = lax.axis_index("head") % 2
    width = x_ref.shape[1]
    half = width // 2
    first, *rest = fetches(
        [
            (attended, a_ref),
            (second.at[:, pl.ds(width, width)], r_ref),
            (scale, scale_ref),
            (grad_mid, gm_ref),
        ],
        sems,
    )

    @pl.when(step == 0)
    def _():
        for copy in (first, *rest):
            copy.start()
        t_ref[...] = x_ref[...].T
        split_rows(t_ref, xt_ref, groups, low_bit)

    @pl.when(step == 3 * tiles)
    def _():
        first.wait()
        t_ref[...] = a_ref[...].T
        split_rows(t_ref, xt_ref, groups, low_bit)

    def one(grads):
        away_ref[...] = dot(xt_ref[:half, :], grads).astype(BF)
        keep_ref[...] = dot(xt_ref[half:, :], grads).astype(BF)

    def projected(grads, start):
        one(grads)
        part = dot(grads, w_ref[...], DIMS_LAST)
        acc_ref[...] = part if start else acc_ref[...] + part

    @pl.when(step == 0)
    def _():
        projected(dq_ref[...], True)

    @pl.when((step > 0) & (step < tiles))
    def _():
        projected(dq_ref[...], False)

    @pl.when((step >= tiles) & (step < 3 * tiles))
    def _():
        grads = functools.reduce(jnp.add, [ref[0].astype(F32) for ref in dkv_refs])
        projected(grads.astype(BF), False)

    @pl.when((step >= 3 * tiles) & (step < 4 * tiles))
    def _():
        one(gl_ref[...])

    @pl.when(step == 4 * tiles)
    def _():
        for copy in rest:
            copy.wait()

    @pl.when(step >= 4 * tiles)
    def _():
        few = gi_ref.shape[0]
        here = pl.ds(pl.multiple_of((step - 4 * tiles) * few, few), few)
        normal, rate = norm_stats(r_ref[here, :].astype(F32))
        grad = acc_ref[here, :]
        grad_in = gm_ref[here, :].astype(F32) + norm_back(grad, normal, rate, scale_ref[here, :])
        gi_ref[...] = grad_in.astype(BF)
        gs_ref[...] = grad.astype(BF)
        gc_ref[...] = (grad * normal).astype(BF)


def near(dq, dkv, w_qkv, normed, attended, grad_low, cot_resid, scale):
    groups = lax.axis_size("head")
    frames, width = dq.shape
    tile = 512
    few = 128
    tiles = width // tile

    def pair(i):
        index = jnp.clip(i - tiles, 0, 2 * tiles - 1)
        return (index // tiles, 0, index % tiles)

    grads = pl.BlockSpec((width // 2, tile), lambda i: (0, jnp.minimum(i, 4 * tiles - 1)))
    part = pl.BlockSpec((few, width), lambda i: (jnp.maximum(i - 4 * tiles, 0), 0))
    out = pltpu.HBM((width // 2, 4 * width), BF)
    low = jax.ShapeDtypeStruct((frames, width), BF)
    return pl.pallas_call(
        functools.partial(near_kernel, groups, len(dkv)),
        grid=(4 * tiles + frames // few,),
        in_specs=[pl.BlockSpec((frames, tile), lambda i: (0, jnp.minimum(i, tiles - 1)))]
        + [pl.BlockSpec((1, frames, tile), pair)] * len(dkv)
        + [
            pl.BlockSpec((width, tile), lambda i: (0, jnp.minimum(i, 3 * tiles - 1))),
            once((frames, width)),
            pl.BlockSpec((frames, tile), lambda i: (0, jnp.clip(i - 3 * tiles, 0, tiles - 1))),
        ]
        + [pl.BlockSpec(memory_space=pl.ANY)] * 4,
        out_specs=[grads, grads, part, part, part],
        out_shape=[out, out, low, low, low],
        scratch_shapes=[
            pltpu.VMEM((width, frames), BF),
            pltpu.VMEM((width, frames), BF),
            pltpu.VMEM((frames, width), F32),
            pltpu.VMEM((frames, width), BF),
            pltpu.VMEM((frames, width), BF),
            pltpu.VMEM((frames, width), F32),
            pltpu.VMEM((frames, width), BF),
            pltpu.SemaphoreType.DMA((4,)),
        ],
        compiler_params=params(52),
        cost_estimate=cost(14 * frames * width * width, 14 * width * width + 30 * frames * width),
    )(dq, *dkv, w_qkv, normed, grad_low, attended, cot_resid, scale, grad_low)


def far_kernel(groups, x_ref, y_ref, f_ref, gi_ref, *refs):
    m_refs, (away_ref, keep_ref, t_ref, st_ref, u_ref, ft_ref) = refs[:4], refs[4:]
    low_bit = lax.axis_index("head") % 2
    width = x_ref.shape[1]

    @pl.when(pl.program_id(0) == 0)
    def _():
        t_ref[:width, :] = x_ref[...].T
        t_ref[width:, :] = y_ref[...].T
        split_rows(t_ref, st_ref, groups, low_bit)
        u_ref[...] = f_ref[...].T
        split_rows(u_ref, ft_ref, groups, low_bit)

    many, few = 2 * width // groups, u_ref.shape[0] // groups
    for part, out_ref in enumerate((away_ref, keep_ref)):
        big = dot(st_ref[part * width : (part + 1) * width, :], gi_ref[...]).astype(BF)
        half = u_ref.shape[0] // 2
        here = ft_ref[part * half : (part + 1) * half, :]
        small = [dot(here, m_ref[...]).astype(BF) for m_ref in m_refs]
        for index in range(groups // 2):
            start = index * (many + 4 * few)
            out_ref[start : start + many, :] = big[index * many : (index + 1) * many]
            for block in range(4):
                first = start + many + block * few
                out_ref[first : first + few, :] = small[block][index * few : (index + 1) * few]


def far(inputs, skips, features, grad_in, grad_mods):
    groups = lax.axis_size("head")
    frames, width = grad_in.shape
    few = features.shape[1]
    tile = 512
    cols = pl.BlockSpec((frames, tile), lambda i: (0, i))
    out = pl.BlockSpec((width + 2 * few, tile), lambda i: (0, i))
    return pl.pallas_call(
        functools.partial(far_kernel, groups),
        grid=(width // tile,),
        in_specs=[once((frames, width)), once((frames, width)), once((frames, few))] + [cols] * 5,
        out_specs=[out, out],
        out_shape=[pltpu.HBM((width + 2 * few, width), BF)] * 2,
        scratch_shapes=[pltpu.VMEM((2 * width, frames), BF)] * 2
        + [pltpu.VMEM((few, frames), BF)] * 2,
        compiler_params=params(34),
        cost_estimate=cost(6 * frames * width * width, 6 * width * width + 20 * frames * width),
    )(inputs, skips, features, grad_in, *grad_mods)


def per_device(
    inputs,
    skips,
    flow_time,
    segment_ids,
    frame_mask,
    cotangent,
    w_skip,
    w_time,
    w_qkv,
    w_out,
    w_up,
    w_down,
):
    groups = lax.axis_size("head")
    micro_count, _, rows, width = inputs.shape
    span = groups // micro_count
    place = lax.axis_index("head")
    mine = place // span
    frames = micro_count * rows
    feature_count = w_time.shape[0]
    inputs, skips, cotangent = inputs[:, 0], skips[:, 0], cotangent[:, 0]

    resid_own = dot(inputs.reshape(frames, width), w_skip[:width]) + dot(
        skips.reshape(frames, width), w_skip[width:]
    )
    own_mod = dot(time_features(flow_time.reshape(-1), feature_count), w_time[:, : 2 * width])
    normed_own = norm_stats(resid_own)[0] * (1.0 + own_mod[:, width:]) + own_mod[:, :width]
    normed_own = cut_parts(normed_own.astype(BF).reshape(micro_count, rows, width), mine)

    meta = jnp.stack(
        [segment_ids[:, 0].astype(F32), frame_mask[:, 0].astype(F32), flow_time[:, 0]], axis=1
    )[None]
    meta = jnp.concatenate([meta, swap(meta, "head", 1)])
    meta, *normed_own = together(meta, *normed_own)
    normed_attn = send_parts(normed_own, span)
    resid_low = resid_own.astype(BF).reshape(micro_count, rows, width)
    for bit in range(1, groups.bit_length() - 1):
        meta = jnp.concatenate([meta, swap(meta, "head", 2**bit)])
        if bit == 1:
            meta, cotangent, resid_low = together(meta, cotangent, resid_low)
    second = [
        jnp.concatenate(pair, axis=1)
        for pair in zip(cut_parts(cotangent, mine), cut_parts(resid_low, mine), strict=True)
    ]
    meta, *rest = together(meta, *normed_attn, *second)
    normed_attn, second = jnp.concatenate(rest[:micro_count]), rest[micro_count:]
    meta = pick(meta, mine, 1).reshape(micro_count, span, 3, rows)
    seg_keys, live_keys, times = [meta[:, :, i].swapaxes(0, 1).reshape(-1) for i in range(3)]
    order = jnp.stack(
        [place ^ other ^ (step * span) for other in range(span) for step in range(micro_count)]
    )
    place_keys = (order[:, None] * rows + jnp.arange(rows)[None, :]).reshape(-1).astype(F32)
    starts = jnp.sum((seg_keys[None, :] < seg_keys[:, None]).astype(F32), axis=1)
    positions = place_keys - starts
    inv_freq = jnp.exp(jnp.arange(HD // 2, dtype=F32) * (-2.0 * math.log(10000.0) / HD))
    turns = positions[:, None] * inv_freq
    cos_half, sin_half = jnp.cos(turns), jnp.sin(turns)
    cos_keys = jnp.concatenate([cos_half] * 4, axis=1)
    sin_keys = jnp.concatenate([-sin_half, sin_half] * 2, axis=1)

    queries, keys_values = project(normed_attn, w_qkv, cos_keys[:frames], sin_keys[:frames])
    keys_values, seg_keys, live_keys, place_keys, times = together(
        keys_values, seg_keys, live_keys, place_keys, times
    )
    pairs_kv = [keys_values] + [swap(keys_values, "head", other) for other in range(1, span)]
    mask_keys, mask_queries = mask_lanes(seg_keys, live_keys, place_keys, groups * rows)
    queries, mask_keys, mask_queries, *pairs_kv = together(
        queries, mask_keys, mask_queries[:frames], *pairs_kv
    )

    second = send_parts(second, span)
    attended, probs, inverses = attend(queries, pairs_kv, mask_keys, mask_queries)
    attended, times = together(attended, times)
    features = time_features(times[:frames], feature_count)
    scale_first, shift_second, scale_second = [
        dot(features, w_time[:, i * width : (i + 1) * width]) for i in range(1, 4)
    ]
    attended, scale_first, shift_second, scale_second, *second = together(
        attended, scale_first, shift_second, scale_second, *second
    )
    second = jnp.concatenate(second)
    resid_mid = second[:, width:].astype(F32) + dot(attended, w_out)
    normal_second = norm_stats(resid_mid)[0]
    normed_ffn = (normal_second * (1.0 + scale_second) + shift_second).astype(BF)

    (
        down_away, down_keep, up_away, up_keep, output, grad_mid, mod_shift, mod_scale, grads, centres
    ) = feed(
        normed_ffn, second, w_up, w_down, resid_mid, scale_second, w_out, attended, inverses
    )
    grads, down_away, up_away, output = together(grads, down_away, up_away, output)
    seq_bits = lax.axis_size("seq").bit_length() - 1
    bits = list(range(seq_bits + 1, seq_bits + groups.bit_length() - 1))
    orders = (bits, bits[::-1])

    def two_ways(*arrays):
        middle_col = arrays[0].shape[1] // 2
        return [Rows(list(arrays), bits, 1, (i * middle_col, middle_col)) for i in range(2)]

    def begin(*pairs, index):
        return [
            away_all([pair[side] for pair in pairs], order[index])
            for side, order in enumerate(orders)
        ]

    def send(away, index):
        return [cross(rows, order[index]) for rows, order in zip(away, orders, strict=True)]

    def end(*pairs, came):
        for side, rows in enumerate(came):
            join_all([pair[side] for pair in pairs], rows)

    down_came, up_came = swap(down_away, "head", 1), swap(up_away, "head", 1)
    output = send_parts(list(output.reshape(micro_count, rows, width)), span)
    dq, dkv = attend_back(queries, pairs_kv, probs, centres, grads, cos_keys, sin_keys)
    dq, down_came, up_came, *rest = together(dq, down_came, up_came, *dkv, *output)
    dkv, output = rest[:span], rest[span:]

    dkv[1:] = [swap(part, "head", other) for other, part in enumerate(dkv) if other > 0]
    down = two_ways(down_keep, down_came)
    half = up_keep.shape[1] // 2
    up_0 = add_low([up_keep[:, :half], up_came[:, :half]])
    up_1 = add_low([up_keep[:, half:], up_came[:, half:]])
    dq, up_0, up_1, down_came, *dkv = together(dq, up_0, up_1, down_came, *dkv)
    up_0 = seq_first(up_0)
    down = two_ways(down_keep, down_came)
    dq, *away = together(dq, *begin(down, index=0))
    came = send(away, 0)
    near_away, near_keep, grad_in_low, first_shift, first_scale = near(
        dq, dkv, w_qkv, normed_attn, attended, grad_mid, second, scale_first
    )
    near_away, grad_in_low, *came = together(near_away, grad_in_low, *came)
    end(down, came=came)

    near_came = swap(near_away, "head", 1)
    for index in range(1, len(bits) - 1):
        end(down, came=send(begin(down, index=index), index))
    last_index = len(bits) - 1
    grad_in_low, *away = together(grad_in_low, *begin(down, index=last_index))
    came = send(away, last_index)
    grad_local = send_parts(list(grad_in_low.reshape(micro_count, rows, width)), span)
    wide = two_ways(near_keep, near_came)
    up_0, *rest = together(up_0, *begin(wide, index=0), *came, *grad_local, *output)
    wide_away, came, rest = rest[:2], rest[2:4], rest[4:]
    grad_local, output = rest[:micro_count], rest[micro_count:]
    end(down, came=came)

    wide_came = send(wide_away, 0)
    grad_local = by_micro(grad_local, mine).reshape(frames, width)
    far_away, far_keep = far(
        inputs.reshape(frames, width),
        skips.reshape(frames, width),
        features,
        grad_local,
        [first_shift, first_scale, mod_shift, mod_scale],
    )
    up_1 = seq_first(up_1)
    down_rows = jnp.concatenate([part.read() for part in down], axis=1)
    far_away, down_rows, *wide_came = together(far_away, down_rows, *wide_came)
    end(wide, came=wide_came)

    far_came = swap(far_away, "head", 1)
    narrow = two_ways(far_keep, far_came)
    for index in range(1, len(bits)):
        wide_came = send(begin(wide, index=index), index)
        if index < last_index:
            end(wide, came=together(*wide_came))
    (down_sum,) = last_sum(down_rows)
    up_1, *rest = together(up_1, *begin(narrow, index=0), *wide_came)
    narrow_away, wide_came = rest[:2], rest[2:]
    end(wide, came=wide_came)

    narrow_came = send(narrow_away, 0)
    wide_sum = jnp.concatenate([wide[0].read(), wide[1].read()], axis=1)
    ups = [Rows([up_0], bits), Rows([up_1], bits)]
    rest = together(wide_sum, down_sum, *begin(ups, index=0), *narrow_came)
    wide_sum, down_sum, up_away = rest[0], rest[1], rest[2:4]
    end(narrow, came=rest[4:])

    (near_sum,) = last_sum(wide_sum)
    for index in range(1, len(bits)):
        end(narrow, came=together(*send(begin(narrow, index=index), index)))
    far_sum = jnp.concatenate([narrow[0].read(), narrow[1].read()], axis=1)
    many = w_skip.shape[0] // groups
    last = [
        Rows([far_sum[:many]], list(range(seq_bits))),
        Rows([far_sum[many:]], list(range(seq_bits)), 4),
    ]
    for index in range(max(seq_bits, len(bits))):
        came, up_came = [], []
        if index < seq_bits:
            came = [cross(away_all(last, index), index)]
        if index < len(bits):
            up_came = send(up_away, index)
        if index == 0:
            near_sum, *rest = together(near_sum, *came, *up_came)
            done = [
                by_micro(output, mine),
                near_sum[:, : 3 * width].astype(F32),
                near_sum[:, 3 * width :].astype(F32),
                down_sum.astype(F32),
            ]
        else:
            *done, rest = together(*done, [*came, *up_came])
        if index < seq_bits:
            join_all(last, rest[0])
        if index < len(bits):
            end(ups, came=rest[len(came) :])
        if index + 1 < len(bits):
            up_away = begin(ups, index=index + 1)
    output, total_qkv, total_out, total_down = done
    total_up = jnp.concatenate([part.read() for part in ups], axis=1).astype(F32)
    total_skip = last[0].read().astype(F32)
    total_time = last[1].read().astype(F32)
    total_time = total_time.reshape(4, -1, width).swapaxes(0, 1).reshape(-1, 4 * width)
    shape = (micro_count, 1, rows, width)
    input_grad = dot(grad_local, w_skip[:width], DIMS_LAST).reshape(shape)
    skip_grad = dot(grad_local, w_skip[width:], DIMS_LAST).reshape(shape)
    return (
        output[:, None],
        input_grad,
        skip_grad,
        total_skip,
        total_time,
        total_qkv,
        total_out,
        total_up,
        total_down,
    )


def solution(mesh):
    frames_spec = P(None, "seq", "head", None)
    line_spec = P(None, "seq", "head")
    shard_spec = P(("head", "seq"), None)
    return jax.shard_map(
        per_device,
        mesh=mesh,
        in_specs=(frames_spec, frames_spec, line_spec, line_spec, line_spec, frames_spec)
        + (P(),) * 6,
        out_specs=(frames_spec,) * 3 + (shard_spec,) * 6,
        check_vma=False,
    )
```
